32 devices in a mesh: groups: 2 (over x), ex: 16 (over z, y, core).
Axes of the slice: x: 2, y: 2, z: 4, core: 2. Of those that a mesh axis runs over, the one named last changes fastest.
Arguments:
- acts: bfloat16 [24576, 5120], P(('groups', 'ex')), parts along dimension 0, may hold values from -6 to 6
- grads: bfloat16 [24576, 1024], P(('groups', 'ex')), parts along dimension 0, may hold values from -6 to 6
- domain: int32 [3072], P(('groups', 'ex')), parts along dimension 0, may hold values from 0 to 47
- listed: int32 [32, 2], P(('groups', 'ex')), parts along dimension 0, may hold values 0 or 1
Outputs:
- influence: float32 [3072, 48], P(('groups', 'ex')), parts along dimension 0
The draws below stay inside these ranges and needn't reach their ends.
There are 2 independent parts, one for each index of `groups`. The reference program is written for one: setup_inputs(seed, part) draws one part's arguments, and reference() takes and returns one part's arrays. A program takes and returns all parts, laid end to end along the dimension named above; each array names one. Nothing has to cross between parts.
All inputs are finite; a program needn't handle non-finite values. No bound on the sum of `listed` on one device may be relied on, other than what follows from the above.
Results may differ from the reference program's by a relative error of at most 0.0003.
Values may be sent and summed in bfloat16 or wider, within the bound.
No kernel may reach another device: no remote copies, remote signals or barrier semaphores. Data moves between devices by JAX's collectives and lax.ppermute only.
A program may use at most 192 MiB of HBM per device.

```python
import math
import jax
import jax.numpy as jnp
from jax import lax

D = 5120
DK = 1024
TOK = 8
DOMAINS = 48
REACH = 2
EX_DEV = 96
EXAMPLES = 1536
N_EX = 16


def plant(array, rng, least, high):
    place = [jax.random.randint(jax.random.fold_in(rng, axis), (), 0, length) for axis, length in enumerate(array.shape)]
    main_axis = array.shape.index(max(array.shape))
    next_to = place[:main_axis] + [(place[main_axis] + 1) % array.shape[main_axis]] + place[main_axis + 1:]
    return array.at[tuple(place)].set(least).at[tuple(next_to)].set(high)


def level_of(key, extent, cuts, least, largest):
    gain = 1.0
    for axis_at, blocks in cuts:
        steps = jax.random.uniform(jax.random.fold_in(jax.random.fold_in(key, 6), axis_at), (blocks,), jnp.float32, least / len(cuts), largest / len(cuts))
        gain = gain * jnp.repeat(jnp.exp(steps), extent[axis_at] // blocks).reshape((-1,) + (1,) * (len(extent) - 1 - axis_at))
    return gain


def centred(key, shape, deviation, reach, split=(), kind=jnp.bfloat16):
    loudness = level_of(key, shape, split, -0.22, 0.18) if split else 1.0
    values = jax.random.normal(key, shape, jnp.float32) * deviation * loudness
    return jnp.minimum(jnp.maximum(values, -reach), reach).astype(kind)


def setup_inputs(seed: int = 0, part: int = 0) -> dict:
    seeds = jax.random.split(jax.random.key(seed), 5)
    own_keys = jax.random.split(jax.random.fold_in(seeds[4], part), 5)
    return {
        "acts": centred(own_keys[0], (EXAMPLES * TOK, D), 1.0, 6.0, ((0, 16),)),
        "grads": centred(own_keys[1], (EXAMPLES * TOK, DK), 1.0, 6.0, ((0, 16),)),
        "domain": plant(jax.random.randint(own_keys[2], (EXAMPLES,), 0, DOMAINS), jax.random.fold_in(own_keys[2], 1), 0, DOMAINS - 1).astype(jnp.int32),
        "listed": plant((jax.random.randint(own_keys[3], (N_EX, REACH), 0, 4) < 3).astype(jnp.int32), jax.random.fold_in(own_keys[3], 1), 0, 1),
    }


def pair_scores(acts_one, grads_one, acts_two, grads_two):
    contract = (((1,), (1,)), ((), ()))
    inner_acts = lax.dot_general(acts_one, acts_two, contract, preferred_element_type=jnp.float32)
    inner_grads = lax.dot_general(grads_one, grads_two, contract, preferred_element_type=jnp.float32)
    per_block = acts_one.shape[0] // TOK
    factor = 1.0 / (TOK * math.sqrt(acts_one.shape[1] * grads_one.shape[1]))
    return (inner_acts * inner_grads).reshape(per_block, TOK, per_block, TOK).sum(axis=(1, 3)) * factor

def reference(acts, grads, domain, listed):
    blocks = N_EX
    rows_block = EX_DEV * TOK
    acts_blocks = acts.reshape(blocks, rows_block, D)
    grads_blocks = grads.reshape(blocks, rows_block, DK)
    one_hot = (domain.reshape(blocks, EX_DEV)[:, :, None] == jnp.arange(DOMAINS, dtype=jnp.int32)[None, None, :]).astype(jnp.float32)
    total = jnp.zeros((blocks, EX_DEV, DOMAINS), jnp.float32)
    for offset in range(REACH):
        distance = offset + 1

        def single(index):
            partner = (index + distance) % blocks
            weight = listed[index, offset].astype(jnp.float32)
            scores = pair_scores(acts_blocks[index], grads_blocks[index], acts_blocks[partner], grads_blocks[partner]) * weight
            row_sums = jnp.dot(scores, one_hot[partner], precision=lax.Precision.HIGHEST)
            col_sums = jnp.dot(scores.T, one_hot[index], precision=lax.Precision.HIGHEST)
            return (row_sums, col_sums)
        row_part, col_part = lax.map(single, jnp.arange(blocks, dtype=jnp.int32))
        total = total + row_part + jnp.roll(col_part, distance, axis=0)
    return total.reshape(blocks * EX_DEV, DOMAINS)
```

```python
import functools
import math

import jax
import jax.numpy as jnp
from jax import lax
from jax.experimental import pallas as pl
from jax.experimental.pallas import tpu as pltpu
from jax.sharding import PartitionSpec as P

TOK = 8
DOMAINS = 48
LANES = 128
VMEM_BYTES = 56 * 1024 * 1024

XS, XC, YS, YC, ZS, ZC = range(6)
PAIRS = (
    (XS, YS, 1), (YS, ZS, 1), (XC, YS, 0), (XS, XC, 0),
    (XC, YC, 1), (YC, ZC, 1), (YC, ZS, 0), (YS, ZC, 0), (XS, YC, 0),
)
ONLY = {2: 0, 6: 0, 7: 1, 8: 1}
SLOT = (0, 1, 2, 3, 4, 5, 6, 6, 2)
FIRST = (0, 1, 2, 3)
SECOND = (4, 5, 6, 7, 8)
NT = (((1,), (1,)), ((), ()))


def across(chip):
    return chip ^ 1


def along(chip):
    return chip + 2 if chip & 1 else chip - 2


def against(chip):
    return chip - 2 if chip & 1 else chip + 2


def stay(chip):
    return chip


def send(value, move, flip):
    chips = lax.axis_size("ex") // 2
    pairs = [
        (2 * chip + core, 2 * (move(chip) % chips) + (core ^ flip))
        for chip in range(chips)
        for core in range(2)
    ]
    return lax.ppermute(value, "ex", pairs)


def cut_kernel(offsets, acts, y_same, z_same, x_half, y_cross, z_cross, sems):
    copies = []
    for at, out in enumerate((y_same, z_same, x_half, y_cross, z_cross)):
        start = pl.multiple_of(offsets[at], LANES)
        copies.append(pltpu.make_async_copy(acts.at[:, pl.ds(start, out.shape[1])], out, sems.at[at]))
    for copy in copies:
        copy.start()
    for copy in copies:
        copy.wait()


def cut(acts, offsets):
    rows, width = acts.shape
    quarter = width // 4
    widths = (quarter, quarter, 2 * quarter, quarter, quarter)
    return pl.pallas_call(
        cut_kernel,
        in_specs=[pl.BlockSpec(memory_space=pltpu.SMEM), pl.BlockSpec(memory_space=pl.ANY)],
        out_specs=[pl.BlockSpec(memory_space=pl.ANY)] * 5,
        out_shape=[jax.ShapeDtypeStruct((rows, w), acts.dtype) for w in widths],
        scratch_shapes=[pltpu.SemaphoreType.DMA((5,))],
        name="cut",
    )(offsets, acts)


def guarded(pair, mirrored, work):
    if pair in ONLY:
        pl.when(mirrored == ONLY[pair])(work)
    else:
        work()


def grams_kernel(flags, xs, xc, ys, yc, zs, zc, out, held, result, in_sems, out_sems):
    mirrored = flags[0]
    loads = [
        pltpu.make_async_copy(source, held.at[at], in_sems.at[at])
        for at, source in enumerate((xs, xc, ys, yc, zs, zc))
    ]
    for load in loads:
        load.start()
    for load in loads:
        load.wait()
    for pair, (one, two, _) in enumerate(PAIRS):
        slot = SLOT[pair]

        def work(one=one, two=two, slot=slot):
            result[slot] = lax.dot_general(
                held[one], held[two], NT, preferred_element_type=jnp.float32
            )
            pltpu.make_async_copy(result.at[slot], out.at[slot], out_sems.at[slot]).start()

        guarded(pair, mirrored, work)
    for slot in range(7):
        pltpu.make_async_copy(result.at[slot], out.at[slot], out_sems.at[slot]).wait()


def grams(flags, blocks):
    rows, width = blocks[0].shape
    return pl.pallas_call(
        grams_kernel,
        in_specs=[pl.BlockSpec(memory_space=pltpu.SMEM)] + [pl.BlockSpec(memory_space=pl.ANY)] * 6,
        out_specs=pl.BlockSpec(memory_space=pl.ANY),
        out_shape=jax.ShapeDtypeStruct((7, rows, rows), jnp.float32),
        scratch_shapes=[
            pltpu.VMEM((6, rows, width), blocks[0].dtype),
            pltpu.VMEM((7, rows, rows), jnp.float32),
            pltpu.SemaphoreType.DMA((6,)),
            pltpu.SemaphoreType.DMA((7,)),
        ],
        compiler_params=pltpu.CompilerParams(vmem_limit_bytes=VMEM_BYTES),
        cost_estimate=pl.CostEstimate(
            flops=14 * rows * rows * width,
            bytes_accessed=12 * rows * width + 28 * rows * rows,
            transcendentals=0,
        ),
        name="grams",
    )(flags, *blocks)


def token_sums(one, two, gram, sums):
    rows = one.shape[0]
    step = math.gcd(rows, 256)
    for at in range(0, rows, step):
        cols = slice(at, at + step)
        inner = lax.dot_general(one[...], two[cols, :], NT, preferred_element_type=jnp.float32)
        weighted = inner * gram[:, cols]
        sums[:, cols] = weighted.reshape(rows // TOK, TOK, step).sum(axis=1)


def three_parts(value):
    high = value.astype(jnp.bfloat16)
    rest = value - high.astype(jnp.float32)
    middle = rest.astype(jnp.bfloat16)
    low = (rest - middle.astype(jnp.float32)).astype(jnp.bfloat16)
    return high, middle, low


def dot_parts(value, table):
    total = None
    for part in reversed(three_parts(value)):
        term = jnp.dot(part, table, preferred_element_type=jnp.float32)
        total = term if total is None else total + term
    return total


def tiles_of(sums, gather):
    count, examples, rows = sums.shape
    flat = dot_parts(sums[...].reshape(count * examples, rows), gather[...])
    return flat.reshape(count, examples, LANES)


def first_kernel(flags, gather, acts, x_half, ys, zs, gram, out,
                 xs_v, xc_v, ys_v, zs_v, own_v, half_v, gram_v, sums, sems):
    mirrored, work_at, half_at, in_half = flags[0], flags[1], flags[2], flags[3]
    quarter = ys.shape[1]
    loads = {
        "xs": (acts.at[:, pl.ds(pl.multiple_of(work_at, LANES), quarter)], xs_v),
        "ys": (ys, ys_v),
        "g0": (gram.at[0], gram_v.at[0]),
        "zs": (zs, zs_v),
        "g1": (gram.at[1], gram_v.at[1]),
        "xc": (x_half.at[:, pl.ds(pl.multiple_of(in_half, LANES), quarter)], xc_v),
        "g2": (gram.at[2], gram_v.at[2]),
        "own": (acts.at[:, pl.ds(pl.multiple_of(half_at, LANES), 2 * quarter)], own_v),
        "half": (x_half, half_v),
        "g3": (gram.at[3], gram_v.at[3]),
    }
    copies = {
        key: pltpu.make_async_copy(source, target, sems.at[at])
        for at, (key, (source, target)) in enumerate(loads.items())
    }
    for copy in copies.values():
        copy.start()
    plan = (
        (("xs", "ys", "g0"), xs_v, ys_v),
        (("zs", "g1"), ys_v, zs_v),
        (("xc", "g2"), xc_v, ys_v),
        (("own", "half", "g3"), own_v, half_v),
    )
    for at, pair in enumerate(FIRST):
        keys, one, two = plan[at]
        for key in keys:
            copies[key].wait()
        if pair in ONLY:
            sums[at] = jnp.zeros(sums.shape[1:], jnp.float32)
        guarded(pair, mirrored, functools.partial(token_sums, one, two, gram_v.at[at], sums.at[at]))
    out[...] = tiles_of(sums, gather)


def second_kernel(flags, weights, gather, hot, first_tiles, acts, x_half, ys, yc, zs, zc, gram,
                  out, xs_v, xc_v, ys_v, yc_v, zs_v, zc_v, gram_v, sums, table, sems):
    mirrored, work_at, in_half = flags[0], flags[1], flags[3]
    quarter = ys.shape[1]
    loads = {
        "yc": (yc, yc_v),
        "xc": (x_half.at[:, pl.ds(pl.multiple_of(in_half, LANES), quarter)], xc_v),
        "g4": (gram.at[4], gram_v.at[0]),
        "zc": (zc, zc_v),
        "g5": (gram.at[5], gram_v.at[1]),
        "ys": (ys, ys_v),
        "zs": (zs, zs_v),
        "g6": (gram.at[6], gram_v.at[2]),
        "xs": (acts.at[:, pl.ds(pl.multiple_of(work_at, LANES), quarter)], xs_v),
        "g2": (gram.at[2], gram_v.at[3]),
    }
    copies = {
        key: pltpu.make_async_copy(source, target, sems.at[at])
        for at, (key, (source, target)) in enumerate(loads.items())
    }
    for copy in copies.values():
        copy.start()
    plan = (
        (("yc", "xc", "g4"), xc_v, yc_v, 0),
        (("zc", "g5"), yc_v, zc_v, 1),
        (("ys", "zs", "g6"), yc_v, zs_v, 2),
        ((), ys_v, zc_v, 2),
        (("xs", "g2"), xs_v, yc_v, 3),
    )
    table[...] = jnp.zeros_like(table)
    for at, pair in enumerate(SECOND):
        keys, one, two, slot = plan[at]
        for key in keys:
            copies[key].wait()
        if pair in ONLY:
            sums[at] = jnp.zeros(sums.shape[1:], jnp.float32)
        guarded(pair, mirrored, functools.partial(token_sums, one, two, gram_v.at[slot], sums.at[at]))
    later = tiles_of(sums, gather)
    examples = sums.shape[1]
    for pair, (one, two, _) in enumerate(PAIRS):
        tile = first_tiles[pair] if pair < len(FIRST) else later[pair - len(FIRST)]
        tile = tile * weights[pair]
        table[one * LANES:one * LANES + examples, two * LANES:(two + 1) * LANES] = tile
        full = jnp.concatenate([tile, jnp.zeros((LANES - examples, LANES), jnp.float32)], axis=0)
        table[two * LANES:(two + 1) * LANES, one * LANES:(one + 1) * LANES] = full.T
    total = dot_parts(table[...], hot[...])
    for block in range(6):
        out[block] = total[block * LANES:block * LANES + examples, :DOMAINS]


def per_device(acts, grads, domain, listed):
    rows, width = acts.shape
    examples = rows // TOK
    quarter = width // 4
    count = lax.axis_size("ex")
    me = lax.axis_index("ex")
    core = me % 2
    side = (me // 2) % 2
    mirrored = core ^ side
    bf16 = acts.dtype

    def work_at(side_at, core_at):
        return core_at * 2 * quarter + (1 - side_at) * quarter

    flags = jnp.stack([
        mirrored, work_at(side, core), core * 2 * quarter, (1 - side) * quarter
    ]).astype(jnp.int32)
    offsets = jnp.stack([
        work_at(1 - side, core),
        work_at(side, core),
        (1 - core) * 2 * quarter,
        work_at(1 - side, 1 - core),
        work_at(side, 1 - core),
    ]).astype(jnp.int32)

    grads_ys = send(grads, across, 0)
    grads_zs = send(grads, along, 0)
    grads_xc = send(grads, stay, 1)
    cut_ys, cut_zs, cut_xh, cut_yc, cut_zc = cut(acts, offsets)
    ys = send(cut_ys, across, 0)
    zs = send(cut_zs, along, 0)
    x_half = send(cut_xh, stay, 1)
    yc = send(cut_yc, across, 1)
    zc = send(cut_zc, along, 1)
    grads_yc = send(grads_ys, stay, 1)
    grads_zc = send(grads_zs, stay, 1)

    info = jnp.concatenate([domain, listed[0], jnp.zeros((LANES - examples - 2,), jnp.int32)])
    every = lax.all_gather(info, "ex")
    zs_at = jnp.where(side == 0, me + 4, me + count - 4) % count
    ids = jnp.stack([me, me ^ 1, me ^ 2, me ^ 3, zs_at, zs_at ^ 1])
    near = every[ids]
    domains = jnp.where(jnp.arange(LANES)[None, :] < examples, near, -1)
    hot = (domains.reshape(6 * LANES)[:, None] == jnp.arange(LANES)[None, :]).astype(jnp.bfloat16)
    flag = near[:, examples:examples + 2].astype(jnp.float32)
    factor = 1.0 / (TOK * math.sqrt(width * grads.shape[1]))
    weights = []
    for one, two, apart in PAIRS:
        if (one, two) == (XS, XC):
            chosen = jnp.where(core == 0, flag[XS, apart], flag[XC, apart])
        else:
            chosen = jnp.where(side == 0, flag[one, apart], flag[two, apart])
        weights.append(chosen * factor)
    weights = jnp.stack(weights)

    gram = grams(flags, (grads, grads_xc, grads_ys, grads_yc, grads_zs, grads_zc))
    gather = (
        (jnp.arange(rows) // TOK)[:, None] == jnp.arange(LANES)[None, :]
    ).astype(jnp.bfloat16)

    smem = pl.BlockSpec(memory_space=pltpu.SMEM)
    vmem = pl.BlockSpec(memory_space=pltpu.VMEM)
    hbm = pl.BlockSpec(memory_space=pl.ANY)
    params = pltpu.CompilerParams(vmem_limit_bytes=VMEM_BYTES)
    slice_v = pltpu.VMEM((rows, quarter), bf16)
    half_v = pltpu.VMEM((rows, 2 * quarter), bf16)
    gram_v = pltpu.VMEM((4, rows, rows), jnp.float32)
    first_tiles = pl.pallas_call(
        first_kernel,
        in_specs=[smem, vmem] + [hbm] * 5,
        out_specs=vmem,
        out_shape=jax.ShapeDtypeStruct((4, examples, LANES), jnp.float32),
        scratch_shapes=[slice_v] * 4 + [half_v] * 2 + [
            gram_v,
            pltpu.VMEM((4, examples, rows), jnp.float32),
            pltpu.SemaphoreType.DMA((10,)),
        ],
        compiler_params=params,
        cost_estimate=pl.CostEstimate(
            flops=10 * rows * rows * quarter,
            bytes_accessed=20 * rows * quarter + 16 * rows * rows,
            transcendentals=0,
        ),
        name="first",
    )(flags, gather, acts, x_half, ys, zs, gram)
    sums = pl.pallas_call(
        second_kernel,
        in_specs=[smem, smem, vmem, vmem, vmem] + [hbm] * 7,
        out_specs=vmem,
        out_shape=jax.ShapeDtypeStruct((6, examples, DOMAINS), jnp.float32),
        scratch_shapes=[slice_v] * 6 + [
            gram_v,
            pltpu.VMEM((5, examples, rows), jnp.float32),
            pltpu.VMEM((6 * LANES, 6 * LANES), jnp.float32),
            pltpu.SemaphoreType.DMA((10,)),
        ],
        compiler_params=params,
        cost_estimate=pl.CostEstimate(
            flops=8 * rows * rows * quarter,
            bytes_accessed=12 * rows * quarter + 16 * rows * rows,
            transcendentals=0,
        ),
        name="second",
    )(flags, weights, gather, hot, first_tiles, acts, x_half, ys, yc, zs, zc, gram)

    total = sums[XS]
    total = total + send(sums[XC], stay, 1)
    total = total + send(sums[YS], across, 0)
    total = total + send(sums[YC], across, 1)
    total = total + send(sums[ZS], against, 0)
    total = total + send(sums[ZC], against, 1)
    return total


def solution(mesh):
    in_specs = (
        P(("groups", "ex"), None),
        P(("groups", "ex"), None),
        P(("groups", "ex")),
        P(("groups", "ex"), None),
    )
    out_specs = P(("groups", "ex"), None)
    return jax.shard_map(
        per_device, mesh=mesh, in_specs=in_specs, out_specs=out_specs, check_vma=False
    )
```

```python
import functools
import math

import jax
import jax.numpy as jnp
from jax import lax
from jax.experimental import pallas as pl
from jax.experimental.pallas import tpu as pltpu
from jax.sharding import PartitionSpec as P

TOK = 8
DOMAINS = 48
LANES = 128
VMEM_BYTES = 40 * 1024 * 1024

XS, XC, YS, YC, ZS, ZC = range(6)
PAIRS = (
    (XS, YS, 1), (YS, ZS, 1), (XC, YS, 0), (XS, XC, 0),
    (XC, YC, 1), (YC, ZC, 1), (YC, ZS, 0), (YS, ZC, 0), (XS, YC, 0),
)
ONLY = {2: 0, 6: 0, 7: 1, 8: 1}
SLOT = (0, 1, 2, 3, 4, 5, 6, 6, 2)
FIRST = (0, 1, 2, 3)
SECOND = (4, 5, 6, 7, 8)
NT = (((1,), (1,)), ((), ()))


def across(chip):
    return chip ^ 1


def along(chip):
    return chip + 2 if chip & 1 else chip - 2


def against(chip):
    return chip - 2 if chip & 1 else chip + 2


def stay(chip):
    return chip


def send(value, move, flip):
    chips = lax.axis_size("ex") // 2
    pairs = [
        (2 * chip + core, 2 * (move(chip) % chips) + (core ^ flip))
        for chip in range(chips)
        for core in range(2)
    ]
    return lax.ppermute(value, "ex", pairs)


def cut_kernel(places, *refs):
    for source, target in zip(refs[:5], refs[5:]):
        target[...] = source[...]


def cut(acts, places):
    rows, width = acts.shape
    quarter = width // 4
    widths = (quarter, quarter, 2 * quarter, quarter, quarter)
    step = math.gcd(rows, 96)
    return pl.pallas_call(
        cut_kernel,
        grid_spec=pltpu.PrefetchScalarGridSpec(
            num_scalar_prefetch=1,
            grid=(rows // step,),
            in_specs=[
                pl.BlockSpec((step, w), functools.partial(lambda at, i, p: (i, p[at]), at))
                for at, w in enumerate(widths)
            ],
            out_specs=[pl.BlockSpec((step, w), lambda i, p: (i, 0)) for w in widths],
        ),
        out_shape=[jax.ShapeDtypeStruct((rows, w), acts.dtype) for w in widths],
        compiler_params=pltpu.CompilerParams(vmem_limit_bytes=VMEM_BYTES),
        name="cut",
    )(places, acts, acts, acts, acts, acts)


def guarded(pair, mirrored, work):
    if pair in ONLY:
        pl.when(mirrored == ONLY[pair])(work)
    else:
        work()


def grams_kernel(flags, xs, xc, ys, yc, zs, zc, out, held, result, in_sems, out_sems):
    mirrored = flags[0]
    loads = [
        pltpu.make_async_copy(source, held.at[at], in_sems.at[at])
        for at, source in enumerate((xs, xc, ys, yc, zs, zc))
    ]
    for load in loads:
        load.start()
    for load in loads:
        load.wait()
    for pair, (one, two, _) in enumerate(PAIRS):
        slot = SLOT[pair]

        def work(one=one, two=two, slot=slot):
            result[slot] = lax.dot_general(
                held[one], held[two], NT, preferred_element_type=jnp.float32
            )
            pltpu.make_async_copy(result.at[slot], out.at[slot], out_sems.at[slot]).start()

        guarded(pair, mirrored, work)
    for slot in range(7):
        pltpu.make_async_copy(result.at[slot], out.at[slot], out_sems.at[slot]).wait()


def grams(flags, blocks):
    rows, width = blocks[0].shape
    return pl.pallas_call(
        grams_kernel,
        in_specs=[pl.BlockSpec(memory_space=pltpu.SMEM)] + [pl.BlockSpec(memory_space=pl.ANY)] * 6,
        out_specs=pl.BlockSpec(memory_space=pl.ANY),
        out_shape=jax.ShapeDtypeStruct((7, rows, rows), jnp.float32),
        scratch_shapes=[
            pltpu.VMEM((6, rows, width), blocks[0].dtype),
            pltpu.VMEM((7, rows, rows), jnp.float32),
            pltpu.SemaphoreType.DMA((6,)),
            pltpu.SemaphoreType.DMA((7,)),
        ],
        compiler_params=pltpu.CompilerParams(vmem_limit_bytes=VMEM_BYTES),
        cost_estimate=pl.CostEstimate(
            flops=14 * rows * rows * width,
            bytes_accessed=12 * rows * width + 28 * rows * rows,
            transcendentals=0,
        ),
        name="grams",
    )(flags, *blocks)


def token_sums(one, two, gram, sums):
    rows = one.shape[0]
    step = math.gcd(rows, 256)
    for at in range(0, rows, step):
        cols = slice(at, at + step)
        inner = lax.dot_general(one[...], two[cols, :], NT, preferred_element_type=jnp.float32)
        weighted = inner * gram[:, cols]
        sums[:, cols] = weighted.reshape(rows // TOK, TOK, step).sum(axis=1)


def two_parts(value):
    high = value.astype(jnp.bfloat16)
    return high, (value - high.astype(jnp.float32)).astype(jnp.bfloat16)


def dot_parts(value, table):
    high, low = two_parts(value)
    return lax.dot_general(low, table, NT, preferred_element_type=jnp.float32) + lax.dot_general(
        high, table, NT, preferred_element_type=jnp.float32
    )


def domain_sums(pairs, factor, flags, info, info_v, sums, table):
    count, examples, rows = sums.shape
    example = lax.broadcasted_iota(jnp.int32, (LANES, rows), 0)
    gather = (lax.broadcasted_iota(jnp.int32, (LANES, rows), 1) // TOK == example)
    tiles = dot_parts(sums[...].reshape(count * examples, rows), gather.astype(jnp.bfloat16))
    tiles = tiles.reshape(count, examples, LANES)
    core, side = flags[4], flags[5]
    table[...] = jnp.zeros_like(table)
    pad = jnp.zeros((LANES - examples, LANES), jnp.float32)
    for at, pair in enumerate(pairs):
        one, two, apart = PAIRS[pair]
        here, there = info[one, examples + apart], info[two, examples + apart]
        own = (one, two) == (XS, XC)
        flag = jnp.where((core if own else side) == 0, here, there)
        tile = jnp.concatenate([tiles[at], pad], axis=0) * (flag.astype(jnp.float32) * factor)
        table[one * LANES:(one + 1) * LANES, two * LANES:(two + 1) * LANES] = tile
        table[two * LANES:(two + 1) * LANES, one * LANES:(one + 1) * LANES] = tile.T
    row = lax.broadcasted_iota(jnp.int32, (LANES, LANES), 0)
    inside = lax.broadcasted_iota(jnp.int32, (LANES, LANES), 1) < examples
    hot = jnp.concatenate(
        [((info_v[block:block + 1, :] == row) & inside).astype(jnp.bfloat16) for block in range(6)],
        axis=1,
    )
    return dot_parts(table[...], hot)


def staged(loads, sems, plan):
    copies = {
        key: pltpu.make_async_copy(source, target, sems.at[at])
        for at, (key, (source, target)) in enumerate(loads.items())
    }

    def start(at):
        if at < len(plan):
            for key in plan[at][0]:
                copies[key].start()

    def ready(at):
        if at == 0:
            start(0)
        for key in plan[at][0]:
            copies[key].wait()
        start(at + 1)

    return ready


def first_kernel(factor, flags, info, info_v, acts, x_half, ys, zs, gram, out,
                 xs_v, xc_v, ys_v, zs_v, own_v, half_v, gram_v, sums, table, sems):
    mirrored, work_at, half_at, in_half = flags[0], flags[1], flags[2], flags[3]
    quarter = ys.shape[1]
    loads = {
        "xs": (acts.at[:, pl.ds(pl.multiple_of(work_at, LANES), quarter)], xs_v),
        "ys": (ys, ys_v),
        "g0": (gram.at[0], gram_v.at[0]),
        "zs": (zs, zs_v),
        "g1": (gram.at[1], gram_v.at[1]),
        "xc": (x_half.at[:, pl.ds(pl.multiple_of(in_half, LANES), quarter)], xc_v),
        "g2": (gram.at[2], gram_v.at[2]),
        "own": (acts.at[:, pl.ds(pl.multiple_of(half_at, LANES), 2 * quarter)], own_v),
        "half": (x_half, half_v),
        "g3": (gram.at[3], gram_v.at[3]),
    }
    plan = (
        (("xs", "ys", "g0"), xs_v, ys_v),
        (("zs", "g1"), ys_v, zs_v),
        (("xc", "g2"), xc_v, ys_v),
        (("own", "half", "g3"), own_v, half_v),
    )
    ready = staged(loads, sems, plan)
    for at, pair in enumerate(FIRST):
        _, one, two = plan[at]
        ready(at)
        if pair in ONLY:
            sums[at] = jnp.zeros(sums.shape[1:], jnp.float32)
        guarded(pair, mirrored, functools.partial(token_sums, one, two, gram_v.at[at], sums.at[at]))
    out[...] = domain_sums(FIRST, factor, flags, info, info_v, sums, table)


def second_kernel(factor, flags, info, info_v, earlier, acts, x_half, ys, yc, zs, zc, gram,
                  *rest):
    outs = rest[:6]
    xs_v, xc_v, ys_v, yc_v, zs_v, zc_v, gram_v, sums, table, sems = rest[6:]
    mirrored, work_at, in_half = flags[0], flags[1], flags[3]
    quarter = ys.shape[1]
    loads = {
        "yc": (yc, yc_v),
        "xc": (x_half.at[:, pl.ds(pl.multiple_of(in_half, LANES), quarter)], xc_v),
        "g4": (gram.at[4], gram_v.at[0]),
        "zc": (zc, zc_v),
        "g5": (gram.at[5], gram_v.at[1]),
        "ys": (ys, ys_v),
        "zs": (zs, zs_v),
        "g6": (gram.at[6], gram_v.at[2]),
        "xs": (acts.at[:, pl.ds(pl.multiple_of(work_at, LANES), quarter)], xs_v),
        "g2": (gram.at[2], gram_v.at[3]),
    }
    plan = (
        (("yc", "xc", "g4"), xc_v, yc_v, 0),
        (("zc", "g5"), yc_v, zc_v, 1),
        (("ys", "zs", "g6"), yc_v, zs_v, 2),
        (("xs", "g2"), ys_v, zc_v, 2),
        ((), xs_v, yc_v, 3),
    )
    ready = staged(loads, sems, plan)
    for at, pair in enumerate(SECOND):
        _, one, two, slot = plan[at]
        ready(at)
        if pair in ONLY:
            sums[at] = jnp.zeros(sums.shape[1:], jnp.float32)
        guarded(pair, mirrored, functools.partial(token_sums, one, two, gram_v.at[slot], sums.at[at]))
    total = (earlier[...] + domain_sums(SECOND, factor, flags, info, info_v, sums, table)).T
    examples = sums.shape[1]
    for block, out in enumerate(outs):
        out[...] = total[:DOMAINS, block * LANES:block * LANES + examples]


def per_device(acts, grads, domain, listed):
    rows, width = acts.shape
    examples = rows // TOK
    quarter = width // 4
    me = lax.axis_index("ex")
    core = me % 2
    side = (me // 2) % 2
    mirrored = core ^ side

    def work_at(side_at, core_at):
        return core_at * 2 * quarter + (1 - side_at) * quarter

    flags = jnp.stack([
        mirrored, work_at(side, core), core * 2 * quarter, (1 - side) * quarter, core, side
    ]).astype(jnp.int32)
    places = jnp.stack([
        core * 2 + side,
        core * 2 + (1 - side),
        1 - core,
        (1 - core) * 2 + side,
        (1 - core) * 2 + (1 - side),
    ]).astype(jnp.int32)

    grads_ys = send(grads, across, 0)
    grads_zs = send(grads, along, 0)
    cut_ys, cut_zs, cut_xh, cut_yc, cut_zc = cut(acts, places)
    ys = send(cut_ys, across, 0)
    zs = send(cut_zs, along, 0)
    grads_xc = send(grads, stay, 1)
    x_half = send(cut_xh, stay, 1)
    yc = send(cut_yc, across, 1)
    zc = send(cut_zc, along, 1)
    grads_yc = send(grads_ys, stay, 1)
    grads_zc = send(grads_zs, stay, 1)

    own_info = jnp.concatenate(
        [domain, listed[0], jnp.zeros((LANES - examples - 2,), jnp.int32)]
    )[None, :]
    info = jnp.concatenate([
        own_info,
        send(own_info, stay, 1),
        send(own_info, across, 0),
        send(own_info, across, 1),
        send(own_info, along, 0),
        send(own_info, along, 1),
    ])
    factor = 1.0 / (TOK * math.sqrt(width * grads.shape[1]))

    gram = grams(flags, (grads, grads_xc, grads_ys, grads_yc, grads_zs, grads_zc))

    smem = pl.BlockSpec(memory_space=pltpu.SMEM)
    vmem = pl.BlockSpec(memory_space=pltpu.VMEM)
    hbm = pl.BlockSpec(memory_space=pl.ANY)
    params = pltpu.CompilerParams(vmem_limit_bytes=VMEM_BYTES)
    slice_v = pltpu.VMEM((rows, quarter), acts.dtype)
    half_v = pltpu.VMEM((rows, 2 * quarter), acts.dtype)
    gram_v = pltpu.VMEM((4, rows, rows), jnp.float32)
    table_v = pltpu.VMEM((6 * LANES, 6 * LANES), jnp.float32)
    first = pl.pallas_call(
        functools.partial(first_kernel, factor),
        in_specs=[smem, smem, vmem] + [hbm] * 5,
        out_specs=vmem,
        out_shape=jax.ShapeDtypeStruct((6 * LANES, LANES), jnp.float32),
        scratch_shapes=[slice_v] * 4 + [half_v] * 2 + [
            gram_v,
            pltpu.VMEM((4, examples, rows), jnp.float32),
            table_v,
            pltpu.SemaphoreType.DMA((10,)),
        ],
        compiler_params=params,
        cost_estimate=pl.CostEstimate(
            flops=10 * rows * rows * quarter,
            bytes_accessed=20 * rows * quarter + 16 * rows * rows,
            transcendentals=0,
        ),
        name="first",
    )(flags, info, info, acts, x_half, ys, zs, gram)
    sums = pl.pallas_call(
        functools.partial(second_kernel, factor),
        in_specs=[smem, smem, vmem, vmem] + [hbm] * 7,
        out_specs=[vmem] * 6,
        out_shape=[jax.ShapeDtypeStruct((DOMAINS, examples), jnp.float32)] * 6,
        scratch_shapes=[slice_v] * 6 + [
            gram_v,
            pltpu.VMEM((5, examples, rows), jnp.float32),
            table_v,
            pltpu.SemaphoreType.DMA((10,)),
        ],
        compiler_params=params,
        cost_estimate=pl.CostEstimate(
            flops=8 * rows * rows * quarter,
            bytes_accessed=12 * rows * quarter + 16 * rows * rows,
            transcendentals=0,
        ),
        name="second",
    )(flags, info, info, first, acts, x_half, ys, yc, zs, zc, gram)

    total = sums[XS]
    total = total + send(sums[XC], stay, 1)
    total = total + send(sums[YS], across, 0)
    total = total + send(sums[YC], across, 1)
    total = total + send(sums[ZS], against, 0)
    total = total + send(sums[ZC], against, 1)
    return total.T


def solution(mesh):
    in_specs = (
        P(("groups", "ex"), None),
        P(("groups", "ex"), None),
        P(("groups", "ex")),
        P(("groups", "ex"), None),
    )
    out_specs = P(("groups", "ex"), None)
    return jax.shard_map(
        per_device, mesh=mesh, in_specs=in_specs, out_specs=out_specs, check_vma=False
    )
```

```python
import functools
import math

import jax
import jax.numpy as jnp
from jax import lax
from jax.experimental import pallas as pl
from jax.experimental.pallas import tpu as pltpu
from jax.sharding import PartitionSpec as P

TOK = 8
DOMAINS = 48
LANES = 128
VMEM_BYTES = 40 * 1024 * 1024
CUT_VMEM_BYTES = 60 * 1024 * 1024

INFO = 16

XS, XC, YS, YC, ZS, ZC = range(6)
PAIRS = (
    (YS, XS, 1), (YS, ZS, 1), (YS, XC, 0), (XC, XS, 0),
    (YC, XC, 1), (YC, ZC, 1), (YC, ZS, 0), (YS, ZC, 0), (YC, XS, 0),
)
ONLY = {2: 0, 6: 0, 7: 1, 8: 1}
SLOT = (0, 1, 2, 3, 4, 5, 6, 6, 2)
FIRST = (0, 1, 2, 3)
SECOND = (4, 5, 6, 7, 8)
SMALL = pl.CostEstimate(flops=1, bytes_accessed=1, transcendentals=0)
NT = (((1,), (1,)), ((), ()))


def across(chip):
    return chip ^ 1


def along(chip):
    return chip + 2 if chip & 1 else chip - 2


def against(chip):
    return chip - 2 if chip & 1 else chip + 2


def stay(chip):
    return chip


def send(value, move, flip):
    chips = lax.axis_size("ex") // 2
    pairs = [
        (2 * chip + core, 2 * (move(chip) % chips) + (core ^ flip))
        for chip in range(chips)
        for core in range(2)
    ]
    return lax.ppermute(value, "ex", pairs)


def token_major(rows):
    to = lax.broadcasted_iota(jnp.int32, (rows, rows), 0)
    source = lax.broadcasted_iota(jnp.int32, (rows, rows), 1)
    examples = rows // TOK
    return ((source % TOK) * examples + source // TOK == to).astype(jnp.bfloat16)


def reorder(order, block):
    return jnp.dot(order, block, preferred_element_type=jnp.float32).astype(jnp.bfloat16)


def put(target, value, info):
    rows = value.shape[0]
    target[:rows, :] = value
    target[rows:, :] = jnp.concatenate([info[...]] * (target.shape[1] // LANES), axis=1)


def cut_kernel(steps, places, info, y_acts, z_acts, grads, y_out, z_out, order):
    step = pl.program_id(0)

    @pl.when(step == 0)
    def _():
        order[...] = token_major(order.shape[0])

    @pl.when(step < steps)
    def _():
        put(y_out, reorder(order[...], y_acts[...]), info)
        put(z_out, z_acts[...], info)

    @pl.when(step >= steps)
    def _():
        put(y_out, reorder(order[...], grads[...]), info)
        put(z_out, grads[...], info)


def cut(acts, grads, info, places, with_grads):
    rows, width = acts.shape
    quarter, depth = width // 4, grads.shape[1]
    step = math.gcd(math.gcd(quarter, depth), 256)
    steps = quarter // step
    more = depth // step if with_grads else 0
    block = (rows, step)
    return pl.pallas_call(
        functools.partial(cut_kernel, steps),
        grid_spec=pltpu.PrefetchScalarGridSpec(
            num_scalar_prefetch=1,
            grid=(steps + more,),
            in_specs=[
                pl.BlockSpec((INFO, LANES), lambda i, p: (0, 0)),
                pl.BlockSpec(block, lambda i, p: (0, p[0] * steps + jnp.minimum(i, steps - 1))),
                pl.BlockSpec(block, lambda i, p: (0, p[1] * steps + jnp.minimum(i, steps - 1))),
                pl.BlockSpec(block, lambda i, p: (0, jnp.maximum(i - steps, 0))),
            ],
            out_specs=[pl.BlockSpec((rows + INFO, step), lambda i, p: (0, i))] * 2,
            scratch_shapes=[pltpu.VMEM((rows, rows), jnp.bfloat16)],
        ),
        out_shape=[
            jax.ShapeDtypeStruct((rows + INFO, quarter + more * step), acts.dtype)
        ] * 2,
        compiler_params=pltpu.CompilerParams(vmem_limit_bytes=CUT_VMEM_BYTES),
        cost_estimate=SMALL,
        name="cut",
    )(places, info, acts, acts, grads)


def half_kernel(steps, place, info, acts, grads, out):
    @pl.when(pl.program_id(0) < steps)
    def _():
        put(out, acts[...], info)

    @pl.when(pl.program_id(0) >= steps)
    def _():
        put(out, grads[...], info)


def cut_half(acts, grads, info, place):
    rows, width = acts.shape
    half, depth = width // 2, grads.shape[1]
    step = math.gcd(math.gcd(half, depth), 512)
    steps = half // step
    return pl.pallas_call(
        functools.partial(half_kernel, steps),
        grid_spec=pltpu.PrefetchScalarGridSpec(
            num_scalar_prefetch=1,
            grid=(steps + depth // step,),
            in_specs=[
                pl.BlockSpec((INFO, LANES), lambda i, p: (0, 0)),
                pl.BlockSpec((rows, step), lambda i, p: (0, p[0] * steps + jnp.minimum(i, steps - 1))),
                pl.BlockSpec((rows, step), lambda i, p: (0, jnp.maximum(i - steps, 0))),
            ],
            out_specs=pl.BlockSpec((rows + INFO, step), lambda i, p: (0, i)),
        ),
        out_shape=jax.ShapeDtypeStruct((rows + INFO, half + depth), acts.dtype),
        compiler_params=pltpu.CompilerParams(vmem_limit_bytes=CUT_VMEM_BYTES),
        cost_estimate=SMALL,
        name="half",
    )(place, info, acts, grads)


def guarded(pair, mirrored, work):
    if pair in ONLY:
        pl.when(mirrored == ONLY[pair])(work)
    else:
        work()


def grams_kernel(flags, xs, xc, ys, yc, zs, zc, out, held, result, in_sems, out_sems):
    mirrored = flags[0]
    rows, depth = xs.shape
    sources = [xs] + [
        message.at[:rows, message.shape[1] - depth:] for message in (xc, ys, yc, zs, zc)
    ]
    loads = [
        pltpu.make_async_copy(source, held.at[at], in_sems.at[at])
        for at, source in enumerate(sources)
    ]
    for load in loads:
        load.start()
    for load in loads:
        load.wait()
    for pair, (one, two, _) in enumerate(PAIRS):
        slot = SLOT[pair]

        def work(one=one, two=two, slot=slot):
            result[slot] = lax.dot_general(
                held[one], held[two], NT, preferred_element_type=jnp.float32
            )
            pltpu.make_async_copy(result.at[slot], out.at[slot], out_sems.at[slot]).start()

        guarded(pair, mirrored, work)
    for slot in range(7):
        pltpu.make_async_copy(result.at[slot], out.at[slot], out_sems.at[slot]).wait()


def grams(flags, grads, *messages):
    rows, width = grads.shape
    return pl.pallas_call(
        grams_kernel,
        in_specs=[pl.BlockSpec(memory_space=pltpu.SMEM)] + [pl.BlockSpec(memory_space=pl.ANY)] * 6,
        out_specs=pl.BlockSpec(memory_space=pl.ANY),
        out_shape=jax.ShapeDtypeStruct((7, rows, rows), jnp.float32),
        scratch_shapes=[
            pltpu.VMEM((6, rows, width), grads.dtype),
            pltpu.VMEM((7, rows, rows), jnp.float32),
            pltpu.SemaphoreType.DMA((6,)),
            pltpu.SemaphoreType.DMA((7,)),
        ],
        compiler_params=pltpu.CompilerParams(vmem_limit_bytes=VMEM_BYTES),
        cost_estimate=SMALL,
        name="grams",
    )(flags, grads, *messages)


def token_sums(one, two, gram, sums, ordered=True):
    examples, rows = sums.shape
    step = math.gcd(rows, 256)
    for at in range(0, rows, step):
        cols = slice(at, at + step)
        inner = lax.dot_general(
            one[:rows, :], two[cols, :], NT, preferred_element_type=jnp.float32
        )
        weighted = inner * gram[:, cols]
        if ordered:
            total = weighted[:examples]
            for token in range(1, TOK):
                total = total + weighted[token * examples:(token + 1) * examples]
        else:
            total = weighted.reshape(examples, TOK, step).sum(axis=1)
        sums[:, cols] = total


def two_parts(value):
    high = value.astype(jnp.bfloat16)
    return high, (value - high.astype(jnp.float32)).astype(jnp.bfloat16)


def dot_parts(value, table):
    high, low = two_parts(value)
    return lax.dot_general(low, table, NT, preferred_element_type=jnp.float32) + lax.dot_general(
        high, table, NT, preferred_element_type=jnp.float32
    )


def domain_sums(pairs, factor, flags, info, sums, table):
    count, examples, rows = sums.shape
    example = lax.broadcasted_iota(jnp.int32, (LANES, rows), 0)
    gather = (lax.broadcasted_iota(jnp.int32, (LANES, rows), 1) // TOK == example)
    tiles = dot_parts(sums[...].reshape(count * examples, rows), gather.astype(jnp.bfloat16))
    tiles = tiles.reshape(count, examples, LANES)
    core, side = flags[3], flags[4]
    lane = lax.broadcasted_iota(jnp.int32, (1, LANES), 1)

    def listed_flag(block, apart):
        return jnp.sum(jnp.where(lane == examples + apart, info[block], 0.0), axis=1, keepdims=True)

    table[...] = jnp.zeros_like(table)
    pad = jnp.zeros((LANES - examples, LANES), jnp.float32)
    for at, pair in enumerate(pairs):
        one, two, apart = PAIRS[pair]
        if one == XC:
            two_leads = core == 0
        elif two in (XS, XC):
            two_leads = side == 0
        else:
            two_leads = side == 1
        flag = jnp.where(two_leads, listed_flag(two, apart), listed_flag(one, apart))
        tile = jnp.concatenate([tiles[at], pad], axis=0) * (flag * factor)
        table[one * LANES:(one + 1) * LANES, two * LANES:(two + 1) * LANES] = tile
        table[two * LANES:(two + 1) * LANES, one * LANES:(one + 1) * LANES] = tile.T
    row = lax.broadcasted_iota(jnp.int32, (LANES, LANES), 0)
    hot = jnp.concatenate(
        [
            ((info[block].astype(jnp.int32) == row) & (lane < examples)).astype(jnp.bfloat16)
            if block in info else jnp.zeros((LANES, LANES), jnp.bfloat16)
            for block in range(6)
        ],
        axis=1,
    )
    return dot_parts(table[...], hot)


def staged(loads, sems, plan):
    copies = {
        key: pltpu.make_async_copy(source, target, sems.at[at])
        for at, (key, (source, target)) in enumerate(loads.items())
    }

    def start(at):
        if at < len(plan):
            for key in plan[at][0]:
                copies[key].start()

    def ready(at):
        if at == 0:
            start(0)
        for key in plan[at][0]:
            copies[key].wait()
        start(at + 1)

    return ready


def info_row(message, rows):
    return message[rows:rows + INFO, :LANES].astype(jnp.float32)[:1]


def first_kernel(factor, flags, xs, acts, x_half, ys, zs, gram, out,
                 xs_v, xc_v, ys_v, zs_v, own_v, half_v, gram_v, sums, table, sems):
    mirrored, half_at, in_half = flags[0], flags[1], flags[2]
    quarter = xs_v.shape[1]
    loads = {
        "xs": (xs.at[:, :quarter], xs_v),
        "ys": (ys.at[:, :quarter], ys_v),
        "g0": (gram.at[0], gram_v.at[0]),
        "zs": (zs.at[:, :quarter], zs_v),
        "g1": (gram.at[1], gram_v.at[1]),
        "xc": (x_half.at[:, pl.ds(pl.multiple_of(in_half, LANES), quarter)], xc_v),
        "g2": (gram.at[2], gram_v.at[2]),
        "own": (acts.at[:, pl.ds(pl.multiple_of(half_at, LANES), 2 * quarter)], own_v),
        "half": (x_half.at[:, :2 * quarter], half_v),
        "g3": (gram.at[3], gram_v.at[3]),
    }
    plan = (
        (("xs", "ys", "g0"), ys_v, xs_v),
        (("zs", "g1"), ys_v, zs_v),
        (("xc", "g2"), ys_v, xc_v),
        (("own", "half", "g3"), half_v, own_v),
    )
    ready = staged(loads, sems, plan)
    for at, pair in enumerate(FIRST):
        _, one, two = plan[at]
        ready(at)
        if pair in ONLY:
            sums[at] = jnp.zeros(sums.shape[1:], jnp.float32)
        guarded(pair, mirrored, functools.partial(
            token_sums, one, two, gram_v.at[at], sums.at[at], PAIRS[pair][0] != XC))
    rows = sums.shape[2]
    info = {XS: info_row(xs_v, rows), XC: info_row(xc_v, rows),
            YS: info_row(ys_v, rows), ZS: info_row(zs_v, rows)}
    out[...] = domain_sums(FIRST, factor, flags, info, sums, table)


def second_kernel(factor, flags, earlier, xs, x_half, ys, yc, zs, zc, gram, *rest):
    outs = rest[:6]
    xs_v, xc_v, ys_v, yc_v, zs_v, zc_v, gram_v, sums, table, sems = rest[6:]
    mirrored, in_half = flags[0], flags[2]
    quarter = xs_v.shape[1]
    loads = {
        "yc": (yc, yc_v),
        "xc": (x_half.at[:, pl.ds(pl.multiple_of(in_half, LANES), quarter)], xc_v),
        "g4": (gram.at[4], gram_v.at[0]),
        "zc": (zc, zc_v),
        "g5": (gram.at[5], gram_v.at[1]),
        "ys": (ys.at[:, :quarter], ys_v),
        "zs": (zs.at[:, :quarter], zs_v),
        "g6": (gram.at[6], gram_v.at[2]),
        "xs": (xs.at[:, :quarter], xs_v),
        "g2": (gram.at[2], gram_v.at[3]),
    }
    plan = (
        (("yc", "xc", "g4"), yc_v, xc_v, 0),
        (("zc", "g5"), yc_v, zc_v, 1),
        (("ys", "zs", "g6"), yc_v, zs_v, 2),
        (("xs", "g2"), ys_v, zc_v, 2),
        ((), yc_v, xs_v, 3),
    )
    ready = staged(loads, sems, plan)
    for at, pair in enumerate(SECOND):
        _, one, two, slot = plan[at]
        ready(at)
        if pair in ONLY:
            sums[at] = jnp.zeros(sums.shape[1:], jnp.float32)
        guarded(pair, mirrored, functools.partial(token_sums, one, two, gram_v.at[slot], sums.at[at]))
    examples, rows = sums.shape[1:]
    info = {
        block: info_row(message, rows)
        for block, message in enumerate((xs_v, xc_v, ys_v, yc_v, zs_v, zc_v))
    }
    total = (earlier[...] + domain_sums(SECOND, factor, flags, info, sums, table)).T
    for block, out in enumerate(outs):
        out[...] = total[:DOMAINS, block * LANES:block * LANES + examples]


def per_device(acts, grads, domain, listed):
    rows, width = acts.shape
    examples = rows // TOK
    quarter = width // 4
    me = lax.axis_index("ex")
    core = me % 2
    side = (me // 2) % 2
    mirrored = core ^ side

    flags = jnp.stack([
        mirrored, core * 2 * quarter, (1 - side) * quarter, core, side
    ]).astype(jnp.int32)
    places = jnp.stack([core * 2 + side, core * 2 + (1 - side)]).astype(jnp.int32)
    cross_places = jnp.stack([(1 - core) * 2 + side, (1 - core) * 2 + (1 - side)]).astype(jnp.int32)
    half_place = jnp.stack([1 - core]).astype(jnp.int32)

    own_info = jnp.concatenate(
        [domain, listed[0], jnp.zeros((LANES - examples - 2,), jnp.int32)]
    )
    own_info = jnp.broadcast_to(own_info.astype(acts.dtype)[None, :], (INFO, LANES))

    cut_ys, cut_zs = cut(acts, grads, own_info, places, True)
    ys = send(cut_ys, across, 0)
    zs = send(cut_zs, along, 0)
    own_info, _ = lax.optimization_barrier((own_info, cut_ys))
    x_half = send(cut_half(acts, grads, own_info, half_place), stay, 1)
    cut_yc, cut_zc = cut(acts, grads, own_info, cross_places, False)
    yc = send(cut_yc, across, 1)
    zc = send(cut_zc, along, 1)
    grads_yc = send(ys[:, quarter:], stay, 1)
    grads_zc = send(zs[:, quarter:], stay, 1)
    factor = 1.0 / (TOK * math.sqrt(width * grads.shape[1]))

    gram = grams(flags, grads, x_half, ys, grads_yc, zs, grads_zc)

    smem = pl.BlockSpec(memory_space=pltpu.SMEM)
    vmem = pl.BlockSpec(memory_space=pltpu.VMEM)
    hbm = pl.BlockSpec(memory_space=pl.ANY)
    params = pltpu.CompilerParams(vmem_limit_bytes=VMEM_BYTES)
    slice_v = pltpu.VMEM((rows + INFO, quarter), acts.dtype)
    half_v = pltpu.VMEM((rows + INFO, 2 * quarter), acts.dtype)
    own_v = pltpu.VMEM((rows, 2 * quarter), acts.dtype)
    gram_v = pltpu.VMEM((4, rows, rows), jnp.float32)
    table_v = pltpu.VMEM((6 * LANES, 6 * LANES), jnp.float32)
    first = pl.pallas_call(
        functools.partial(first_kernel, factor),
        in_specs=[smem] + [hbm] * 6,
        out_specs=vmem,
        out_shape=jax.ShapeDtypeStruct((6 * LANES, LANES), jnp.float32),
        scratch_shapes=[slice_v] * 4 + [own_v, half_v] + [
            gram_v,
            pltpu.VMEM((4, examples, rows), jnp.float32),
            table_v,
            pltpu.SemaphoreType.DMA((10,)),
        ],
        compiler_params=params,
        cost_estimate=SMALL,
        name="first",
    )(flags, cut_zs, acts, x_half, ys, zs, gram)
    sums = pl.pallas_call(
        functools.partial(second_kernel, factor),
        in_specs=[smem, vmem] + [hbm] * 7,
        out_specs=[vmem] * 6,
        out_shape=[jax.ShapeDtypeStruct((DOMAINS, examples), jnp.float32)] * 6,
        scratch_shapes=[slice_v] * 6 + [
            gram_v,
            pltpu.VMEM((5, examples, rows), jnp.float32),
            table_v,
            pltpu.SemaphoreType.DMA((10,)),
        ],
        compiler_params=params,
        cost_estimate=SMALL,
        name="second",
    )(flags, first, cut_zs, x_half, ys, yc, zs, zc, gram)

    total = sums[XS]
    total = total + send(sums[XC], stay, 1)
    total = total + send(sums[YS], across, 0)
    total = total + send(sums[YC], across, 1)
    total = total + send(sums[ZS], against, 0)
    total = total + send(sums[ZC], against, 1)
    return total.T


def solution(mesh):
    in_specs = (
        P(("groups", "ex"), None),
        P(("groups", "ex"), None),
        P(("groups", "ex")),
        P(("groups", "ex"), None),
    )
    out_specs = P(("groups", "ex"), None)
    return jax.shard_map(
        per_device, mesh=mesh, in_specs=in_specs, out_specs=out_specs, check_vma=False
    )
```

```python
import functools
import math

import jax
import jax.numpy as jnp
from jax import lax
from jax.experimental import pallas as pl
from jax.experimental.pallas import tpu as pltpu
from jax.sharding import PartitionSpec as P

TOK = 8
DOMAINS = 48
LANES = 128
VMEM_BYTES = 40 * 1024 * 1024
CUT_VMEM_BYTES = 60 * 1024 * 1024

INFO = 16

XS, XC, YS, YC, ZS, ZC = range(6)
PAIRS = (
    (YS, XS, 1), (YS, ZS, 1), (YS, XC, 0), (XC, XS, 0),
    (YC, XC, 1), (YC, ZC, 1), (YC, ZS, 0), (YS, ZC, 0), (YC, XS, 0),
)
ONLY = {2: 0, 6: 0, 7: 1, 8: 1}
SLOT = (0, 1, 2, 3, 4, 5, 6, 6, 2)
FIRST = (0, 1, 2, 3)
SMALL = pl.CostEstimate(flops=1, bytes_accessed=1, transcendentals=0)
NT = (((1,), (1,)), ((), ()))


def across(chip):
    return chip ^ 1


def along(chip):
    return chip + 2 if chip & 1 else chip - 2


def against(chip):
    return chip - 2 if chip & 1 else chip + 2


def stay(chip):
    return chip


def send(value, move, flip):
    chips = lax.axis_size("ex") // 2
    pairs = [
        (2 * chip + core, 2 * (move(chip) % chips) + (core ^ flip))
        for chip in range(chips)
        for core in range(2)
    ]
    return lax.ppermute(value, "ex", pairs)


def token_major(rows):
    to = lax.broadcasted_iota(jnp.int32, (rows, rows), 0)
    source = lax.broadcasted_iota(jnp.int32, (rows, rows), 1)
    examples = rows // TOK
    return ((source % TOK) * examples + source // TOK == to).astype(jnp.bfloat16)


def reorder(order, block):
    return jnp.dot(order, block, preferred_element_type=jnp.float32).astype(jnp.bfloat16)


def put(target, value, info):
    rows = value.shape[0]
    target[:rows, :] = value
    target[rows:, :] = jnp.concatenate([info[...]] * (target.shape[1] // LANES), axis=1)


def cut_kernel(places, info, y_acts, z_acts, y_one, z_one, y_two, z_two, order):
    order[...] = token_major(order.shape[0])
    for step, (y_out, z_out) in enumerate(((y_one, z_one), (y_two, z_two))):
        @pl.when(pl.program_id(0) == step)
        def _():
            put(y_out, reorder(order[...], y_acts[...]), info)
            put(z_out, z_acts[...], info)


def cut(acts, info, places):
    rows, width = acts.shape
    eighth = width // 8
    block = (rows, eighth)
    return pl.pallas_call(
        cut_kernel,
        grid_spec=pltpu.PrefetchScalarGridSpec(
            num_scalar_prefetch=1,
            grid=(2,),
            in_specs=[
                pl.BlockSpec((INFO, LANES), lambda i, p: (0, 0)),
                pl.BlockSpec(block, lambda i, p: (0, 2 * p[0] + i)),
                pl.BlockSpec(block, lambda i, p: (0, 2 * p[1] + i)),
            ],
            out_specs=[pl.BlockSpec((rows + INFO, eighth), lambda i, p: (0, 0))] * 4,
            scratch_shapes=[pltpu.VMEM((rows, rows), jnp.bfloat16)],
        ),
        out_shape=[jax.ShapeDtypeStruct((rows + INFO, eighth), acts.dtype)] * 4,
        compiler_params=pltpu.CompilerParams(vmem_limit_bytes=CUT_VMEM_BYTES),
        cost_estimate=SMALL,
        name="cut",
    )(places, info, acts, acts)


def half_kernel(steps, place, info, acts, grads, out):
    @pl.when(pl.program_id(0) < steps)
    def _():
        put(out, acts[...], info)

    @pl.when(pl.program_id(0) >= steps)
    def _():
        put(out, grads[...], info)


def cut_half(acts, grads, info, place):
    rows, width = acts.shape
    half, depth = width // 2, grads.shape[1]
    step = math.gcd(math.gcd(half, depth), 512)
    steps = half // step
    return pl.pallas_call(
        functools.partial(half_kernel, steps),
        grid_spec=pltpu.PrefetchScalarGridSpec(
            num_scalar_prefetch=1,
            grid=(steps + depth // step,),
            in_specs=[
                pl.BlockSpec((INFO, LANES), lambda i, p: (0, 0)),
                pl.BlockSpec((rows, step), lambda i, p: (0, p[0] * steps + jnp.minimum(i, steps - 1))),
                pl.BlockSpec((rows, step), lambda i, p: (0, jnp.maximum(i - steps, 0))),
            ],
            out_specs=pl.BlockSpec((rows + INFO, step), lambda i, p: (0, i)),
        ),
        out_shape=jax.ShapeDtypeStruct((rows + INFO, half + depth), acts.dtype),
        compiler_params=pltpu.CompilerParams(vmem_limit_bytes=CUT_VMEM_BYTES),
        cost_estimate=SMALL,
        name="half",
    )(place, info, acts, grads)


def guarded(pair, mirrored, work):
    if pair in ONLY:
        pl.when(mirrored == ONLY[pair])(work)
    else:
        work()


def grams_kernel(flags, xs, xc, ys, yc, zs, zc, out, held, result, in_sems, out_sems):
    mirrored = flags[0]
    rows, depth = xs.shape
    order = token_major(rows)
    sources = (xs, xc.at[:rows, xc.shape[1] - depth:], ys, yc, zs, zc)
    loads = [
        pltpu.make_async_copy(source, held.at[at], in_sems.at[at])
        for at, source in enumerate(sources)
    ]
    for load in loads:
        load.start()
    for load in loads:
        load.wait()
    for block in (YS, YC):
        held[block] = reorder(order, held[block])
    for pair, (one, two, _) in enumerate(PAIRS):
        slot = SLOT[pair]

        def work(one=one, two=two, slot=slot):
            result[slot] = lax.dot_general(
                held[one], held[two], NT, preferred_element_type=jnp.float32
            )
            pltpu.make_async_copy(result.at[slot], out.at[slot], out_sems.at[slot]).start()

        guarded(pair, mirrored, work)
    for slot in range(7):
        pltpu.make_async_copy(result.at[slot], out.at[slot], out_sems.at[slot]).wait()


def grams(flags, grads, *messages):
    rows, width = grads.shape
    return pl.pallas_call(
        grams_kernel,
        in_specs=[pl.BlockSpec(memory_space=pltpu.SMEM)] + [pl.BlockSpec(memory_space=pl.ANY)] * 6,
        out_specs=pl.BlockSpec(memory_space=pl.ANY),
        out_shape=jax.ShapeDtypeStruct((7, rows, rows), jnp.float32),
        scratch_shapes=[
            pltpu.VMEM((6, rows, width), grads.dtype),
            pltpu.VMEM((7, rows, rows), jnp.float32),
            pltpu.SemaphoreType.DMA((6,)),
            pltpu.SemaphoreType.DMA((7,)),
        ],
        compiler_params=pltpu.CompilerParams(vmem_limit_bytes=VMEM_BYTES),
        cost_estimate=SMALL,
        name="grams",
    )(flags, grads, *messages)


def product(one, two, inner):
    rows = inner.shape[0]
    inner[...] = lax.dot_general(
        one[:rows, :], two[:rows, :], NT, preferred_element_type=jnp.float32
    )


def token_sums(inner, gram, sums, ordered=True):
    examples, rows = sums.shape
    if ordered:
        sums[...] = sum(
            inner[at:at + examples, :] * gram[at:at + examples, :]
            for at in range(0, rows, examples)
        )
    else:
        weighted = inner[...] * gram[...]
        sums[...] = weighted.reshape(examples, TOK, rows).sum(axis=1)


def two_parts(value):
    high = value.astype(jnp.bfloat16)
    return high, (value - high.astype(jnp.float32)).astype(jnp.bfloat16)


def dot_parts(value, table):
    high, low = two_parts(value)
    return lax.dot_general(low, table, NT, preferred_element_type=jnp.float32) + lax.dot_general(
        high, table, NT, preferred_element_type=jnp.float32
    )


def domain_sums(pairs, factor, flags, info, sums, table):
    count, examples, rows = sums.shape
    example = lax.broadcasted_iota(jnp.int32, (LANES, rows), 0)
    gather = (lax.broadcasted_iota(jnp.int32, (LANES, rows), 1) // TOK == example)
    tiles = dot_parts(sums[...].reshape(count * examples, rows), gather.astype(jnp.bfloat16))
    tiles = tiles.reshape(count, examples, LANES)
    core, side = flags[3], flags[4]
    lane = lax.broadcasted_iota(jnp.int32, (1, LANES), 1)

    def listed_flag(block, apart):
        return jnp.sum(jnp.where(lane == examples + apart, info[block], 0.0), axis=1, keepdims=True)

    table[...] = jnp.zeros_like(table)
    pad = jnp.zeros((LANES - examples, LANES), jnp.float32)
    for at, pair in pairs:
        one, two, apart = PAIRS[pair]
        if one == XC:
            two_leads = core == 0
        elif two in (XS, XC):
            two_leads = side == 0
        else:
            two_leads = side == 1
        flag = jnp.where(two_leads, listed_flag(two, apart), listed_flag(one, apart))
        if pair in ONLY:
            flag = jnp.where(flags[0] == ONLY[pair], flag, 0.0)
        tile = jnp.concatenate([tiles[at], pad], axis=0) * (flag * factor)
        table[one * LANES:(one + 1) * LANES, two * LANES:(two + 1) * LANES] = tile
        table[two * LANES:(two + 1) * LANES, one * LANES:(one + 1) * LANES] = tile.T
    row = lax.broadcasted_iota(jnp.int32, (LANES, LANES), 0)
    hot = jnp.concatenate(
        [
            ((info[block].astype(jnp.int32) == row) & (lane < examples)).astype(jnp.bfloat16)
            if block in info else jnp.zeros((LANES, LANES), jnp.bfloat16)
            for block in range(6)
        ],
        axis=1,
    )
    return dot_parts(table[...], hot)


def copies_of(loads, sems):
    return {
        key: pltpu.make_async_copy(source, target, sems.at[at])
        for at, (key, (source, target)) in enumerate(loads.items())
    }


def start(copies, *keys):
    for key in keys:
        copies[key].start()


def wait(copies, *keys):
    for key in keys:
        copies[key].wait()


def info_row(message, rows):
    return message[rows:rows + INFO, :LANES].astype(jnp.float32)[:1]


def columns(ref, at, width):
    return ref.at[:, pl.ds(pl.multiple_of(at, LANES), width)]


def first_kernel(factor, flags, own_info, acts, x_half, ys_one, zs_one, ys_two, zs_two, gram, out,
                 xs_v, xc_v, ys_v, zs_v, own_v, half_v, gram_v, inner, sums, table, sems):
    mirrored, half_at, in_half, work_at = flags[0], flags[1], flags[2], flags[5]
    quarter = xs_v.shape[1]
    eighth = quarter // 2
    rows = inner.shape[1]
    copies = copies_of({
        "xs": (columns(acts, work_at, quarter), xs_v),
        "ys": (ys_one, ys_v.at[:, :eighth]),
        "ys2": (ys_two, ys_v.at[:, eighth:]),
        "g0": (gram.at[0], gram_v.at[0]),
        "zs": (zs_one, zs_v.at[:, :eighth]),
        "zs2": (zs_two, zs_v.at[:, eighth:]),
        "g1": (gram.at[1], gram_v.at[1]),
        "xc": (columns(x_half, in_half, quarter), xc_v),
        "g2": (gram.at[2], gram_v.at[2]),
        "own": (columns(acts, half_at, 2 * quarter), own_v),
        "half": (x_half.at[:, :2 * quarter], half_v),
        "g3": (gram.at[3], gram_v.at[3]),
    }, sems)
    start(copies, "xs", "ys", "ys2", "g0")
    wait(copies, "xs", "ys", "ys2")
    start(copies, "zs", "zs2", "g1", "xc", "g2")
    product(ys_v, xs_v, inner.at[0])
    wait(copies, "g0", "zs", "zs2", "xc")
    product(ys_v, zs_v, inner.at[1])
    token_sums(inner.at[0], gram_v.at[0], sums.at[0])
    start(copies, "own", "half", "g3")
    wait(copies, "g1", "g2")
    product(ys_v, xc_v, inner.at[0])
    token_sums(inner.at[1], gram_v.at[1], sums.at[1])
    wait(copies, "own", "half")
    product(half_v, own_v, inner.at[1])
    token_sums(inner.at[0], gram_v.at[2], sums.at[2])
    wait(copies, "g3")
    token_sums(inner.at[1], gram_v.at[3], sums.at[3], ordered=False)
    info = {XS: own_info[...].astype(jnp.float32)[:1], XC: info_row(xc_v, rows),
            YS: info_row(ys_v, rows), ZS: info_row(zs_v, rows)}
    pairs = tuple(enumerate(FIRST))
    out[...] = domain_sums(pairs, factor, flags, info, sums, table)


def later_kernel(factor, part, flags, own_info, earlier, *refs):
    (acts, x_half, ys, yc, zs, zc, gram), refs = refs[:7], refs[7:]
    outs, (held, gram_v, inner, sums, table, sems) = refs[:-6], refs[-6:]
    mirrored, in_half, work_at = flags[0], flags[2], flags[5]
    rows, eighth = inner.shape[1], held.shape[2]
    copies = copies_of({
        XS: (columns(acts, work_at + part * eighth, eighth), held.at[XS, :rows, :]),
        XC: (columns(x_half, in_half + part * eighth, eighth), held.at[XC]),
        YS: (ys, held.at[YS]),
        YC: (yc, held.at[YC]),
        ZS: (zs, held.at[ZS]),
        ZC: (zc, held.at[ZC]),
        "g4": (gram.at[4], gram_v.at[0]),
        "g5": (gram.at[5], gram_v.at[1]),
        "g6": (gram.at[6], gram_v.at[2]),
        "g2": (gram.at[2], gram_v.at[3]),
    }, sems)
    start(copies, YC, XC, ZC, "g4", YS, ZS, "g5", XS, "g6", "g2")
    wait(copies, YC, XC)
    product(held.at[YC], held.at[XC], inner.at[0])
    wait(copies, ZC, "g4")
    product(held.at[YC], held.at[ZC], inner.at[1])
    token_sums(inner.at[0], gram_v.at[0], sums.at[0])
    wait(copies, YS, ZS, "g5")
    product(held.at[jnp.where(mirrored == 0, YC, YS)], held.at[jnp.where(mirrored == 0, ZS, ZC)], inner.at[0])
    token_sums(inner.at[1], gram_v.at[1], sums.at[1])
    wait(copies, XS, "g6", "g2")

    @pl.when(mirrored == 1)
    def _():
        product(held.at[YC], held.at[XS], inner.at[1])
        token_sums(inner.at[0], gram_v.at[2], sums.at[2])
        token_sums(inner.at[1], gram_v.at[3], sums.at[3])

    @pl.when(mirrored == 0)
    def _():
        token_sums(inner.at[0], gram_v.at[2], sums.at[2])
        sums[3] = jnp.zeros(sums.shape[1:], jnp.float32)

    info = {block: info_row(held.at[block], rows) for block in range(1, 6)}
    info[XS] = own_info[...].astype(jnp.float32)[:1]
    pairs = ((0, 4), (1, 5), (2, 6), (2, 7), (3, 8))
    total = domain_sums(pairs, factor, flags, info, sums, table)
    total = total + earlier[...]
    if len(outs) == 1:
        outs[0][...] = total
        return
    total = total.T
    examples = sums.shape[1]
    for block, out in enumerate(outs):
        out[...] = total[:DOMAINS, block * LANES:block * LANES + examples]


def per_device(acts, grads, domain, listed):
    rows, width = acts.shape
    examples = rows // TOK
    quarter = width // 4
    me = lax.axis_index("ex")
    core = me % 2
    side = (me // 2) % 2
    mirrored = core ^ side

    flags = jnp.stack([
        mirrored, core * 2 * quarter, (1 - side) * quarter, core, side,
        core * 2 * quarter + (1 - side) * quarter,
    ]).astype(jnp.int32)
    places = jnp.stack([core * 2 + side, core * 2 + (1 - side)]).astype(jnp.int32)
    cross_places = jnp.stack([(1 - core) * 2 + side, (1 - core) * 2 + (1 - side)]).astype(jnp.int32)
    half_place = jnp.stack([1 - core]).astype(jnp.int32)

    own_info = jnp.concatenate(
        [domain, listed[0], jnp.zeros((LANES - examples - 2,), jnp.int32)]
    )
    own_info = jnp.broadcast_to(own_info.astype(acts.dtype)[None, :], (INFO, LANES))

    grads_ys = send(grads, across, 0)
    grads_zs = send(grads, along, 0)
    cut_ys, zs_one, ys_two, zs_two = cut(acts, own_info, places)
    ys_one = send(cut_ys, across, 0)
    zs_one = send(zs_one, along, 0)
    ys_two = send(ys_two, across, 0)
    zs_two = send(zs_two, along, 0)
    own_info, _ = lax.optimization_barrier((own_info, cut_ys))
    yc_one, zc_one, yc_two, zc_two = cut(acts, own_info, cross_places)
    yc_one = send(yc_one, across, 1)
    zc_one = send(zc_one, along, 1)
    yc_two = send(yc_two, across, 1)
    zc_two = send(zc_two, along, 1)

    def exchange(*values):
        return tuple(send(value, stay, 1) for value in values)

    x_half, grads_yc, grads_zc = lax.cond(
        listed[0, 0] < 2, exchange, lambda *values: values,
        cut_half(acts, grads, own_info, half_place), grads_ys, grads_zs,
    )
    factor = 1.0 / (TOK * math.sqrt(width * grads.shape[1]))

    gram = grams(flags, grads, x_half, grads_ys, grads_yc, grads_zs, grads_zc)

    smem = pl.BlockSpec(memory_space=pltpu.SMEM)
    vmem = pl.BlockSpec(memory_space=pltpu.VMEM)
    hbm = pl.BlockSpec(memory_space=pl.ANY)
    params = pltpu.CompilerParams(vmem_limit_bytes=VMEM_BYTES)
    own_v = pltpu.VMEM((rows, quarter), acts.dtype)
    slice_v = pltpu.VMEM((rows + INFO, quarter), acts.dtype)
    shared = [
        pltpu.VMEM((4, rows, rows), jnp.float32),
        pltpu.VMEM((2, rows, rows), jnp.float32),
        pltpu.VMEM((4, examples, rows), jnp.float32),
        pltpu.VMEM((6 * LANES, 6 * LANES), jnp.float32),
    ]
    partial_sums = jax.ShapeDtypeStruct((6 * LANES, LANES), jnp.float32)
    first = pl.pallas_call(
        functools.partial(first_kernel, factor),
        in_specs=[smem, vmem] + [hbm] * 7,
        out_specs=vmem,
        out_shape=partial_sums,
        scratch_shapes=[own_v] + [slice_v] * 3 + [
            pltpu.VMEM((rows, 2 * quarter), acts.dtype),
            pltpu.VMEM((rows + INFO, 2 * quarter), acts.dtype),
        ] + shared + [pltpu.SemaphoreType.DMA((12,))],
        compiler_params=params,
        cost_estimate=SMALL,
        name="first",
    )(flags, own_info, acts, x_half, ys_one, zs_one, ys_two, zs_two, gram)

    def later(part, earlier, messages, out_shape):
        return pl.pallas_call(
            functools.partial(later_kernel, factor, part),
            in_specs=[smem] + [vmem] * 2 + [hbm] * 7,
            out_specs=[vmem] * len(out_shape),
            out_shape=out_shape,
            scratch_shapes=[
                pltpu.VMEM((6, rows + INFO, quarter // 2), acts.dtype)
            ] + shared + [pltpu.SemaphoreType.DMA((10,))],
            compiler_params=params,
            cost_estimate=SMALL,
            name="later",
        )(flags, own_info, earlier, acts, x_half, *messages, gram)

    second, = later(0, first, (ys_one, yc_one, zs_one, zc_one), [partial_sums])
    sums = later(
        1, second, (ys_two, yc_two, zs_two, zc_two),
        [jax.ShapeDtypeStruct((DOMAINS, examples), jnp.float32)] * 6,
    )

    total = sums[XS]
    total = total + send(sums[XC], stay, 1)
    total = total + send(sums[YS], across, 0)
    total = total + send(sums[YC], across, 1)
    total = total + send(sums[ZS], against, 0)
    total = total + send(sums[ZC], against, 1)
    return total.T


def solution(mesh):
    in_specs = (
        P(("groups", "ex"), None),
        P(("groups", "ex"), None),
        P(("groups", "ex")),
        P(("groups", "ex"), None),
    )
    out_specs = P(("groups", "ex"), None)
    return jax.shard_map(
        per_device, mesh=mesh, in_specs=in_specs, out_specs=out_specs, check_vma=False
    )
```

```python
import functools
import math

import jax
import jax.numpy as jnp
from jax import lax
from jax.experimental import pallas as pl
from jax.experimental.pallas import tpu as pltpu
from jax.sharding import PartitionSpec as P

TOK = 8
TOK_BITS = 3
DOMAINS = 48
LANES = 128
VMEM_BYTES = 63 * 1024 * 1024

INFO = 16

XS, XC, YS, YC, ZS, ZC = range(6)
PAIRS = (
    (YS, XS, 1), (YS, ZS, 1), (YS, XC, 0), (XC, XS, 0),
    (YC, XC, 1), (YC, ZC, 1), (YC, ZS, 0), (YS, ZC, 0), (YC, XS, 0),
)
ONLY = {2: 0, 6: 0, 7: 1, 8: 1}
SLOT = (0, 1, 2, 3, 4, 5, 6, 6, 2)
FIRST = (0, 1, 2, 3)
SMALL = pl.CostEstimate(flops=1, bytes_accessed=1, transcendentals=0)
NT = (((1,), (1,)), ((), ()))
NN = (((1,), (0,)), ((), ()))


def across(chip):
    return chip ^ 1


def along(chip):
    return chip + 2 if chip & 1 else chip - 2


def against(chip):
    return chip - 2 if chip & 1 else chip + 2


def stay(chip):
    return chip


def send(value, move, flip):
    chips = lax.axis_size("ex") // 2
    pairs = [
        (2 * chip + core, 2 * (move(chip) % chips) + (core ^ flip))
        for chip in range(chips)
        for core in range(2)
    ]
    return lax.ppermute(value, "ex", pairs)


def token_major(rows):
    to = lax.broadcasted_iota(jnp.int32, (rows, rows), 0)
    source = lax.broadcasted_iota(jnp.int32, (rows, rows), 1)
    examples = rows // TOK
    place = (source & (TOK - 1)) * examples + lax.shift_right_logical(source, TOK_BITS)
    return (place == to).astype(jnp.bfloat16)


def reorder(order, block):
    return jnp.dot(order, block, preferred_element_type=jnp.float32).astype(jnp.bfloat16)


def put(target, value, info):
    rows = value.shape[0]
    target[:rows, :] = value
    target[rows:, :] = jnp.concatenate([info[...]] * (target.shape[1] // LANES), axis=1)


def cut_kernel(places, info, y_acts, z_acts, y_one, z_one, y_two, z_two, order):
    order[...] = token_major(order.shape[0])
    for step, (y_out, z_out) in enumerate(((y_one, z_one), (y_two, z_two))):
        @pl.when(pl.program_id(0) == step)
        def _():
            put(y_out, reorder(order[...], y_acts[...]), info)
            put(z_out, z_acts[...], info)


def cut(acts, info, places):
    rows, width = acts.shape
    eighth = width // 8
    block = (rows, eighth)
    return pl.pallas_call(
        cut_kernel,
        grid_spec=pltpu.PrefetchScalarGridSpec(
            num_scalar_prefetch=1,
            grid=(2,),
            in_specs=[
                pl.BlockSpec((INFO, LANES), lambda i, p: (0, 0)),
                pl.BlockSpec(block, lambda i, p: (0, 2 * p[0] + i)),
                pl.BlockSpec(block, lambda i, p: (0, 2 * p[1] + i)),
            ],
            out_specs=[pl.BlockSpec((rows + INFO, eighth), lambda i, p: (0, 0))] * 4,
            scratch_shapes=[pltpu.VMEM((rows, rows), jnp.bfloat16)],
        ),
        out_shape=[jax.ShapeDtypeStruct((rows + INFO, eighth), acts.dtype)] * 4,
        compiler_params=pltpu.CompilerParams(vmem_limit_bytes=VMEM_BYTES),
        cost_estimate=SMALL,
        name="cut",
    )(places, info, acts, acts)


def half_kernel(steps, place, info, acts, grads, out):
    @pl.when(pl.program_id(0) < steps)
    def _():
        put(out, acts[...], info)

    @pl.when(pl.program_id(0) >= steps)
    def _():
        put(out, grads[...], info)


def cut_half(acts, grads, info, place):
    rows, width = acts.shape
    half, depth = width // 2, grads.shape[1]
    step = math.gcd(math.gcd(half, depth), 512)
    steps = half // step
    return pl.pallas_call(
        functools.partial(half_kernel, steps),
        grid_spec=pltpu.PrefetchScalarGridSpec(
            num_scalar_prefetch=1,
            grid=(steps + depth // step,),
            in_specs=[
                pl.BlockSpec((INFO, LANES), lambda i, p: (0, 0)),
                pl.BlockSpec((rows, step), lambda i, p: (0, p[0] * steps + jnp.minimum(i, steps - 1))),
                pl.BlockSpec((rows, step), lambda i, p: (0, jnp.maximum(i - steps, 0))),
            ],
            out_specs=pl.BlockSpec((rows + INFO, step), lambda i, p: (0, i)),
        ),
        out_shape=jax.ShapeDtypeStruct((rows + INFO, half + depth), acts.dtype),
        compiler_params=pltpu.CompilerParams(vmem_limit_bytes=VMEM_BYTES),
        cost_estimate=SMALL,
        name="half",
    )(place, info, acts, grads)


def guarded(pair, mirrored, work):
    if pair in ONLY:
        pl.when(mirrored == ONLY[pair])(work)
    else:
        work()


def grams_kernel(flags, xs, xc, ys, yc, zs, zc, out, held, result, in_sems, out_sems):
    mirrored = flags[0]
    rows, depth = xs.shape
    order = token_major(rows)
    sources = (xs, xc.at[:rows, xc.shape[1] - depth:], ys, yc, zs, zc)
    loads = [
        pltpu.make_async_copy(source, held.at[at], in_sems.at[at])
        for at, source in enumerate(sources)
    ]
    for block in (YS, XS, ZS, XC, YC, ZC):
        loads[block].start()
    here = set()

    def ready(*blocks):
        for block in blocks:
            if block not in here:
                here.add(block)
                loads[block].wait()
                if block in (YS, YC):
                    held[block] = reorder(order, held[block])

    for pair, (one, two, _) in enumerate(PAIRS):
        ready(one, two)
        slot = SLOT[pair]

        def work(one=one, two=two, slot=slot):
            result[slot] = lax.dot_general(
                held[one], held[two], NT, preferred_element_type=jnp.float32
            )
            pltpu.make_async_copy(result.at[slot], out.at[slot], out_sems.at[slot]).start()

        guarded(pair, mirrored, work)
    for slot in range(7):
        pltpu.make_async_copy(result.at[slot], out.at[slot], out_sems.at[slot]).wait()


def grams(flags, grads, *messages):
    rows, width = grads.shape
    return pl.pallas_call(
        grams_kernel,
        in_specs=[pl.BlockSpec(memory_space=pltpu.SMEM)] + [pl.BlockSpec(memory_space=pl.ANY)] * 6,
        out_specs=pl.BlockSpec(memory_space=pl.ANY),
        out_shape=jax.ShapeDtypeStruct((7, rows, rows), jnp.float32),
        scratch_shapes=[
            pltpu.VMEM((6, rows, width), grads.dtype),
            pltpu.VMEM((7, rows, rows), jnp.float32),
            pltpu.SemaphoreType.DMA((6,)),
            pltpu.SemaphoreType.DMA((7,)),
        ],
        compiler_params=pltpu.CompilerParams(vmem_limit_bytes=VMEM_BYTES),
        cost_estimate=SMALL,
        name="grams",
    )(flags, grads, *messages)


def product(one, two, inner):
    rows = inner.shape[0]
    inner[...] = lax.dot_general(
        one[:rows, :], two[:rows, :], NT, preferred_element_type=jnp.float32
    )


def token_sums(inner, gram, sums, ordered=True):
    examples, rows = sums.shape
    if ordered:
        sums[...] = sum(
            inner[at:at + examples, :] * gram[at:at + examples, :]
            for at in range(0, rows, examples)
        )
    else:
        weighted = inner[...] * gram[...]
        sums[...] = weighted.reshape(examples, TOK, rows).sum(axis=1)


def two_parts(value):
    high = value.astype(jnp.bfloat16)
    return high, (value - high.astype(jnp.float32)).astype(jnp.bfloat16)


def dot_parts(value, table):
    high, low = two_parts(value)
    return lax.dot_general(low, table, NT, preferred_element_type=jnp.float32) + lax.dot_general(
        high, table, NT, preferred_element_type=jnp.float32
    )


def domain_sums(pairs, factor, flags, info, sums):
    count, examples, rows = sums.shape
    example = lax.broadcasted_iota(jnp.int32, (LANES, rows), 0)
    column = lax.broadcasted_iota(jnp.int32, (LANES, rows), 1)
    gather = (lax.shift_right_logical(column, TOK_BITS) == example).astype(jnp.bfloat16)
    tiles = dot_parts(sums[...].reshape(count * examples, rows), gather)
    tiles = tiles.reshape(count, examples, LANES)
    core, side = flags[3], flags[4]
    lane = lax.broadcasted_iota(jnp.int32, (1, LANES), 1)
    row = lax.broadcasted_iota(jnp.int32, (DOMAINS, LANES), 0)
    hot = {
        block: ((value.astype(jnp.int32) == row) & (lane < examples)).astype(jnp.bfloat16)
        for block, value in info.items()
    }

    def listed_flag(block, apart):
        return jnp.sum(jnp.where(lane == examples + apart, info[block], 0.0), axis=1, keepdims=True)

    pad = jnp.zeros((LANES - examples, LANES), jnp.float32)
    total = {}
    for at, pair in pairs:
        one, two, apart = PAIRS[pair]
        if one == XC:
            two_leads = core == 0
        elif two in (XS, XC):
            two_leads = side == 0
        else:
            two_leads = side == 1
        flag = jnp.where(two_leads, listed_flag(two, apart), listed_flag(one, apart))
        if pair in ONLY:
            flag = jnp.where(flags[0] == ONLY[pair], flag, 0.0)
        tile = jnp.concatenate([tiles[at], pad], axis=0) * (flag * factor)
        high, low = two_parts(tile)
        for block, table, dims in ((one, hot[two], NT), (two, hot[one], NN)):
            for part in (low, high):
                term = lax.dot_general(table, part, dims, preferred_element_type=jnp.float32)
                total[block] = total[block] + term if block in total else term
    return total


def copies_of(loads, sems):
    return {
        key: pltpu.make_async_copy(source, target, sems.at[at])
        for at, (key, (source, target)) in enumerate(loads.items())
    }


def start(copies, *keys):
    for key in keys:
        copies[key].start()


def wait(copies, *keys):
    for key in keys:
        copies[key].wait()


def info_row(message, rows):
    return message[rows:rows + INFO, :LANES].astype(jnp.float32)[:1]


def columns(ref, at, width):
    return ref.at[:, pl.ds(pl.multiple_of(at, LANES), width)]


def first_kernel(factor, flags, own_info, acts, x_half, ys_one, zs_one, ys_two, zs_two, gram, out,
                 xs_v, xc_v, ys_v, zs_v, own_v, half_v, gram_v, inner, sums, sems):
    half_at, in_half, work_at = flags[1], flags[2], flags[5]
    quarter = xs_v.shape[1]
    eighth = quarter // 2
    rows = inner.shape[1]
    copies = copies_of({
        "xs": (columns(acts, work_at, quarter), xs_v),
        "ys": (ys_one, ys_v.at[:, :eighth]),
        "ys2": (ys_two, ys_v.at[:, eighth:]),
        "g0": (gram.at[0], gram_v.at[0]),
        "zs": (zs_one, zs_v.at[:, :eighth]),
        "zs2": (zs_two, zs_v.at[:, eighth:]),
        "g1": (gram.at[1], gram_v.at[1]),
        "xc": (columns(x_half, in_half, quarter), xc_v),
        "g2": (gram.at[2], gram_v.at[2]),
        "own": (columns(acts, half_at, 2 * quarter), own_v),
        "half": (x_half.at[:, :2 * quarter], half_v),
        "g3": (gram.at[3], gram_v.at[3]),
    }, sems)
    start(copies, "xs", "ys", "ys2", "g0")
    wait(copies, "xs", "ys", "ys2")
    start(copies, "zs", "zs2", "g1", "xc", "g2")
    product(ys_v, xs_v, inner.at[0])
    wait(copies, "g0", "zs", "zs2", "xc")
    product(ys_v, zs_v, inner.at[1])
    token_sums(inner.at[0], gram_v.at[0], sums.at[0])
    start(copies, "own", "half", "g3")
    wait(copies, "g1", "g2")
    product(ys_v, xc_v, inner.at[0])
    token_sums(inner.at[1], gram_v.at[1], sums.at[1])
    wait(copies, "own", "half")
    product(half_v, own_v, inner.at[1])
    token_sums(inner.at[0], gram_v.at[2], sums.at[2])
    wait(copies, "g3")
    token_sums(inner.at[1], gram_v.at[3], sums.at[3], ordered=False)
    info = {XS: own_info[...].astype(jnp.float32)[:1], XC: info_row(xc_v, rows),
            YS: info_row(ys_v, rows), ZS: info_row(zs_v, rows)}
    total = domain_sums(tuple(enumerate(FIRST)), factor, flags, info, sums)
    out[...] = jnp.zeros_like(out)
    for block, value in total.items():
        out[block] = value


def later_kernel(factor, part, flags, own_info, earlier, *refs):
    (acts, x_half, ys, yc, zs, zc, gram), refs = refs[:7], refs[7:]
    outs, (held, gram_v, inner, sums, sems) = refs[:-5], refs[-5:]
    mirrored, in_half, work_at = flags[0], flags[2], flags[5]
    rows, eighth = inner.shape[1], held.shape[2]
    copies = copies_of({
        XS: (columns(acts, work_at + part * eighth, eighth), held.at[XS, :rows, :]),
        XC: (columns(x_half, in_half + part * eighth, eighth), held.at[XC]),
        YS: (ys, held.at[YS]),
        YC: (yc, held.at[YC]),
        ZS: (zs, held.at[ZS]),
        ZC: (zc, held.at[ZC]),
        "g4": (gram.at[4], gram_v.at[0]),
        "g5": (gram.at[5], gram_v.at[1]),
        "g6": (gram.at[6], gram_v.at[2]),
        "g2": (gram.at[2], gram_v.at[3]),
    }, sems)
    start(copies, YC, XC, ZC, "g4", YS, ZS, "g5", XS, "g6", "g2")
    wait(copies, YC, XC)
    product(held.at[YC], held.at[XC], inner.at[0])
    wait(copies, ZC, "g4")
    product(held.at[YC], held.at[ZC], inner.at[1])
    token_sums(inner.at[0], gram_v.at[0], sums.at[0])
    wait(copies, YS, ZS, "g5")
    product(held.at[jnp.where(mirrored == 0, YC, YS)], held.at[jnp.where(mirrored == 0, ZS, ZC)], inner.at[0])
    token_sums(inner.at[1], gram_v.at[1], sums.at[1])
    wait(copies, XS, "g6", "g2")

    @pl.when(mirrored == 1)
    def _():
        product(held.at[YC], held.at[XS], inner.at[1])
        token_sums(inner.at[0], gram_v.at[2], sums.at[2])
        token_sums(inner.at[1], gram_v.at[3], sums.at[3])

    @pl.when(mirrored == 0)
    def _():
        token_sums(inner.at[0], gram_v.at[2], sums.at[2])
        sums[3] = jnp.zeros(sums.shape[1:], jnp.float32)

    info = {block: info_row(held.at[block], rows) for block in range(1, 6)}
    info[XS] = own_info[...].astype(jnp.float32)[:1]
    pairs = ((0, 4), (1, 5), (2, 6), (2, 7), (3, 8))
    total = domain_sums(pairs, factor, flags, info, sums)
    examples = sums.shape[1]
    for block, value in total.items():
        value = value + earlier[block]
        if len(outs) == 1:
            outs[0][block] = value
        else:
            outs[block][...] = value[:, :examples]


def per_device(acts, grads, domain, listed):
    rows, width = acts.shape
    examples = rows // TOK
    quarter = width // 4
    me = lax.axis_index("ex")
    core = me % 2
    side = (me // 2) % 2
    mirrored = core ^ side

    flags = jnp.stack([
        mirrored, core * 2 * quarter, (1 - side) * quarter, core, side,
        core * 2 * quarter + (1 - side) * quarter,
    ]).astype(jnp.int32)
    places = jnp.stack([core * 2 + side, core * 2 + (1 - side)]).astype(jnp.int32)
    cross_places = jnp.stack([(1 - core) * 2 + side, (1 - core) * 2 + (1 - side)]).astype(jnp.int32)
    half_place = jnp.stack([1 - core]).astype(jnp.int32)

    own_info = jnp.concatenate(
        [domain, listed[0], jnp.zeros((LANES - examples - 2,), jnp.int32)]
    )
    own_info = jnp.broadcast_to(own_info.astype(acts.dtype)[None, :], (INFO, LANES))

    grads_ys = send(grads, across, 0)
    grads_zs = send(grads, along, 0)
    cut_ys, zs_one, ys_two, zs_two = cut(acts, own_info, places)
    ys_one = send(cut_ys, across, 0)
    zs_one = send(zs_one, along, 0)
    ys_two = send(ys_two, across, 0)
    zs_two = send(zs_two, along, 0)
    own_info, _ = lax.optimization_barrier((own_info, cut_ys))
    yc_one, zc_one, yc_two, zc_two = cut(acts, own_info, cross_places)
    yc_one = send(yc_one, across, 1)
    zc_one = send(zc_one, along, 1)
    yc_two = send(yc_two, across, 1)

    def exchange(*values):
        return tuple(send(value, stay, 1) for value in values)

    x_half, grads_yc, grads_zc = lax.cond(
        listed[0, 0] < 2, exchange, lambda *values: values,
        cut_half(acts, grads, own_info, half_place), grads_ys, grads_zs,
    )
    factor = 1.0 / (TOK * math.sqrt(width * grads.shape[1]))

    gram = grams(flags, grads, x_half, grads_ys, grads_yc, grads_zs, grads_zc)
    zc_two, gram = lax.optimization_barrier((zc_two, gram))
    zc_two = send(zc_two, along, 1)

    smem = pl.BlockSpec(memory_space=pltpu.SMEM)
    vmem = pl.BlockSpec(memory_space=pltpu.VMEM)
    hbm = pl.BlockSpec(memory_space=pl.ANY)
    params = pltpu.CompilerParams(vmem_limit_bytes=VMEM_BYTES)
    own_v = pltpu.VMEM((rows, quarter), acts.dtype)
    slice_v = pltpu.VMEM((rows + INFO, quarter), acts.dtype)
    shared = [
        pltpu.VMEM((4, rows, rows), jnp.float32),
        pltpu.VMEM((2, rows, rows), jnp.float32),
        pltpu.VMEM((4, examples, rows), jnp.float32),
    ]
    partial_sums = jax.ShapeDtypeStruct((6, DOMAINS, LANES), jnp.float32)
    first = pl.pallas_call(
        functools.partial(first_kernel, factor),
        in_specs=[smem, vmem] + [hbm] * 7,
        out_specs=vmem,
        out_shape=partial_sums,
        scratch_shapes=[own_v] + [slice_v] * 3 + [
            pltpu.VMEM((rows, 2 * quarter), acts.dtype),
            pltpu.VMEM((rows + INFO, 2 * quarter), acts.dtype),
        ] + shared + [pltpu.SemaphoreType.DMA((12,))],
        compiler_params=params,
        cost_estimate=SMALL,
        name="first",
    )(flags, own_info, acts, x_half, ys_one, zs_one, ys_two, zs_two, gram)

    def later(part, earlier, messages, out_shape):
        return pl.pallas_call(
            functools.partial(later_kernel, factor, part),
            in_specs=[smem] + [vmem] * 2 + [hbm] * 7,
            out_specs=[vmem] * len(out_shape),
            out_shape=out_shape,
            scratch_shapes=[
                pltpu.VMEM((6, rows + INFO, quarter // 2), acts.dtype)
            ] + shared + [pltpu.SemaphoreType.DMA((10,))],
            compiler_params=pltpu.CompilerParams(vmem_limit_bytes=VMEM_BYTES),
            cost_estimate=SMALL,
            name="later",
        )(flags, own_info, earlier, acts, x_half, *messages, gram)

    second, = later(0, first, (ys_one, yc_one, zs_one, zc_one), [partial_sums])
    sums = later(
        1, second, (ys_two, yc_two, zs_two, zc_two),
        [jax.ShapeDtypeStruct((DOMAINS, examples), jnp.float32)] * 6,
    )

    total = sums[XS]
    total = total + send(sums[XC], stay, 1)
    total = total + send(sums[YS], across, 0)
    total = total + send(sums[YC], across, 1)
    total = total + send(sums[ZS], against, 0)
    total = total + send(sums[ZC], against, 1)
    return total.T


def solution(mesh):
    in_specs = (
        P(("groups", "ex"), None),
        P(("groups", "ex"), None),
        P(("groups", "ex")),
        P(("groups", "ex"), None),
    )
    out_specs = P(("groups", "ex"), None)
    return jax.shard_map(
        per_device, mesh=mesh, in_specs=in_specs, out_specs=out_specs, check_vma=False
    )
```

```python
import functools
import math

import jax
import jax.numpy as jnp
from jax import lax
from jax.experimental import pallas as pl
from jax.experimental.pallas import tpu as pltpu
from jax.sharding import PartitionSpec as P

TOK = 8
TOK_BITS = 3
DOMAINS = 48
LANES = 128
VMEM_BYTES = 63 * 1024 * 1024

INFO = 16

XS, XC, YS, YC, ZS, ZC = range(6)
PAIRS = (
    (YS, XS, 1), (YS, ZS, 1), (YS, XC, 0), (XC, XS, 0),
    (YC, XC, 1), (YC, ZC, 1), (YC, ZS, 0), (YS, ZC, 0), (YC, XS, 0),
)
ONLY = {2: 0, 6: 0, 7: 1, 8: 1}
SLOT = (0, 1, 2, 3, 4, 5, 6, 6, 2)
FIRST = (0, 1, 2, 3)
SMALL = pl.CostEstimate(flops=1, bytes_accessed=1, transcendentals=0)
NT = (((1,), (1,)), ((), ()))
NN = (((1,), (0,)), ((), ()))


def across(chip):
    return chip ^ 1


def along(chip):
    return chip + 2 if chip & 1 else chip - 2


def against(chip):
    return chip - 2 if chip & 1 else chip + 2


def stay(chip):
    return chip


def send(value, move, flip):
    chips = lax.axis_size("ex") // 2
    pairs = [
        (2 * chip + core, 2 * (move(chip) % chips) + (core ^ flip))
        for chip in range(chips)
        for core in range(2)
    ]
    return lax.ppermute(value, "ex", pairs)


def token_major(rows):
    to = lax.broadcasted_iota(jnp.int32, (rows, rows), 0)
    source = lax.broadcasted_iota(jnp.int32, (rows, rows), 1)
    examples = rows // TOK
    place = (source & (TOK - 1)) * examples + lax.shift_right_logical(source, TOK_BITS)
    return (place == to).astype(jnp.bfloat16)


def reorder(order, block):
    return jnp.dot(order, block, preferred_element_type=jnp.float32).astype(jnp.bfloat16)


def put(target, value, info):
    rows = value.shape[0]
    target[:rows, :] = value
    target[rows:, :] = jnp.concatenate([info[...]] * (target.shape[1] // LANES), axis=1)


def chunks(quarter):
    second = quarter // LANES // 2 * LANES
    return quarter - second, second


def cut_kernel(places, info, y_acts, z_acts, y_one, z_one, y_two, z_two, order):
    rows, split = order.shape[0], y_one.shape[1]
    order[...] = token_major(rows)
    put(y_one, reorder(order[...], y_acts[:, :split]), info)
    put(z_one, z_acts[:, :split], info)
    put(y_two, reorder(order[...], y_acts[:, split:]), info)
    put(z_two, z_acts[:, split:], info)


def cut(acts, info, places):
    rows, width = acts.shape
    quarter = width // 4
    one, two = chunks(quarter)
    shapes = [(rows + INFO, one)] * 2 + [(rows + INFO, two)] * 2
    return pl.pallas_call(
        cut_kernel,
        grid_spec=pltpu.PrefetchScalarGridSpec(
            num_scalar_prefetch=1,
            grid=(1,),
            in_specs=[
                pl.BlockSpec((INFO, LANES), lambda i, p: (0, 0)),
                pl.BlockSpec((rows, quarter), lambda i, p: (0, p[0])),
                pl.BlockSpec((rows, quarter), lambda i, p: (0, p[1])),
            ],
            out_specs=[pl.BlockSpec(shape, lambda i, p: (0, 0)) for shape in shapes],
            scratch_shapes=[pltpu.VMEM((rows, rows), jnp.bfloat16)],
        ),
        out_shape=[jax.ShapeDtypeStruct(shape, acts.dtype) for shape in shapes],
        compiler_params=pltpu.CompilerParams(vmem_limit_bytes=VMEM_BYTES),
        cost_estimate=SMALL,
        name="cut",
    )(places, info, acts, acts)


def half_kernel(steps, place, info, acts, grads, out):
    @pl.when(pl.program_id(0) < steps)
    def _():
        put(out, acts[...], info)

    @pl.when(pl.program_id(0) >= steps)
    def _():
        put(out, grads[...], info)


def cut_half(acts, grads, info, place):
    rows, width = acts.shape
    half, depth = width // 2, grads.shape[1]
    step = math.gcd(math.gcd(half, depth), 512)
    steps = half // step
    return pl.pallas_call(
        functools.partial(half_kernel, steps),
        grid_spec=pltpu.PrefetchScalarGridSpec(
            num_scalar_prefetch=1,
            grid=(steps + depth // step,),
            in_specs=[
                pl.BlockSpec((INFO, LANES), lambda i, p: (0, 0)),
                pl.BlockSpec((rows, step), lambda i, p: (0, p[0] * steps + jnp.minimum(i, steps - 1))),
                pl.BlockSpec((rows, step), lambda i, p: (0, jnp.maximum(i - steps, 0))),
            ],
            out_specs=pl.BlockSpec((rows + INFO, step), lambda i, p: (0, i)),
        ),
        out_shape=jax.ShapeDtypeStruct((rows + INFO, half + depth), acts.dtype),
        compiler_params=pltpu.CompilerParams(vmem_limit_bytes=VMEM_BYTES),
        cost_estimate=SMALL,
        name="half",
    )(place, info, acts, grads)


def guarded(pair, mirrored, work):
    if pair in ONLY:
        pl.when(mirrored == ONLY[pair])(work)
    else:
        work()


def grams_kernel(flags, xs, xc, ys, yc, zs, zc, out, held, result, in_sems, out_sems):
    mirrored = flags[0]
    rows, depth = xs.shape
    order = token_major(rows)
    sources = (xs, xc.at[:rows, xc.shape[1] - depth:], ys, yc, zs, zc)
    loads = [
        pltpu.make_async_copy(source, held.at[at], in_sems.at[at])
        for at, source in enumerate(sources)
    ]
    for block in (YS, XS, ZS, XC, YC, ZC):
        loads[block].start()
    here = set()

    def ready(*blocks):
        for block in blocks:
            if block not in here:
                here.add(block)
                loads[block].wait()
                if block in (YS, YC):
                    held[block] = reorder(order, held[block])

    for pair, (one, two, _) in enumerate(PAIRS):
        ready(one, two)
        slot = SLOT[pair]

        def work(one=one, two=two, slot=slot):
            result[slot] = lax.dot_general(
                held[one], held[two], NT, preferred_element_type=jnp.float32
            )
            pltpu.make_async_copy(result.at[slot], out.at[slot], out_sems.at[slot]).start()

        guarded(pair, mirrored, work)
    for slot in range(7):
        pltpu.make_async_copy(result.at[slot], out.at[slot], out_sems.at[slot]).wait()


def grams(flags, grads, *messages):
    rows, width = grads.shape
    return pl.pallas_call(
        grams_kernel,
        in_specs=[pl.BlockSpec(memory_space=pltpu.SMEM)] + [pl.BlockSpec(memory_space=pl.ANY)] * 6,
        out_specs=pl.BlockSpec(memory_space=pl.ANY),
        out_shape=jax.ShapeDtypeStruct((7, rows, rows), jnp.float32),
        scratch_shapes=[
            pltpu.VMEM((6, rows, width), grads.dtype),
            pltpu.VMEM((7, rows, rows), jnp.float32),
            pltpu.SemaphoreType.DMA((6,)),
            pltpu.SemaphoreType.DMA((7,)),
        ],
        compiler_params=pltpu.CompilerParams(vmem_limit_bytes=VMEM_BYTES),
        cost_estimate=SMALL,
        name="grams",
    )(flags, grads, *messages)


def product(one, two, inner):
    rows = inner.shape[0]
    inner[...] = lax.dot_general(
        one[:rows, :], two[:rows, :], NT, preferred_element_type=jnp.float32
    )


def token_sums(inner, gram, sums, ordered=True):
    examples, rows = sums.shape
    if ordered:
        sums[...] = sum(
            inner[at:at + examples, :] * gram[at:at + examples, :]
            for at in range(0, rows, examples)
        )
    else:
        weighted = inner[...] * gram[...]
        sums[...] = weighted.reshape(examples, TOK, rows).sum(axis=1)


def two_parts(value):
    high = value.astype(jnp.bfloat16)
    return high, (value - high.astype(jnp.float32)).astype(jnp.bfloat16)


def dot_parts(value, table):
    high, low = two_parts(value)
    return lax.dot_general(low, table, NT, preferred_element_type=jnp.float32) + lax.dot_general(
        high, table, NT, preferred_element_type=jnp.float32
    )


def domain_sums(pairs, factor, flags, info, sums):
    count, examples, rows = sums.shape
    example = lax.broadcasted_iota(jnp.int32, (LANES, rows), 0)
    column = lax.broadcasted_iota(jnp.int32, (LANES, rows), 1)
    gather = (lax.shift_right_logical(column, TOK_BITS) == example).astype(jnp.bfloat16)
    tiles = dot_parts(sums[...].reshape(count * examples, rows), gather)
    tiles = tiles.reshape(count, examples, LANES)
    core, side = flags[3], flags[4]
    lane = lax.broadcasted_iota(jnp.int32, (1, LANES), 1)
    row = lax.broadcasted_iota(jnp.int32, (DOMAINS, LANES), 0)
    hot = {
        block: ((value.astype(jnp.int32) == row) & (lane < examples)).astype(jnp.bfloat16)
        for block, value in info.items()
    }

    def listed_flag(block, apart):
        return jnp.sum(jnp.where(lane == examples + apart, info[block], 0.0), axis=1, keepdims=True)

    pad = jnp.zeros((LANES - examples, LANES), jnp.float32)
    total = {}
    for at, pair in pairs:
        one, two, apart = PAIRS[pair]
        if one == XC:
            two_leads = core == 0
        elif two in (XS, XC):
            two_leads = side == 0
        else:
            two_leads = side == 1
        flag = jnp.where(two_leads, listed_flag(two, apart), listed_flag(one, apart))
        if pair in ONLY:
            flag = jnp.where(flags[0] == ONLY[pair], flag, 0.0)
        tile = jnp.concatenate([tiles[at], pad], axis=0) * (flag * factor)
        high, low = two_parts(tile)
        for block, table, dims in ((one, hot[two], NT), (two, hot[one], NN)):
            for part in (low, high):
                term = lax.dot_general(table, part, dims, preferred_element_type=jnp.float32)
                total[block] = total[block] + term if block in total else term
    return total


def copies_of(loads, sems):
    return {
        key: pltpu.make_async_copy(source, target, sems.at[at])
        for at, (key, (source, target)) in enumerate(loads.items())
    }


def start(copies, *keys):
    for key in keys:
        copies[key].start()


def wait(copies, *keys):
    for key in keys:
        copies[key].wait()


def info_row(notes, block):
    return notes[block].astype(jnp.float32)[:1]


def columns(ref, at, width):
    return ref.at[:, pl.ds(pl.multiple_of(at, LANES), width)]


def first_kernel(factor, flags, own_info, acts, x_half, ys_one, zs_one, ys_two, zs_two, gram, out, notes,
                 xs_v, xc_v, ys_v, zs_v, own_v, half_v, gram_v, inner, sums, sems):
    half_at, in_half, work_at = flags[1], flags[2], flags[5]
    quarter = xs_v.shape[1]
    split = ys_one.shape[1]
    rows = inner.shape[1]
    copies = copies_of({
        "xs": (columns(acts, work_at, quarter), xs_v),
        "ys": (ys_one, ys_v.at[:, :split]),
        "ys2": (ys_two, ys_v.at[:, split:]),
        "g0": (gram.at[0], gram_v.at[0]),
        "zs": (zs_one, zs_v.at[:, :split]),
        "zs2": (zs_two, zs_v.at[:, split:]),
        "g1": (gram.at[1], gram_v.at[1]),
        "xc": (columns(x_half, in_half, quarter), xc_v),
        "g2": (gram.at[2], gram_v.at[2]),
        "own": (columns(acts, half_at, 2 * quarter), own_v),
        "half": (x_half.at[:, :2 * quarter], half_v),
        "g3": (gram.at[3], gram_v.at[3]),
    }, sems)
    start(copies, "xs", "ys", "ys2", "g0")
    wait(copies, "xs", "ys", "ys2")
    start(copies, "zs", "zs2", "g1", "xc", "g2")
    product(ys_v, xs_v, inner.at[0])
    wait(copies, "g0", "zs", "zs2", "xc")
    product(ys_v, zs_v, inner.at[1])
    token_sums(inner.at[0], gram_v.at[0], sums.at[0])
    start(copies, "own", "half", "g3")
    wait(copies, "g1", "g2")
    product(ys_v, xc_v, inner.at[0])
    token_sums(inner.at[1], gram_v.at[1], sums.at[1])
    wait(copies, "own", "half")
    product(half_v, own_v, inner.at[1])
    token_sums(inner.at[0], gram_v.at[2], sums.at[2])
    wait(copies, "g3")
    token_sums(inner.at[1], gram_v.at[3], sums.at[3], ordered=False)
    notes[...] = jnp.zeros_like(notes)
    notes[XS] = own_info[...]
    notes[XC] = xc_v[rows:, :LANES]
    notes[YS] = ys_v[rows:, split:split + LANES]
    notes[ZS] = zs_v[rows:, split:split + LANES]
    info = {block: info_row(notes, block) for block in (XS, XC, YS, ZS)}
    total = domain_sums(tuple(enumerate(FIRST)), factor, flags, info, sums)
    out[...] = jnp.zeros_like(out)
    for block, value in total.items():
        out[block] = value


def later_kernel(factor, at, flags, notes, earlier, *refs):
    (acts, x_half, ys, yc, zs, zc, gram), refs = refs[:7], refs[7:]
    outs, (held, gram_v, inner, sums, sems) = refs[:-5], refs[-5:]
    mirrored, in_half, work_at = flags[0], flags[2], flags[5]
    rows, width = inner.shape[1], held.shape[2]
    copies = copies_of({
        XS: (columns(acts, work_at + at, width), held.at[XS, :rows, :]),
        XC: (columns(x_half, in_half + at, width), held.at[XC]),
        YS: (ys, held.at[YS, :ys.shape[0], :]),
        YC: (yc, held.at[YC, :yc.shape[0], :]),
        ZS: (zs, held.at[ZS, :zs.shape[0], :]),
        ZC: (zc, held.at[ZC, :zc.shape[0], :]),
        "g4": (gram.at[4], gram_v.at[0]),
        "g5": (gram.at[5], gram_v.at[1]),
        "g6": (gram.at[6], gram_v.at[2]),
        "g2": (gram.at[2], gram_v.at[3]),
    }, sems)
    start(copies, YC, XC, ZC)
    wait(copies, YC, XC)
    start(copies, "g4", YS, ZS)
    product(held.at[YC], held.at[XC], inner.at[0])
    wait(copies, ZC)
    start(copies, "g5", XS)
    product(held.at[YC], held.at[ZC], inner.at[1])
    wait(copies, "g4", YS, ZS)
    start(copies, "g6", "g2")
    token_sums(inner.at[0], gram_v.at[0], sums.at[0])
    product(held.at[jnp.where(mirrored == 0, YC, YS)], held.at[jnp.where(mirrored == 0, ZS, ZC)], inner.at[0])
    wait(copies, "g5", XS)
    token_sums(inner.at[1], gram_v.at[1], sums.at[1])
    wait(copies, "g6", "g2")

    @pl.when(mirrored == 1)
    def _():
        product(held.at[YC], held.at[XS], inner.at[1])
        token_sums(inner.at[0], gram_v.at[2], sums.at[2])
        token_sums(inner.at[1], gram_v.at[3], sums.at[3])

    @pl.when(mirrored == 0)
    def _():
        token_sums(inner.at[0], gram_v.at[2], sums.at[2])
        sums[3] = jnp.zeros(sums.shape[1:], jnp.float32)

    if at == 0:
        total_out, notes_out = outs
        notes_out[...] = notes[...]
        for block in (YC, ZC):
            notes_out[block] = held[block, rows:, :LANES]
        notes = notes_out
    info = {block: info_row(notes, block) for block in range(6)}
    pairs = ((0, 4), (1, 5), (2, 6), (2, 7), (3, 8))
    total = domain_sums(pairs, factor, flags, info, sums)
    examples = sums.shape[1]
    for block, value in total.items():
        value = value + earlier[block]
        if at == 0:
            total_out[block] = value
        else:
            outs[block][...] = value[:, :examples]


def per_device(acts, grads, domain, listed):
    rows, width = acts.shape
    examples = rows // TOK
    quarter = width // 4
    me = lax.axis_index("ex")
    core = me % 2
    side = (me // 2) % 2
    mirrored = core ^ side

    flags = jnp.stack([
        mirrored, core * 2 * quarter, (1 - side) * quarter, core, side,
        core * 2 * quarter + (1 - side) * quarter,
    ]).astype(jnp.int32)
    places = jnp.stack([core * 2 + side, core * 2 + (1 - side)]).astype(jnp.int32)
    cross_places = jnp.stack([(1 - core) * 2 + side, (1 - core) * 2 + (1 - side)]).astype(jnp.int32)
    half_place = jnp.stack([1 - core]).astype(jnp.int32)

    own_info = jnp.concatenate(
        [domain, listed[0], jnp.zeros((LANES - examples - 2,), jnp.int32)]
    )
    own_info = jnp.broadcast_to(own_info.astype(acts.dtype)[None, :], (INFO, LANES))

    grads_ys = send(grads, across, 0)
    grads_zs = send(grads, along, 0)
    cut_ys, cut_zs, cut_ys_two, cut_zs_two = cut(acts, own_info, places)
    own_info, _ = lax.optimization_barrier((own_info, cut_ys))
    cut_yc, cut_zc, cut_yc_two, cut_zc_two = cut(acts, own_info, cross_places)
    own_info, _ = lax.optimization_barrier((own_info, cut_yc))
    ys_one = send(cut_ys, across, 0)
    zs_one = send(cut_zs, along, 0)
    ys_two = send(cut_ys_two, across, 0)
    zs_two = send(cut_zs_two, along, 0)
    yc_one = send(cut_yc, across, 1)
    zc_one = send(cut_zc, along, 1)
    yc_two = send(cut_yc_two, across, 1)

    def exchange(*values):
        return lax.cond(
            listed[0, 0] < 2,
            lambda *sent: tuple(send(value, stay, 1) for value in sent),
            lambda *sent: tuple(jnp.zeros_like(value) for value in sent),
            *values,
        )

    x_half, = exchange(cut_half(acts, grads, own_info, half_place))
    grads_ys, grads_zs, x_half = lax.optimization_barrier((grads_ys, grads_zs, x_half))
    grads_yc, grads_zc = exchange(grads_ys, grads_zs)
    factor = 1.0 / (TOK * math.sqrt(width * grads.shape[1]))

    grads_yc, ys_one, zs_one = lax.optimization_barrier((grads_yc, ys_one, zs_one))
    gram = grams(flags, grads, x_half, grads_ys, grads_yc, grads_zs, grads_zc)
    cut_zc_two, gram = lax.optimization_barrier((cut_zc_two, gram))
    zc_two = send(cut_zc_two, along, 1)

    smem = pl.BlockSpec(memory_space=pltpu.SMEM)
    vmem = pl.BlockSpec(memory_space=pltpu.VMEM)
    hbm = pl.BlockSpec(memory_space=pl.ANY)
    params = pltpu.CompilerParams(vmem_limit_bytes=VMEM_BYTES)
    own_v = pltpu.VMEM((rows, quarter), acts.dtype)
    slice_v = pltpu.VMEM((rows + INFO, quarter), acts.dtype)
    shared = [
        pltpu.VMEM((4, rows, rows), jnp.float32),
        pltpu.VMEM((2, rows, rows), jnp.float32),
        pltpu.VMEM((4, examples, rows), jnp.float32),
    ]
    partial_sums = jax.ShapeDtypeStruct((6, DOMAINS, LANES), jnp.float32)
    all_notes = jax.ShapeDtypeStruct((6, INFO, LANES), acts.dtype)
    first, notes = pl.pallas_call(
        functools.partial(first_kernel, factor),
        in_specs=[smem, vmem] + [hbm] * 7,
        out_specs=[vmem, vmem],
        out_shape=[partial_sums, all_notes],
        scratch_shapes=[own_v] + [slice_v] * 3 + [
            pltpu.VMEM((rows, 2 * quarter), acts.dtype),
            pltpu.VMEM((rows + INFO, 2 * quarter), acts.dtype),
        ] + shared + [pltpu.SemaphoreType.DMA((12,))],
        compiler_params=params,
        cost_estimate=SMALL,
        name="first",
    )(flags, own_info, acts, x_half, ys_one, zs_one, ys_two, zs_two, gram)

    def later(at, notes, earlier, messages, out_shape):
        return pl.pallas_call(
            functools.partial(later_kernel, factor, at),
            in_specs=[smem] + [vmem] * 2 + [hbm] * 7,
            out_specs=[vmem] * len(out_shape),
            out_shape=out_shape,
            scratch_shapes=[
                pltpu.VMEM((6, rows + INFO, messages[0].shape[1]), acts.dtype)
            ] + shared + [pltpu.SemaphoreType.DMA((10,))],
            compiler_params=params,
            cost_estimate=SMALL,
            name="later",
        )(flags, notes, earlier, acts, x_half, *messages, gram)

    second, notes = later(
        0, notes, first, (ys_one, yc_one, zs_one, zc_one),
        [partial_sums, all_notes],
    )
    sums = later(
        ys_one.shape[1], notes, second, (ys_two, yc_two, zs_two, zc_two),
        [jax.ShapeDtypeStruct((DOMAINS, examples), jnp.float32)] * 6,
    )

    total = sums[XS]
    total = total + send(sums[XC], stay, 1)
    total = total + send(sums[YS], across, 0)
    total = total + send(sums[YC], across, 1)
    total = total + send(sums[ZS], against, 0)
    total = total + send(sums[ZC], against, 1)
    return total.T


def solution(mesh):
    in_specs = (
        P(("groups", "ex"), None),
        P(("groups", "ex"), None),
        P(("groups", "ex")),
        P(("groups", "ex"), None),
    )
    out_specs = P(("groups", "ex"), None)
    return jax.shard_map(
        per_device, mesh=mesh, in_specs=in_specs, out_specs=out_specs, check_vma=False
    )
```

```python
import functools
import math

import jax
import jax.numpy as jnp
from jax import lax
from jax.experimental import pallas as pl
from jax.experimental.pallas import tpu as pltpu
from jax.sharding import PartitionSpec as P

TOK = 8
TOK_BITS = 3
DOMAINS = 48
LANES = 128
VMEM_BYTES = 63 * 1024 * 1024
LATER_VMEM_BYTES = 44 * 1024 * 1024

INFO = 16

XS, XC, YS, YC, ZS, ZC = range(6)
PAIRS = (
    (YS, XS, 1), (YS, ZS, 1), (YS, XC, 0), (XC, XS, 0),
    (YC, XC, 1), (YC, ZC, 1), (YC, ZS, 0), (YS, ZC, 0), (YC, XS, 0),
)
ONLY = {2: 0, 6: 0, 7: 1, 8: 1}
SLOT = (0, 1, 2, 3, 4, 5, 6, 6, 2)
FIRST = (0, 1, 2, 3)
SMALL = pl.CostEstimate(flops=1, bytes_accessed=1, transcendentals=0)
NT = (((1,), (1,)), ((), ()))
NN = (((1,), (0,)), ((), ()))


def across(chip):
    return chip ^ 1


def along(chip):
    return chip + 2 if chip & 1 else chip - 2


def against(chip):
    return chip - 2 if chip & 1 else chip + 2


def stay(chip):
    return chip


def send(value, move, flip):
    chips = lax.axis_size("ex") // 2
    pairs = [
        (2 * chip + core, 2 * (move(chip) % chips) + (core ^ flip))
        for chip in range(chips)
        for core in range(2)
    ]
    return lax.ppermute(value, "ex", pairs)


def token_major(rows):
    to = lax.broadcasted_iota(jnp.int32, (rows, rows), 0)
    source = lax.broadcasted_iota(jnp.int32, (rows, rows), 1)
    examples = rows // TOK
    place = (source & (TOK - 1)) * examples + lax.shift_right_logical(source, TOK_BITS)
    return (place == to).astype(jnp.bfloat16)


def reorder(order, block):
    return jnp.dot(order, block, preferred_element_type=jnp.float32).astype(jnp.bfloat16)


def put(target, value, info):
    rows = value.shape[0]
    target[:rows, :] = value
    target[rows:, :] = jnp.concatenate([info[...]] * (target.shape[1] // LANES), axis=1)


def chunks(quarter):
    second = quarter // LANES // 2 * LANES
    return quarter - second, second


def cut_kernel(places, info, y_acts, z_acts, y_one, z_one, y_two, z_two, order):
    rows, split = order.shape[0], y_one.shape[1]
    order[...] = token_major(rows)
    put(y_one, reorder(order[...], y_acts[:, :split]), info)
    put(z_one, z_acts[:, :split], info)
    put(y_two, reorder(order[...], y_acts[:, split:]), info)
    put(z_two, z_acts[:, split:], info)


def cut(acts, info, places):
    rows, width = acts.shape
    quarter = width // 4
    one, two = chunks(quarter)
    shapes = [(rows + INFO, one)] * 2 + [(rows + INFO, two)] * 2
    return pl.pallas_call(
        cut_kernel,
        grid_spec=pltpu.PrefetchScalarGridSpec(
            num_scalar_prefetch=1,
            grid=(1,),
            in_specs=[
                pl.BlockSpec((INFO, LANES), lambda i, p: (0, 0)),
                pl.BlockSpec((rows, quarter), lambda i, p: (0, p[0])),
                pl.BlockSpec((rows, quarter), lambda i, p: (0, p[1])),
            ],
            out_specs=[pl.BlockSpec(shape, lambda i, p: (0, 0)) for shape in shapes],
            scratch_shapes=[pltpu.VMEM((rows, rows), jnp.bfloat16)],
        ),
        out_shape=[jax.ShapeDtypeStruct(shape, acts.dtype) for shape in shapes],
        compiler_params=pltpu.CompilerParams(vmem_limit_bytes=VMEM_BYTES),
        cost_estimate=SMALL,
        name="cut",
    )(places, info, acts, acts)


def half_kernel(steps, place, info, acts, grads, out):
    @pl.when(pl.program_id(0) < steps)
    def _():
        put(out, acts[...], info)

    @pl.when(pl.program_id(0) >= steps)
    def _():
        put(out, grads[...], info)


def cut_half(acts, grads, info, place):
    rows, width = acts.shape
    half, depth = width // 2, grads.shape[1]
    step = math.gcd(math.gcd(half, depth), 512)
    steps = half // step
    return pl.pallas_call(
        functools.partial(half_kernel, steps),
        grid_spec=pltpu.PrefetchScalarGridSpec(
            num_scalar_prefetch=1,
            grid=(steps + depth // step,),
            in_specs=[
                pl.BlockSpec((INFO, LANES), lambda i, p: (0, 0)),
                pl.BlockSpec((rows, step), lambda i, p: (0, p[0] * steps + jnp.minimum(i, steps - 1))),
                pl.BlockSpec((rows, step), lambda i, p: (0, jnp.maximum(i - steps, 0))),
            ],
            out_specs=pl.BlockSpec((rows + INFO, step), lambda i, p: (0, i)),
        ),
        out_shape=jax.ShapeDtypeStruct((rows + INFO, half + depth), acts.dtype),
        compiler_params=pltpu.CompilerParams(vmem_limit_bytes=VMEM_BYTES),
        cost_estimate=SMALL,
        name="half",
    )(place, info, acts, grads)


def guarded(pair, mirrored, work):
    if pair in ONLY:
        pl.when(mirrored == ONLY[pair])(work)
    else:
        work()


def grams_kernel(flags, xs, xc, ys, yc, zs, zc, out, held, result, in_sems, out_sems):
    mirrored = flags[0]
    rows, depth = xs.shape
    order = token_major(rows)
    sources = (xs, xc.at[:rows, xc.shape[1] - depth:], ys, yc, zs, zc)
    loads = [
        pltpu.make_async_copy(source, held.at[at], in_sems.at[at])
        for at, source in enumerate(sources)
    ]
    for block in (YS, XS, ZS, XC, YC, ZC):
        loads[block].start()
    here = set()

    def ready(*blocks):
        for block in blocks:
            if block not in here:
                here.add(block)
                loads[block].wait()
                if block in (YS, YC):
                    held[block] = reorder(order, held[block])

    for pair, (one, two, _) in enumerate(PAIRS):
        ready(one, two)
        slot = SLOT[pair]

        def work(one=one, two=two, slot=slot):
            result[slot] = lax.dot_general(
                held[one], held[two], NT, preferred_element_type=jnp.float32
            )
            pltpu.make_async_copy(result.at[slot], out.at[slot], out_sems.at[slot]).start()

        guarded(pair, mirrored, work)
    for slot in range(7):
        pltpu.make_async_copy(result.at[slot], out.at[slot], out_sems.at[slot]).wait()


def grams(flags, grads, *messages):
    rows, width = grads.shape
    return pl.pallas_call(
        grams_kernel,
        in_specs=[pl.BlockSpec(memory_space=pltpu.SMEM)] + [pl.BlockSpec(memory_space=pl.ANY)] * 6,
        out_specs=pl.BlockSpec(memory_space=pl.ANY),
        out_shape=jax.ShapeDtypeStruct((7, rows, rows), jnp.float32),
        scratch_shapes=[
            pltpu.VMEM((6, rows, width), grads.dtype),
            pltpu.VMEM((7, rows, rows), jnp.float32),
            pltpu.SemaphoreType.DMA((6,)),
            pltpu.SemaphoreType.DMA((7,)),
        ],
        compiler_params=pltpu.CompilerParams(vmem_limit_bytes=VMEM_BYTES),
        cost_estimate=SMALL,
        name="grams",
    )(flags, grads, *messages)


def product(one, two, inner):
    rows = inner.shape[0]
    inner[...] = lax.dot_general(
        one[:rows, :], two[:rows, :], NT, preferred_element_type=jnp.float32
    )


def token_sums(inner, gram, sums, ordered=True):
    examples, rows = sums.shape
    if ordered:
        sums[...] = sum(
            inner[at:at + examples, :] * gram[at:at + examples, :]
            for at in range(0, rows, examples)
        )
    else:
        weighted = inner[...] * gram[...]
        sums[...] = weighted.reshape(examples, TOK, rows).sum(axis=1)


def two_parts(value):
    high = value.astype(jnp.bfloat16)
    return high, (value - high.astype(jnp.float32)).astype(jnp.bfloat16)


def dot_parts(value, table):
    high, low = two_parts(value)
    return lax.dot_general(low, table, NT, preferred_element_type=jnp.float32) + lax.dot_general(
        high, table, NT, preferred_element_type=jnp.float32
    )


def side_by_side(values):
    return jnp.concatenate(values, axis=1)


def domain_sums(pairs, factor, place, info, sums):
    count, examples, rows = sums.shape
    example = lax.broadcasted_iota(jnp.int32, (LANES, rows), 0)
    column = lax.broadcasted_iota(jnp.int32, (LANES, rows), 1)
    gather = (lax.shift_right_logical(column, TOK_BITS) == example).astype(jnp.bfloat16)
    tiles = dot_parts(sums[...].reshape(count * examples, rows), gather)
    tiles = tiles.reshape(count, examples, LANES)
    mirrored, core, side = place
    lane = lax.broadcasted_iota(jnp.int32, (1, LANES), 1)
    row = lax.broadcasted_iota(jnp.int32, (DOMAINS, LANES), 0)
    hot = {
        block: ((value.astype(jnp.int32) == row) & (lane < examples)).astype(jnp.bfloat16)
        for block, value in info.items()
    }

    def listed_flag(block, apart):
        return jnp.sum(jnp.where(lane == examples + apart, info[block], 0.0), axis=1, keepdims=True)

    pad = jnp.zeros((LANES - examples, LANES), jnp.float32)
    groups = {}
    for at, pair in pairs:
        one, two, apart = PAIRS[pair]
        if one == XC:
            two_leads = core == 0
        elif two in (XS, XC):
            two_leads = side == 0
        else:
            two_leads = side == 1
        flag = jnp.where(two_leads, listed_flag(two, apart), listed_flag(one, apart))
        if pair in ONLY:
            flag = jnp.where(mirrored == ONLY[pair], flag, 0.0)
        tile = jnp.concatenate([tiles[at], pad], axis=0) * (flag * factor)
        groups.setdefault(one, []).append((two, *two_parts(tile)))
    total = {}

    def add(block, term):
        total[block] = total[block] + term if block in total else term

    for one, group in groups.items():
        others = side_by_side([hot[two] for two, _, _ in group])
        highs = side_by_side([high for _, high, _ in group])
        lows = side_by_side([low for _, _, low in group])
        add(one, lax.dot_general(
            side_by_side([others, others]), side_by_side([highs, lows]), NT,
            preferred_element_type=jnp.float32,
        ))
        columns_of = lax.dot_general(
            side_by_side([hot[one], hot[one]]), jnp.concatenate([highs, lows], axis=0), NN,
            preferred_element_type=jnp.float32,
        )
        for at, (two, _, _) in enumerate(group):
            add(two, columns_of[:, at * LANES:(at + 1) * LANES])
    return total


def copies_of(loads, sems):
    return {
        key: pltpu.make_async_copy(source, target, sems.at[at])
        for at, (key, (source, target)) in enumerate(loads.items())
    }


def start(copies, *keys):
    for key in keys:
        copies[key].start()


def wait(copies, *keys):
    for key in keys:
        copies[key].wait()


def info_row(notes, block):
    return notes[block].astype(jnp.float32)[:1]


def columns(ref, at, width):
    return ref.at[:, pl.ds(pl.multiple_of(at, LANES), width)]


def first_kernel(factor, flags, own_info, acts, x_half, ys_one, zs_one, ys_two, zs_two, gram, out, notes,
                 xs_v, xc_v, ys_v, zs_v, own_v, half_v, gram_v, inner, sums, sems):
    half_at, in_half, work_at = flags[1], flags[2], flags[5]
    quarter = xs_v.shape[1]
    split = ys_one.shape[1]
    rows = inner.shape[1]
    copies = copies_of({
        "xs": (columns(acts, work_at, quarter), xs_v),
        "ys": (ys_one, ys_v.at[:, :split]),
        "ys2": (ys_two, ys_v.at[:, split:]),
        "g0": (gram.at[0], gram_v.at[0]),
        "zs": (zs_one, zs_v.at[:, :split]),
        "zs2": (zs_two, zs_v.at[:, split:]),
        "g1": (gram.at[1], gram_v.at[1]),
        "xc": (columns(x_half, in_half, quarter), xc_v),
        "g2": (gram.at[2], gram_v.at[2]),
        "own": (columns(acts, half_at, 2 * quarter), own_v),
        "half": (x_half.at[:, :2 * quarter], half_v),
        "g3": (gram.at[3], gram_v.at[3]),
    }, sems)
    start(copies, "xs", "ys", "ys2", "g0")
    wait(copies, "xs", "ys", "ys2")
    start(copies, "zs", "zs2", "g1", "xc", "g2")
    product(ys_v, xs_v, inner.at[0])
    wait(copies, "g0", "zs", "zs2", "xc")
    product(ys_v, zs_v, inner.at[1])
    token_sums(inner.at[0], gram_v.at[0], sums.at[0])
    start(copies, "own", "half", "g3")
    wait(copies, "g1", "g2")
    product(ys_v, xc_v, inner.at[0])
    token_sums(inner.at[1], gram_v.at[1], sums.at[1])
    wait(copies, "own", "half")
    product(half_v, own_v, inner.at[1])
    token_sums(inner.at[0], gram_v.at[2], sums.at[2])
    wait(copies, "g3")
    token_sums(inner.at[1], gram_v.at[3], sums.at[3], ordered=False)
    notes[...] = jnp.zeros_like(notes)
    notes[XS] = own_info[...]
    notes[XC] = xc_v[rows:, :LANES]
    notes[YS] = ys_v[rows:, split:split + LANES]
    notes[ZS] = zs_v[rows:, split:split + LANES]
    info = {block: info_row(notes, block) for block in (XS, XC, YS, ZS)}
    place = flags[0], flags[3], flags[4]
    total = domain_sums(tuple(enumerate(FIRST)), factor, place, info, sums)
    out[...] = jnp.zeros_like(out)
    for block, value in total.items():
        out[block] = value


def position():
    me = lax.axis_index("ex")
    return me & 1, lax.shift_right_logical(me, 1) & 1


def later_kernel(factor, at, notes, earlier, *refs):
    (acts, x_half, ys, yc, zs, zc, gram), refs = refs[:7], refs[7:]
    outs, (held, notes_v, earlier_v, gram_v, inner, sums, sems) = refs[:-7], refs[-7:]
    rows, width = inner.shape[1], held.shape[2]
    quarter = acts.shape[1] // 4
    core, side = position()
    mirrored = core ^ side
    in_half = (1 - side) * quarter
    work_at = core * 2 * quarter + in_half
    copies = copies_of({
        XS: (columns(acts, work_at + at, width), held.at[XS, :rows, :]),
        XC: (columns(x_half, in_half + at, width), held.at[XC]),
        YS: (ys, held.at[YS, :ys.shape[0], :]),
        YC: (yc, held.at[YC, :yc.shape[0], :]),
        ZS: (zs, held.at[ZS, :zs.shape[0], :]),
        ZC: (zc, held.at[ZC, :zc.shape[0], :]),
        "g4": (gram.at[4], gram_v.at[0]),
        "g5": (gram.at[5], gram_v.at[1]),
        "g6": (gram.at[6], gram_v.at[2]),
        "g2": (gram.at[2], gram_v.at[3]),
        "notes": (notes, notes_v),
        "earlier": (earlier, earlier_v),
    }, sems)
    start(copies, YC, XC, ZC)
    wait(copies, YC, XC)
    start(copies, "g4", YS, ZS)
    product(held.at[YC], held.at[XC], inner.at[0])
    wait(copies, ZC)
    start(copies, "g5", XS)
    product(held.at[YC], held.at[ZC], inner.at[1])
    wait(copies, "g4", YS, ZS)
    start(copies, "g6", "g2", "notes", "earlier")
    token_sums(inner.at[0], gram_v.at[0], sums.at[0])
    product(held.at[jnp.where(mirrored == 0, YC, YS)], held.at[jnp.where(mirrored == 0, ZS, ZC)], inner.at[0])
    wait(copies, "g5", XS)
    token_sums(inner.at[1], gram_v.at[1], sums.at[1])
    wait(copies, "g6", "g2", "notes", "earlier")

    @pl.when(mirrored == 1)
    def _():
        product(held.at[YC], held.at[XS], inner.at[1])
        token_sums(inner.at[0], gram_v.at[2], sums.at[2])
        token_sums(inner.at[1], gram_v.at[3], sums.at[3])

    @pl.when(mirrored == 0)
    def _():
        token_sums(inner.at[0], gram_v.at[2], sums.at[2])
        sums[3] = jnp.zeros(sums.shape[1:], jnp.float32)

    if at == 0:
        total_out, notes_out = outs
        for block in (YC, ZC):
            notes_v[block] = held[block, rows:, :LANES]
        notes_out[...] = notes_v[...]
    info = {block: info_row(notes_v, block) for block in range(6)}
    pairs = ((0, 4), (1, 5), (2, 6), (2, 7), (3, 8))
    total = domain_sums(pairs, factor, (mirrored, core, side), info, sums)
    examples = sums.shape[1]
    for block, value in total.items():
        value = value + earlier_v[block]
        if at == 0:
            total_out[block] = value
        else:
            outs[block][...] = value[:, :examples]


def per_device(acts, grads, domain, listed):
    rows, width = acts.shape
    examples = rows // TOK
    quarter = width // 4
    me = lax.axis_index("ex")
    core = me % 2
    side = (me // 2) % 2
    mirrored = core ^ side

    flags = jnp.stack([
        mirrored, core * 2 * quarter, (1 - side) * quarter, core, side,
        core * 2 * quarter + (1 - side) * quarter,
    ]).astype(jnp.int32)
    places = jnp.stack([core * 2 + side, core * 2 + (1 - side)]).astype(jnp.int32)
    cross_places = jnp.stack([(1 - core) * 2 + side, (1 - core) * 2 + (1 - side)]).astype(jnp.int32)
    half_place = jnp.stack([1 - core]).astype(jnp.int32)

    own_info = jnp.concatenate(
        [domain, listed[0], jnp.zeros((LANES - examples - 2,), jnp.int32)]
    )
    own_info = jnp.broadcast_to(own_info.astype(acts.dtype)[None, :], (INFO, LANES))

    grads_ys = send(grads, across, 0)
    grads_zs = send(grads, along, 0)
    cut_ys, cut_zs, cut_ys_two, cut_zs_two = cut(acts, own_info, places)
    own_info, _ = lax.optimization_barrier((own_info, cut_ys))
    cut_yc, cut_zc, cut_yc_two, cut_zc_two = cut(acts, own_info, cross_places)
    own_info, _ = lax.optimization_barrier((own_info, cut_yc))
    ys_one = send(cut_ys, across, 0)
    zs_one = send(cut_zs, along, 0)
    ys_two = send(cut_ys_two, across, 0)
    zs_two = send(cut_zs_two, along, 0)
    yc_one = send(cut_yc, across, 1)
    zc_one = send(cut_zc, along, 1)
    yc_two = send(cut_yc_two, across, 1)

    def exchange(*values):
        return lax.cond(
            listed[0, 0] < 2,
            lambda *sent: tuple(send(value, stay, 1) for value in sent),
            lambda *sent: tuple(jnp.zeros_like(value) for value in sent),
            *values,
        )

    x_half, = exchange(cut_half(acts, grads, own_info, half_place))
    grads_ys, grads_zs, x_half = lax.optimization_barrier((grads_ys, grads_zs, x_half))
    grads_yc, grads_zc = exchange(grads_ys, grads_zs)
    factor = 1.0 / (TOK * math.sqrt(width * grads.shape[1]))

    grads_yc, ys_one, zs_one = lax.optimization_barrier((grads_yc, ys_one, zs_one))
    gram = grams(flags, grads, x_half, grads_ys, grads_yc, grads_zs, grads_zc)
    cut_zc_two, gram = lax.optimization_barrier((cut_zc_two, gram))
    zc_two = send(cut_zc_two, along, 1)

    smem = pl.BlockSpec(memory_space=pltpu.SMEM)
    vmem = pl.BlockSpec(memory_space=pltpu.VMEM)
    hbm = pl.BlockSpec(memory_space=pl.ANY)
    params = pltpu.CompilerParams(vmem_limit_bytes=VMEM_BYTES)
    own_v = pltpu.VMEM((rows, quarter), acts.dtype)
    slice_v = pltpu.VMEM((rows + INFO, quarter), acts.dtype)
    shared = [
        pltpu.VMEM((4, rows, rows), jnp.float32),
        pltpu.VMEM((2, rows, rows), jnp.float32),
        pltpu.VMEM((4, examples, rows), jnp.float32),
    ]
    partial_sums = jax.ShapeDtypeStruct((6, DOMAINS, LANES), jnp.float32)
    all_notes = jax.ShapeDtypeStruct((6, INFO, LANES), acts.dtype)
    first, notes = pl.pallas_call(
        functools.partial(first_kernel, factor),
        in_specs=[smem, vmem] + [hbm] * 7,
        out_specs=[vmem, vmem],
        out_shape=[partial_sums, all_notes],
        scratch_shapes=[own_v] + [slice_v] * 3 + [
            pltpu.VMEM((rows, 2 * quarter), acts.dtype),
            pltpu.VMEM((rows + INFO, 2 * quarter), acts.dtype),
        ] + shared + [pltpu.SemaphoreType.DMA((12,))],
        compiler_params=params,
        cost_estimate=SMALL,
        name="first",
    )(flags, own_info, acts, x_half, ys_one, zs_one, ys_two, zs_two, gram)

    def later(at, notes, earlier, messages, out_shape):
        return pl.pallas_call(
            functools.partial(later_kernel, factor, at),
            in_specs=[hbm] * 9,
            out_specs=[vmem] * len(out_shape),
            out_shape=out_shape,
            scratch_shapes=[
                pltpu.VMEM((6, rows + INFO, messages[0].shape[1]), acts.dtype),
                pltpu.VMEM(all_notes.shape, acts.dtype),
                pltpu.VMEM(partial_sums.shape, jnp.float32),
            ] + shared + [pltpu.SemaphoreType.DMA((12,))],
            compiler_params=pltpu.CompilerParams(vmem_limit_bytes=LATER_VMEM_BYTES),
            cost_estimate=SMALL,
            name="later",
        )(notes, earlier, acts, x_half, *messages, gram)

    second, notes = later(
        0, notes, first, (ys_one, yc_one, zs_one, zc_one),
        [partial_sums, all_notes],
    )
    sums = later(
        ys_one.shape[1], notes, second, (ys_two, yc_two, zs_two, zc_two),
        [jax.ShapeDtypeStruct((DOMAINS, examples), jnp.float32)] * 6,
    )

    total = sums[XS]
    total = total + send(sums[XC], stay, 1)
    total = total + send(sums[YS], across, 0)
    total = total + send(sums[YC], across, 1)
    total = total + send(sums[ZS], against, 0)
    total = total + send(sums[ZC], against, 1)
    return total.T


def solution(mesh):
    in_specs = (
        P(("groups", "ex"), None),
        P(("groups", "ex"), None),
        P(("groups", "ex")),
        P(("groups", "ex"), None),
    )
    out_specs = P(("groups", "ex"), None)
    return jax.shard_map(
        per_device, mesh=mesh, in_specs=in_specs, out_specs=out_specs, check_vma=False
    )
```

```python
import functools
import math

import jax
import jax.numpy as jnp
from jax import lax
from jax.experimental import pallas as pl
from jax.experimental.pallas import tpu as pltpu
from jax.sharding import PartitionSpec as P

TOK = 8
TOK_BITS = 3
DOMAINS = 48
LANES = 128
VMEM_BYTES = 63 * 1024 * 1024
LATER_VMEM_BYTES = 44 * 1024 * 1024

INFO = 16

XS, XC, YS, YC, ZS, ZC = range(6)
PAIRS = (
    (YS, XS, 1), (YS, ZS, 1), (YS, XC, 0), (XC, XS, 0),
    (YC, XC, 1), (YC, ZC, 1), (YC, ZS, 0), (YS, ZC, 0), (YC, XS, 0),
)
ONLY = {2: 0, 6: 0, 7: 1, 8: 1}
SLOT = (0, 1, 2, 3, 4, 5, 6, 6, 2)
FIRST = (0, 1, 2, 3)
SMALL = pl.CostEstimate(flops=1, bytes_accessed=1, transcendentals=0)
NT = (((1,), (1,)), ((), ()))
NN = (((1,), (0,)), ((), ()))


def across(chip):
    return chip ^ 1


def along(chip):
    return chip + 2 if chip & 1 else chip - 2


def against(chip):
    return chip - 2 if chip & 1 else chip + 2


def stay(chip):
    return chip


def send(value, move, flip):
    chips = lax.axis_size("ex") // 2
    pairs = [
        (2 * chip + core, 2 * (move(chip) % chips) + (core ^ flip))
        for chip in range(chips)
        for core in range(2)
    ]
    return lax.ppermute(value, "ex", pairs)


def token_major(rows):
    to = lax.broadcasted_iota(jnp.int32, (rows, rows), 0)
    source = lax.broadcasted_iota(jnp.int32, (rows, rows), 1)
    examples = rows // TOK
    place = (source & (TOK - 1)) * examples + lax.shift_right_logical(source, TOK_BITS)
    return (place == to).astype(jnp.bfloat16)


def reorder(order, block):
    return jnp.dot(order, block, preferred_element_type=jnp.float32).astype(jnp.bfloat16)


def put(target, value, info):
    rows = value.shape[0]
    target[:rows, :] = value
    target[rows:, :] = jnp.concatenate([info[...]] * (target.shape[1] // LANES), axis=1)


def chunks(quarter):
    second = quarter // LANES // 2 * LANES
    return quarter - second, second


def cut_kernel(places, info, y_acts, z_acts, y_one, z_one, y_two, z_two, order):
    rows, split = order.shape[0], y_one.shape[1]
    order[...] = token_major(rows)
    put(y_one, reorder(order[...], y_acts[:, :split]), info)
    put(z_one, z_acts[:, :split], info)
    put(y_two, reorder(order[...], y_acts[:, split:]), info)
    put(z_two, z_acts[:, split:], info)


def cut(acts, info, places):
    rows, width = acts.shape
    quarter = width // 4
    one, two = chunks(quarter)
    shapes = [(rows + INFO, one)] * 2 + [(rows + INFO, two)] * 2
    return pl.pallas_call(
        cut_kernel,
        grid_spec=pltpu.PrefetchScalarGridSpec(
            num_scalar_prefetch=1,
            grid=(1,),
            in_specs=[
                pl.BlockSpec((INFO, LANES), lambda i, p: (0, 0)),
                pl.BlockSpec((rows, quarter), lambda i, p: (0, p[0])),
                pl.BlockSpec((rows, quarter), lambda i, p: (0, p[1])),
            ],
            out_specs=[pl.BlockSpec(shape, lambda i, p: (0, 0)) for shape in shapes],
            scratch_shapes=[pltpu.VMEM((rows, rows), jnp.bfloat16)],
        ),
        out_shape=[jax.ShapeDtypeStruct(shape, acts.dtype) for shape in shapes],
        compiler_params=pltpu.CompilerParams(vmem_limit_bytes=VMEM_BYTES),
        cost_estimate=SMALL,
        name="cut",
    )(places, info, acts, acts)


def half_kernel(steps, place, info, acts, grads, out):
    @pl.when(pl.program_id(0) < steps)
    def _():
        put(out, acts[...], info)

    @pl.when(pl.program_id(0) >= steps)
    def _():
        put(out, grads[...], info)


def cut_half(acts, grads, info, place):
    rows, width = acts.shape
    half, depth = width // 2, grads.shape[1]
    step = math.gcd(math.gcd(half, depth), 512)
    steps = half // step
    return pl.pallas_call(
        functools.partial(half_kernel, steps),
        grid_spec=pltpu.PrefetchScalarGridSpec(
            num_scalar_prefetch=1,
            grid=(steps + depth // step,),
            in_specs=[
                pl.BlockSpec((INFO, LANES), lambda i, p: (0, 0)),
                pl.BlockSpec((rows, step), lambda i, p: (0, p[0] * steps + jnp.minimum(i, steps - 1))),
                pl.BlockSpec((rows, step), lambda i, p: (0, jnp.maximum(i - steps, 0))),
            ],
            out_specs=pl.BlockSpec((rows + INFO, step), lambda i, p: (0, i)),
        ),
        out_shape=jax.ShapeDtypeStruct((rows + INFO, half + depth), acts.dtype),
        compiler_params=pltpu.CompilerParams(vmem_limit_bytes=VMEM_BYTES),
        cost_estimate=SMALL,
        name="half",
    )(place, info, acts, grads)


def guarded(pair, mirrored, work):
    if pair in ONLY:
        pl.when(mirrored == ONLY[pair])(work)
    else:
        work()


def grams_kernel(flags, xs, xc, ys, yc, zs, zc, out, held, result, in_sems, out_sems):
    mirrored = flags[0]
    rows, depth = xs.shape
    order = token_major(rows)
    sources = (xs, xc.at[:rows, xc.shape[1] - depth:], ys, yc, zs, zc)
    loads = [
        pltpu.make_async_copy(source, held.at[at], in_sems.at[at])
        for at, source in enumerate(sources)
    ]
    for block in (YS, XS, ZS, XC, YC, ZC):
        loads[block].start()
    here = set()

    def ready(*blocks):
        for block in blocks:
            if block not in here:
                here.add(block)
                loads[block].wait()
                if block in (YS, YC):
                    held[block] = reorder(order, held[block])

    for pair, (one, two, _) in enumerate(PAIRS):
        ready(one, two)
        slot = SLOT[pair]

        def work(one=one, two=two, slot=slot):
            result[slot] = lax.dot_general(
                held[one], held[two], NT, preferred_element_type=jnp.float32
            )
            pltpu.make_async_copy(result.at[slot], out.at[slot], out_sems.at[slot]).start()

        guarded(pair, mirrored, work)
    for slot in range(7):
        pltpu.make_async_copy(result.at[slot], out.at[slot], out_sems.at[slot]).wait()


def grams(flags, grads, *messages):
    rows, width = grads.shape
    return pl.pallas_call(
        grams_kernel,
        in_specs=[pl.BlockSpec(memory_space=pltpu.SMEM)] + [pl.BlockSpec(memory_space=pl.ANY)] * 6,
        out_specs=pl.BlockSpec(memory_space=pl.ANY),
        out_shape=jax.ShapeDtypeStruct((7, rows, rows), jnp.float32),
        scratch_shapes=[
            pltpu.VMEM((6, rows, width), grads.dtype),
            pltpu.VMEM((7, rows, rows), jnp.float32),
            pltpu.SemaphoreType.DMA((6,)),
            pltpu.SemaphoreType.DMA((7,)),
        ],
        compiler_params=pltpu.CompilerParams(vmem_limit_bytes=VMEM_BYTES),
        cost_estimate=SMALL,
        name="grams",
    )(flags, grads, *messages)


def product(one, two, inner):
    rows = inner.shape[0]
    inner[...] = lax.dot_general(
        one[:rows, :], two[:rows, :], NT, preferred_element_type=jnp.float32
    )


def token_sums(inner, gram, sums, ordered=True):
    examples, rows = sums.shape
    if ordered:
        sums[...] = sum(
            inner[at:at + examples, :] * gram[at:at + examples, :]
            for at in range(0, rows, examples)
        )
    else:
        weighted = inner[...] * gram[...]
        sums[...] = weighted.reshape(examples, TOK, rows).sum(axis=1)


def two_parts(value):
    high = value.astype(jnp.bfloat16)
    return high, (value - high.astype(jnp.float32)).astype(jnp.bfloat16)


def dot_parts(value, table):
    high, low = two_parts(value)
    return lax.dot_general(low, table, NT, preferred_element_type=jnp.float32) + lax.dot_general(
        high, table, NT, preferred_element_type=jnp.float32
    )


def side_by_side(values):
    return jnp.concatenate(values, axis=1)


def domain_sums(pairs, factor, place, info, sums):
    count, examples, rows = sums.shape
    example = lax.broadcasted_iota(jnp.int32, (LANES, rows), 0)
    column = lax.broadcasted_iota(jnp.int32, (LANES, rows), 1)
    gather = (lax.shift_right_logical(column, TOK_BITS) == example).astype(jnp.bfloat16)
    tiles = dot_parts(sums[...].reshape(count * examples, rows), gather)
    tiles = tiles.reshape(count, examples, LANES)
    mirrored, core, side = place
    lane = lax.broadcasted_iota(jnp.int32, (1, LANES), 1)
    row = lax.broadcasted_iota(jnp.int32, (DOMAINS, LANES), 0)
    hot = {
        block: ((value.astype(jnp.int32) == row) & (lane < examples)).astype(jnp.bfloat16)
        for block, value in info.items()
    }

    def listed_flag(block, apart):
        return jnp.sum(jnp.where(lane == examples + apart, info[block], 0.0), axis=1, keepdims=True)

    pad = jnp.zeros((LANES - examples, LANES), jnp.float32)
    groups = {}
    for at, pair in pairs:
        one, two, apart = PAIRS[pair]
        if one == XC:
            two_leads = core == 0
        elif two in (XS, XC):
            two_leads = side == 0
        else:
            two_leads = side == 1
        flag = jnp.where(two_leads, listed_flag(two, apart), listed_flag(one, apart))
        if pair in ONLY:
            flag = jnp.where(mirrored == ONLY[pair], flag, 0.0)
        tile = jnp.concatenate([tiles[at], pad], axis=0) * (flag * factor)
        groups.setdefault(one, []).append((two, *two_parts(tile)))
    total = {}

    def add(block, term):
        total[block] = total[block] + term if block in total else term

    for one, group in groups.items():
        others = side_by_side([hot[two] for two, _, _ in group])
        highs = side_by_side([high for _, high, _ in group])
        lows = side_by_side([low for _, _, low in group])
        add(one, lax.dot_general(
            side_by_side([others, others]), side_by_side([highs, lows]), NT,
            preferred_element_type=jnp.float32,
        ))
        columns_of = lax.dot_general(
            side_by_side([hot[one], hot[one]]), jnp.concatenate([highs, lows], axis=0), NN,
            preferred_element_type=jnp.float32,
        )
        for at, (two, _, _) in enumerate(group):
            add(two, columns_of[:, at * LANES:(at + 1) * LANES])
    return total


def copies_of(loads, sems, step=None):
    copies = {}
    for at, (key, (source, target)) in enumerate(loads.items()):
        rows = target.shape[0]
        pieces = [
            (first, min(step or rows, rows - first)) for first in range(0, rows, step or rows)
        ]
        copies[key] = [
            pltpu.make_async_copy(
                source.at[pl.ds(first, size)], target.at[pl.ds(first, size)], sems.at[at, piece]
            )
            for piece, (first, size) in enumerate(pieces)
        ]
    return copies


def start(copies, *keys):
    for key in keys:
        for copy in copies[key]:
            copy.start()


def wait(copies, *keys):
    for key in keys:
        for copy in copies[key]:
            copy.wait()


def info_row(notes, block):
    return notes[block].astype(jnp.float32)[:1]


def columns(ref, at, width):
    return ref.at[:, pl.ds(pl.multiple_of(at, LANES), width)]


def first_kernel(factor, flags, own_info, acts, x_half, ys_one, zs_one, ys_two, zs_two, gram, out, notes,
                 xs_v, xc_v, ys_v, zs_v, own_v, half_v, gram_v, inner, sums, sems):
    half_at, in_half, work_at = flags[1], flags[2], flags[5]
    quarter = xs_v.shape[1]
    split = ys_one.shape[1]
    rows = inner.shape[1]
    copies = copies_of({
        "xs": (columns(acts, work_at, quarter), xs_v),
        "ys": (ys_one, ys_v.at[:, :split]),
        "ys2": (ys_two, ys_v.at[:, split:]),
        "g0": (gram.at[0], gram_v.at[0]),
        "zs": (zs_one, zs_v.at[:, :split]),
        "zs2": (zs_two, zs_v.at[:, split:]),
        "g1": (gram.at[1], gram_v.at[1]),
        "xc": (columns(x_half, in_half, quarter), xc_v),
        "g2": (gram.at[2], gram_v.at[2]),
        "own": (columns(acts, half_at, 2 * quarter), own_v),
        "half": (x_half.at[:, :2 * quarter], half_v),
        "g3": (gram.at[3], gram_v.at[3]),
    }, sems)
    start(copies, "xs", "ys", "ys2", "g0")
    wait(copies, "xs", "ys", "ys2")
    start(copies, "zs", "zs2", "g1", "xc", "g2")
    product(ys_v, xs_v, inner.at[0])
    wait(copies, "g0", "zs", "zs2", "xc")
    product(ys_v, zs_v, inner.at[1])
    token_sums(inner.at[0], gram_v.at[0], sums.at[0])
    start(copies, "own", "half", "g3")
    wait(copies, "g1", "g2")
    product(ys_v, xc_v, inner.at[0])
    token_sums(inner.at[1], gram_v.at[1], sums.at[1])
    wait(copies, "own", "half")
    product(half_v, own_v, inner.at[1])
    token_sums(inner.at[0], gram_v.at[2], sums.at[2])
    wait(copies, "g3")
    token_sums(inner.at[1], gram_v.at[3], sums.at[3], ordered=False)
    notes[...] = jnp.zeros_like(notes)
    notes[XS] = own_info[...]
    notes[XC] = xc_v[rows:, :LANES]
    notes[YS] = ys_v[rows:, split:split + LANES]
    notes[ZS] = zs_v[rows:, split:split + LANES]
    info = {block: info_row(notes, block) for block in (XS, XC, YS, ZS)}
    place = flags[0], flags[3], flags[4]
    total = domain_sums(tuple(enumerate(FIRST)), factor, place, info, sums)
    out[...] = jnp.zeros_like(out)
    for block, value in total.items():
        out[block] = value


def position():
    me = lax.axis_index("ex")
    return me & 1, lax.shift_right_logical(me, 1) & 1


def later_kernel(factor, at, notes, earlier, *refs):
    (acts, x_half, ys, yc, zs, zc, gram), refs = refs[:7], refs[7:]
    outs, (held, notes_v, earlier_v, gram_v, inner, sums, sems) = refs[:-7], refs[-7:]
    rows, width = inner.shape[1], held.shape[2]
    quarter = acts.shape[1] // 4
    core, side = position()
    mirrored = core ^ side
    in_half = (1 - side) * quarter
    work_at = core * 2 * quarter + in_half
    copies = copies_of({
        XS: (columns(acts, work_at + at, width), held.at[XS, :rows, :]),
        XC: (columns(x_half, in_half + at, width), held.at[XC]),
        YS: (ys, held.at[YS, :ys.shape[0], :]),
        YC: (yc, held.at[YC, :yc.shape[0], :]),
        ZS: (zs, held.at[ZS, :zs.shape[0], :]),
        ZC: (zc, held.at[ZC, :zc.shape[0], :]),
        "g4": (gram.at[4], gram_v.at[0]),
        "g5": (gram.at[5], gram_v.at[1]),
        "g6": (gram.at[6], gram_v.at[2]),
        "g2": (gram.at[2], gram_v.at[3]),
        "notes": (notes, notes_v),
        "earlier": (earlier, earlier_v),
    }, sems, 192)
    start(copies, YC, XC, ZC)
    wait(copies, YC, XC)
    start(copies, "g4", YS, ZS)
    product(held.at[YC], held.at[XC], inner.at[0])
    wait(copies, ZC)
    start(copies, "g5", XS)
    product(held.at[YC], held.at[ZC], inner.at[1])
    wait(copies, "g4", YS, ZS)
    start(copies, "g6", "g2", "notes", "earlier")
    token_sums(inner.at[0], gram_v.at[0], sums.at[0])
    product(held.at[jnp.where(mirrored == 0, YC, YS)], held.at[jnp.where(mirrored == 0, ZS, ZC)], inner.at[0])
    wait(copies, "g5", XS)
    token_sums(inner.at[1], gram_v.at[1], sums.at[1])
    wait(copies, "g6", "g2", "notes", "earlier")

    @pl.when(mirrored == 1)
    def _():
        product(held.at[YC], held.at[XS], inner.at[1])
        token_sums(inner.at[0], gram_v.at[2], sums.at[2])
        token_sums(inner.at[1], gram_v.at[3], sums.at[3])

    @pl.when(mirrored == 0)
    def _():
        token_sums(inner.at[0], gram_v.at[2], sums.at[2])
        sums[3] = jnp.zeros(sums.shape[1:], jnp.float32)

    if at == 0:
        total_out, notes_out = outs
        for block in (YC, ZC):
            notes_v[block] = held[block, rows:, :LANES]
        notes_out[...] = notes_v[...]
    info = {block: info_row(notes_v, block) for block in range(6)}
    pairs = ((0, 4), (1, 5), (2, 6), (2, 7), (3, 8))
    total = domain_sums(pairs, factor, (mirrored, core, side), info, sums)
    examples = sums.shape[1]
    for block, value in total.items():
        value = value + earlier_v[block]
        if at == 0:
            total_out[block] = value
        else:
            outs[block][...] = value[:, :examples]


def per_device(acts, grads, domain, listed):
    rows, width = acts.shape
    examples = rows // TOK
    quarter = width // 4
    me = lax.axis_index("ex")
    core = me % 2
    side = (me // 2) % 2
    mirrored = core ^ side

    flags = jnp.stack([
        mirrored, core * 2 * quarter, (1 - side) * quarter, core, side,
        core * 2 * quarter + (1 - side) * quarter,
    ]).astype(jnp.int32)
    places = jnp.stack([core * 2 + side, core * 2 + (1 - side)]).astype(jnp.int32)
    cross_places = jnp.stack([(1 - core) * 2 + side, (1 - core) * 2 + (1 - side)]).astype(jnp.int32)
    half_place = jnp.stack([1 - core]).astype(jnp.int32)

    own_info = jnp.concatenate(
        [domain, listed[0], jnp.zeros((LANES - examples - 2,), jnp.int32)]
    )
    own_info = jnp.broadcast_to(own_info.astype(acts.dtype)[None, :], (INFO, LANES))

    grads_ys = send(grads, across, 0)
    grads_zs = send(grads, along, 0)
    cut_ys, cut_zs, cut_ys_two, cut_zs_two = cut(acts, own_info, places)
    own_info, _ = lax.optimization_barrier((own_info, cut_ys))
    cut_yc, cut_zc, cut_yc_two, cut_zc_two = cut(acts, own_info, cross_places)
    own_info, _ = lax.optimization_barrier((own_info, cut_yc))
    ys_one = send(cut_ys, across, 0)
    zs_one = send(cut_zs, along, 0)
    ys_two = send(cut_ys_two, across, 0)
    zs_two = send(cut_zs_two, along, 0)
    yc_one = send(cut_yc, across, 1)
    zc_one = send(cut_zc, along, 1)
    yc_two = send(cut_yc_two, across, 1)

    def exchange(*values):
        return lax.cond(
            listed[0, 0] < 2,
            lambda *sent: tuple(send(value, stay, 1) for value in sent),
            lambda *sent: tuple(jnp.zeros_like(value) for value in sent),
            *values,
        )

    x_half, = exchange(cut_half(acts, grads, own_info, half_place))
    grads_ys, grads_zs, x_half = lax.optimization_barrier((grads_ys, grads_zs, x_half))
    grads_yc, grads_zc = exchange(grads_ys, grads_zs)
    factor = 1.0 / (TOK * math.sqrt(width * grads.shape[1]))

    grads_yc, ys_one, zs_one = lax.optimization_barrier((grads_yc, ys_one, zs_one))
    gram = grams(flags, grads, x_half, grads_ys, grads_yc, grads_zs, grads_zc)
    cut_zc_two, gram = lax.optimization_barrier((cut_zc_two, gram))
    zc_two = send(cut_zc_two, along, 1)

    smem = pl.BlockSpec(memory_space=pltpu.SMEM)
    vmem = pl.BlockSpec(memory_space=pltpu.VMEM)
    hbm = pl.BlockSpec(memory_space=pl.ANY)
    params = pltpu.CompilerParams(vmem_limit_bytes=VMEM_BYTES)
    own_v = pltpu.VMEM((rows, quarter), acts.dtype)
    slice_v = pltpu.VMEM((rows + INFO, quarter), acts.dtype)
    shared = [
        pltpu.VMEM((4, rows, rows), jnp.float32),
        pltpu.VMEM((2, rows, rows), jnp.float32),
        pltpu.VMEM((4, examples, rows), jnp.float32),
    ]
    partial_sums = jax.ShapeDtypeStruct((6, DOMAINS, LANES), jnp.float32)
    all_notes = jax.ShapeDtypeStruct((6, INFO, LANES), acts.dtype)
    first, notes = pl.pallas_call(
        functools.partial(first_kernel, factor),
        in_specs=[smem, vmem] + [hbm] * 7,
        out_specs=[vmem, vmem],
        out_shape=[partial_sums, all_notes],
        scratch_shapes=[own_v] + [slice_v] * 3 + [
            pltpu.VMEM((rows, 2 * quarter), acts.dtype),
            pltpu.VMEM((rows + INFO, 2 * quarter), acts.dtype),
        ] + shared + [pltpu.SemaphoreType.DMA((12, 1))],
        compiler_params=params,
        cost_estimate=SMALL,
        name="first",
    )(flags, own_info, acts, x_half, ys_one, zs_one, ys_two, zs_two, gram)

    def later(at, notes, earlier, messages, out_shape):
        return pl.pallas_call(
            functools.partial(later_kernel, factor, at),
            in_specs=[hbm] * 9,
            out_specs=[vmem] * len(out_shape),
            out_shape=out_shape,
            scratch_shapes=[
                pltpu.VMEM((6, rows + INFO, messages[0].shape[1]), acts.dtype),
                pltpu.VMEM(all_notes.shape, acts.dtype),
                pltpu.VMEM(partial_sums.shape, jnp.float32),
            ] + shared + [pltpu.SemaphoreType.DMA((12, 5))],
            compiler_params=pltpu.CompilerParams(vmem_limit_bytes=LATER_VMEM_BYTES),
            cost_estimate=SMALL,
            name="later",
        )(notes, earlier, acts, x_half, *messages, gram)

    second, notes = later(
        0, notes, first, (ys_one, yc_one, zs_one, zc_one),
        [partial_sums, all_notes],
    )
    sums = later(
        ys_one.shape[1], notes, second, (ys_two, yc_two, zs_two, zc_two),
        [jax.ShapeDtypeStruct((DOMAINS, examples), jnp.float32)] * 6,
    )

    total = sums[XS]
    total = total + send(sums[ZS], against, 0)
    total = total + send(sums[ZC], against, 1)
    total = total + send(sums[YS], across, 0)
    total = total + send(sums[YC], across, 1)
    total = total + send(sums[XC], stay, 1)
    return total.T


def solution(mesh):
    in_specs = (
        P(("groups", "ex"), None),
        P(("groups", "ex"), None),
        P(("groups", "ex")),
        P(("groups", "ex"), None),
    )
    out_specs = P(("groups", "ex"), None)
    return jax.shard_map(
        per_device, mesh=mesh, in_specs=in_specs, out_specs=out_specs, check_vma=False
    )
```

```python
import functools
import math

import jax
import jax.numpy as jnp
from jax import lax
from jax.experimental import pallas as pl
from jax.experimental.pallas import tpu as pltpu
from jax.sharding import PartitionSpec as P

TOK = 8
TOK_BITS = 3
DOMAINS = 48
LANES = 128
VMEM_BYTES = 63 * 1024 * 1024
PAIRS_VMEM_BYTES = 44 * 1024 * 1024

INFO = 16

XS, XC, YS, YC, ZS, ZC = range(6)
PAIRS = (
    (YS, XS, 1), (YS, ZS, 1), (YS, XC, 0), (XC, XS, 0),
    (YC, XC, 1), (YC, ZC, 1), (YC, ZS, 0), (YS, ZC, 0), (YC, XS, 0),
)
ONLY = {2: 0, 6: 0, 7: 1, 8: 1}
SLOT = (0, 1, 2, 3, 4, 5, 6, 6, 2)
FIRST = (0, 1, 2, 3)
SMALL = pl.CostEstimate(flops=1, bytes_accessed=1, transcendentals=0)
NT = (((1,), (1,)), ((), ()))
NN = (((1,), (0,)), ((), ()))


def across(chip):
    return chip ^ 1


def along(chip):
    return chip + 2 if chip & 1 else chip - 2


def against(chip):
    return chip - 2 if chip & 1 else chip + 2


def stay(chip):
    return chip


def send(value, move, flip):
    chips = lax.axis_size("ex") // 2
    pairs = [
        (2 * chip + core, 2 * (move(chip) % chips) + (core ^ flip))
        for chip in range(chips)
        for core in range(2)
    ]
    return lax.ppermute(value, "ex", pairs)


def token_major(rows):
    to = lax.broadcasted_iota(jnp.int32, (rows, rows), 0)
    source = lax.broadcasted_iota(jnp.int32, (rows, rows), 1)
    examples = rows // TOK
    place = (source & (TOK - 1)) * examples + lax.shift_right_logical(source, TOK_BITS)
    return (place == to).astype(jnp.bfloat16)


def reorder(order, block):
    return jnp.dot(order, block, preferred_element_type=jnp.float32).astype(jnp.bfloat16)


def put(target, value, info):
    rows = value.shape[0]
    target[:rows, :] = value
    target[rows:, :] = jnp.concatenate([info[...]] * (target.shape[1] // LANES), axis=1)


def chunks(quarter):
    second = quarter // LANES * 3 // 10 * LANES
    return quarter - second, second


def cut_kernel(places, info, y_acts, z_acts, y_one, z_one, y_two, z_two, order):
    rows, split = order.shape[0], y_one.shape[1]
    order[...] = token_major(rows)
    put(y_one, reorder(order[...], y_acts[:, :split]), info)
    put(z_one, z_acts[:, :split], info)
    y_two[...] = reorder(order[...], y_acts[:, split:])
    z_two[...] = z_acts[:, split:]


def cut(acts, info, places):
    rows, width = acts.shape
    quarter = width // 4
    one, two = chunks(quarter)
    shapes = [(rows + INFO, one)] * 2 + [(rows, two)] * 2
    return pl.pallas_call(
        cut_kernel,
        grid_spec=pltpu.PrefetchScalarGridSpec(
            num_scalar_prefetch=1,
            grid=(1,),
            in_specs=[
                pl.BlockSpec((INFO, LANES), lambda i, p: (0, 0)),
                pl.BlockSpec((rows, quarter), lambda i, p: (0, p[0])),
                pl.BlockSpec((rows, quarter), lambda i, p: (0, p[1])),
            ],
            out_specs=[pl.BlockSpec(shape, lambda i, p: (0, 0)) for shape in shapes],
            scratch_shapes=[pltpu.VMEM((rows, rows), jnp.bfloat16)],
        ),
        out_shape=[jax.ShapeDtypeStruct(shape, acts.dtype) for shape in shapes],
        compiler_params=pltpu.CompilerParams(vmem_limit_bytes=VMEM_BYTES),
        cost_estimate=SMALL,
        name="cut",
    )(places, info, acts, acts)


def half_kernel(steps, place, info, acts, grads, out):
    @pl.when(pl.program_id(0) < steps)
    def _():
        put(out, acts[...], info)

    @pl.when(pl.program_id(0) >= steps)
    def _():
        put(out, grads[...], info)


def cut_half(acts, grads, info, place):
    rows, width = acts.shape
    half, depth = width // 2, grads.shape[1]
    step = math.gcd(math.gcd(half, depth), 512)
    steps = half // step
    return pl.pallas_call(
        functools.partial(half_kernel, steps),
        grid_spec=pltpu.PrefetchScalarGridSpec(
            num_scalar_prefetch=1,
            grid=(steps + depth // step,),
            in_specs=[
                pl.BlockSpec((INFO, LANES), lambda i, p: (0, 0)),
                pl.BlockSpec((rows, step), lambda i, p: (0, p[0] * steps + jnp.minimum(i, steps - 1))),
                pl.BlockSpec((rows, step), lambda i, p: (0, jnp.maximum(i - steps, 0))),
            ],
            out_specs=pl.BlockSpec((rows + INFO, step), lambda i, p: (0, i)),
        ),
        out_shape=jax.ShapeDtypeStruct((rows + INFO, half + depth), acts.dtype),
        compiler_params=pltpu.CompilerParams(vmem_limit_bytes=VMEM_BYTES),
        cost_estimate=SMALL,
        name="half",
    )(place, info, acts, grads)


def guarded(pair, mirrored, work):
    if pair in ONLY:
        pl.when(mirrored == ONLY[pair])(work)
    else:
        work()


def grams_kernel(flags, xs, xc, ys, yc, zs, zc, out, held, result, in_sems, out_sems):
    mirrored = flags[0]
    rows, depth = xs.shape
    order = token_major(rows)
    sources = (xs, xc.at[:rows, xc.shape[1] - depth:], ys, yc, zs, zc)
    loads = [
        pltpu.make_async_copy(source, held.at[at], in_sems.at[at])
        for at, source in enumerate(sources)
    ]
    for block in (YS, XS, ZS, XC, YC, ZC):
        loads[block].start()
    here = set()

    def ready(*blocks):
        for block in blocks:
            if block not in here:
                here.add(block)
                loads[block].wait()
                if block in (YS, YC):
                    held[block] = reorder(order, held[block])

    for pair, (one, two, _) in enumerate(PAIRS):
        ready(one, two)
        slot = SLOT[pair]

        def work(one=one, two=two, slot=slot):
            result[slot] = lax.dot_general(
                held[one], held[two], NT, preferred_element_type=jnp.float32
            )
            pltpu.make_async_copy(result.at[slot], out.at[slot], out_sems.at[slot]).start()

        guarded(pair, mirrored, work)
    for slot in range(7):
        pltpu.make_async_copy(result.at[slot], out.at[slot], out_sems.at[slot]).wait()


def grams(flags, grads, *messages):
    rows, width = grads.shape
    return pl.pallas_call(
        grams_kernel,
        in_specs=[pl.BlockSpec(memory_space=pltpu.SMEM)] + [pl.BlockSpec(memory_space=pl.ANY)] * 6,
        out_specs=pl.BlockSpec(memory_space=pl.ANY),
        out_shape=jax.ShapeDtypeStruct((7, rows, rows), jnp.float32),
        scratch_shapes=[
            pltpu.VMEM((6, rows, width), grads.dtype),
            pltpu.VMEM((7, rows, rows), jnp.float32),
            pltpu.SemaphoreType.DMA((6,)),
            pltpu.SemaphoreType.DMA((7,)),
        ],
        compiler_params=pltpu.CompilerParams(vmem_limit_bytes=VMEM_BYTES),
        cost_estimate=SMALL,
        name="grams",
    )(flags, grads, *messages)


def product(one, two, inner):
    rows = inner.shape[0]
    inner[...] = lax.dot_general(
        one[:rows, :], two[:rows, :], NT, preferred_element_type=jnp.float32
    )


def token_sums(inner, gram, sums, ordered=True):
    examples, rows = sums.shape
    if ordered:
        sums[...] = sum(
            inner[at:at + examples, :] * gram[at:at + examples, :]
            for at in range(0, rows, examples)
        )
    else:
        weighted = inner[...] * gram[...]
        sums[...] = weighted.reshape(examples, TOK, rows).sum(axis=1)


def two_parts(value):
    high = value.astype(jnp.bfloat16)
    return high, (value - high.astype(jnp.float32)).astype(jnp.bfloat16)


def dot_parts(value, table):
    high, low = two_parts(value)
    return lax.dot_general(low, table, NT, preferred_element_type=jnp.float32) + lax.dot_general(
        high, table, NT, preferred_element_type=jnp.float32
    )


def side_by_side(values):
    return jnp.concatenate(values, axis=1)


def domain_sums(pairs, factor, place, info, sums):
    count, examples, rows = sums.shape
    example = lax.broadcasted_iota(jnp.int32, (LANES, rows), 0)
    column = lax.broadcasted_iota(jnp.int32, (LANES, rows), 1)
    gather = (lax.shift_right_logical(column, TOK_BITS) == example).astype(jnp.bfloat16)
    tiles = dot_parts(sums[...].reshape(count * examples, rows), gather)
    tiles = tiles.reshape(count, examples, LANES)
    mirrored, core, side = place
    lane = lax.broadcasted_iota(jnp.int32, (1, LANES), 1)
    row = lax.broadcasted_iota(jnp.int32, (DOMAINS, LANES), 0)
    hot = {
        block: ((value.astype(jnp.int32) == row) & (lane < examples)).astype(jnp.bfloat16)
        for block, value in info.items()
    }

    def listed_flag(block, apart):
        return jnp.sum(jnp.where(lane == examples + apart, info[block], 0.0), axis=1, keepdims=True)

    pad = jnp.zeros((LANES - examples, LANES), jnp.float32)
    groups = {}
    for at, pair in pairs:
        one, two, apart = PAIRS[pair]
        if one == XC:
            two_leads = core == 0
        elif two in (XS, XC):
            two_leads = side == 0
        else:
            two_leads = side == 1
        flag = jnp.where(two_leads, listed_flag(two, apart), listed_flag(one, apart))
        if pair in ONLY:
            flag = jnp.where(mirrored == ONLY[pair], flag, 0.0)
        tile = jnp.concatenate([tiles[at], pad], axis=0) * (flag * factor)
        groups.setdefault(one, []).append((two, *two_parts(tile)))
    total = {}

    def add(block, term):
        total[block] = total[block] + term if block in total else term

    for one, group in groups.items():
        others = side_by_side([hot[two] for two, _, _ in group])
        highs = side_by_side([high for _, high, _ in group])
        lows = side_by_side([low for _, _, low in group])
        add(one, lax.dot_general(
            side_by_side([others, others]), side_by_side([highs, lows]), NT,
            preferred_element_type=jnp.float32,
        ))
        columns_of = lax.dot_general(
            side_by_side([hot[one], hot[one]]), jnp.concatenate([highs, lows], axis=0), NN,
            preferred_element_type=jnp.float32,
        )
        for at, (two, _, _) in enumerate(group):
            add(two, columns_of[:, at * LANES:(at + 1) * LANES])
    return total


def copies_of(loads, sems):
    return {
        key: pltpu.make_async_copy(source, target, sems.at[at])
        for at, (key, (source, target)) in enumerate(loads.items())
    }


def start(copies, *keys):
    for key in keys:
        copies[key].start()


def wait(copies, *keys):
    for key in keys:
        copies[key].wait()


def info_row(notes, block):
    return notes[block].astype(jnp.float32)[:1]


def columns(ref, at, width):
    return ref.at[:, pl.ds(pl.multiple_of(at, LANES), width)]


def same_one_kernel(factor, own_info, acts, x_half, ys, zs, gram, out, notes,
                    held, own_v, half_v, gram_v, inner, sums, sems):
    rows, width = inner.shape[1], held.shape[2]
    quarter = acts.shape[1] // 4
    core, side = position()
    mirrored = core ^ side
    in_half = (1 - side) * quarter
    half_at = core * 2 * quarter
    copies = copies_of({
        XS: (columns(acts, half_at + in_half, width), held.at[XS, :rows]),
        XC: (columns(x_half, in_half, width), held.at[XC]),
        YS: (ys, held.at[YS]),
        ZS: (zs, held.at[ZS]),
        "g0": (gram.at[0], gram_v.at[0]),
        "g1": (gram.at[1], gram_v.at[1]),
        "g2": (gram.at[2], gram_v.at[2]),
        "own": (columns(acts, half_at, 2 * quarter), own_v),
        "half": (x_half.at[:, :2 * quarter], half_v),
        "g3": (gram.at[3], gram_v.at[3]),
        "info": (own_info, held.at[XS, rows:, :LANES]),
    }, sems)
    start(copies, YS, XS, "g0", ZS, "info")
    wait(copies, YS, XS, "info")
    start(copies, "g1", XC, "g2")
    product(held.at[YS], held.at[XS], inner.at[0])
    wait(copies, "g0", ZS)
    product(held.at[YS], held.at[ZS], inner.at[1])
    token_sums(inner.at[0], gram_v.at[0], sums.at[0])
    start(copies, "own", "half", "g3")
    wait(copies, "g1", XC, "g2")
    product(held.at[YS], held.at[XC], inner.at[0])
    token_sums(inner.at[1], gram_v.at[1], sums.at[1])
    wait(copies, "own", "half")
    product(half_v, own_v, inner.at[1])
    token_sums(inner.at[0], gram_v.at[2], sums.at[2])
    wait(copies, "g3")
    token_sums(inner.at[1], gram_v.at[3], sums.at[3], ordered=False)
    notes[...] = jnp.zeros_like(notes)
    for block in (XS, XC, YS, ZS):
        notes[block] = held[block, rows:, :LANES]
    info = {block: info_row(notes, block) for block in (XS, XC, YS, ZS)}
    total = domain_sums(tuple(enumerate(FIRST)), factor, (mirrored, core, side), info, sums)
    out[...] = jnp.zeros_like(out)
    for block, value in total.items():
        out[block] = value


def same_two_kernel(factor, at, notes, earlier, acts, x_half, ys, zs, gram, out,
                    held, notes_v, earlier_v, gram_v, inner, sums, sems):
    rows, width = inner.shape[1], held.shape[2]
    quarter = acts.shape[1] // 4
    core, side = position()
    mirrored = core ^ side
    in_half = (1 - side) * quarter
    copies = copies_of({
        XS: (columns(acts, core * 2 * quarter + in_half + at, width), held.at[XS, :rows]),
        XC: (columns(x_half, in_half + at, width), held.at[XC]),
        YS: (ys, held.at[YS, :rows]),
        ZS: (zs, held.at[ZS, :rows]),
        "g0": (gram.at[0], gram_v.at[0]),
        "g1": (gram.at[1], gram_v.at[1]),
        "g2": (gram.at[2], gram_v.at[2]),
        "notes": (notes, notes_v),
        "earlier": (earlier, earlier_v),
    }, sems)
    start(copies, YS, XS, ZS, "g0", "g1", XC, "g2", "notes", "earlier")
    wait(copies, YS, XS)
    product(held.at[YS], held.at[XS], inner.at[0])
    wait(copies, ZS, "g0")
    product(held.at[YS], held.at[ZS], inner.at[1])
    token_sums(inner.at[0], gram_v.at[0], sums.at[0])
    wait(copies, "g1", XC, "g2", "notes", "earlier")
    product(held.at[YS], held.at[XC], inner.at[0])
    token_sums(inner.at[1], gram_v.at[1], sums.at[1])
    token_sums(inner.at[0], gram_v.at[2], sums.at[2])
    info = {block: info_row(notes_v, block) for block in (XS, XC, YS, ZS)}
    pairs = ((0, 0), (1, 1), (2, 2))
    total = domain_sums(pairs, factor, (mirrored, core, side), info, sums)
    out[...] = earlier_v[...]
    for block, value in total.items():
        out[block] = earlier_v[block] + value


def position():
    me = lax.axis_index("ex")
    return me & 1, lax.shift_right_logical(me, 1) & 1


def cross_kernel(factor, at, notes, earlier, *refs):
    (acts, x_half, ys, yc, zs, zc, gram), refs = refs[:7], refs[7:]
    outs, (held, notes_v, earlier_v, gram_v, inner, sums, sems) = refs[:-7], refs[-7:]
    rows, width = inner.shape[1], held.shape[2]
    quarter = acts.shape[1] // 4
    core, side = position()
    mirrored = core ^ side
    in_half = (1 - side) * quarter
    work_at = core * 2 * quarter + in_half
    copies = copies_of({
        XS: (columns(acts, work_at + at, width), held.at[XS, :rows, :]),
        XC: (columns(x_half, in_half + at, width), held.at[XC]),
        YS: (ys, held.at[YS, :ys.shape[0]]),
        YC: (yc, held.at[YC, :yc.shape[0]]),
        ZS: (zs, held.at[ZS, :zs.shape[0]]),
        ZC: (zc, held.at[ZC, :zc.shape[0]]),
        "g4": (gram.at[4], gram_v.at[0]),
        "g5": (gram.at[5], gram_v.at[1]),
        "g6": (gram.at[6], gram_v.at[2]),
        "g2": (gram.at[2], gram_v.at[3]),
        "notes": (notes, notes_v),
        "earlier": (earlier, earlier_v),
    }, sems)
    start(copies, YC, XC, ZC)
    wait(copies, YC, XC)
    start(copies, "g4", YS, ZS)
    product(held.at[YC], held.at[XC], inner.at[0])
    wait(copies, ZC)
    start(copies, "g5", XS)
    product(held.at[YC], held.at[ZC], inner.at[1])
    wait(copies, "g4", YS, ZS)
    start(copies, "g6", "g2", "notes", "earlier")
    token_sums(inner.at[0], gram_v.at[0], sums.at[0])
    product(held.at[jnp.where(mirrored == 0, YC, YS)], held.at[jnp.where(mirrored == 0, ZS, ZC)], inner.at[0])
    wait(copies, "g5", XS)
    token_sums(inner.at[1], gram_v.at[1], sums.at[1])
    wait(copies, "g6", "g2", "notes", "earlier")

    @pl.when(mirrored == 1)
    def _():
        product(held.at[YC], held.at[XS], inner.at[1])
        token_sums(inner.at[0], gram_v.at[2], sums.at[2])
        token_sums(inner.at[1], gram_v.at[3], sums.at[3])

    @pl.when(mirrored == 0)
    def _():
        token_sums(inner.at[0], gram_v.at[2], sums.at[2])
        sums[3] = jnp.zeros(sums.shape[1:], jnp.float32)

    if at == 0:
        total_out, notes_out = outs
        for block in (YC, ZC):
            notes_v[block] = held[block, rows:, :LANES]
        notes_out[...] = notes_v[...]
    info = {block: info_row(notes_v, block) for block in range(6)}
    pairs = ((0, 4), (1, 5), (2, 6), (2, 7), (3, 8))
    total = domain_sums(pairs, factor, (mirrored, core, side), info, sums)
    examples = sums.shape[1]
    for block, value in total.items():
        value = value + earlier_v[block]
        if at == 0:
            total_out[block] = value
        else:
            outs[block][...] = value[:, :examples]


def per_device(acts, grads, domain, listed):
    rows, width = acts.shape
    examples = rows // TOK
    quarter = width // 4
    me = lax.axis_index("ex")
    core = me % 2
    side = (me // 2) % 2
    mirrored = core ^ side

    flags = jnp.stack([mirrored]).astype(jnp.int32)
    places = jnp.stack([core * 2 + side, core * 2 + (1 - side)]).astype(jnp.int32)
    cross_places = jnp.stack([(1 - core) * 2 + side, (1 - core) * 2 + (1 - side)]).astype(jnp.int32)
    half_place = jnp.stack([1 - core]).astype(jnp.int32)

    own_info = jnp.concatenate(
        [domain, listed[0], jnp.zeros((LANES - examples - 2,), jnp.int32)]
    )
    own_info = jnp.broadcast_to(own_info.astype(acts.dtype)[None, :], (INFO, LANES))

    grads_ys = send(grads, across, 0)
    grads_zs = send(grads, along, 0)
    cut_ys, cut_zs, cut_ys_two, cut_zs_two = cut(acts, own_info, places)
    own_info, _ = lax.optimization_barrier((own_info, cut_ys))
    cut_yc, cut_zc, cut_yc_two, cut_zc_two = cut(acts, own_info, cross_places)
    own_info, _ = lax.optimization_barrier((own_info, cut_yc))
    ys_one = send(cut_ys, across, 0)
    zs_one = send(cut_zs, along, 0)
    ys_two = send(cut_ys_two, across, 0)
    zs_two = send(cut_zs_two, along, 0)
    yc_one = send(cut_yc, across, 1)
    zc_one = send(cut_zc, along, 1)
    yc_two = send(cut_yc_two, across, 1)

    def exchange(*values):
        return lax.cond(
            listed[0, 0] < 2,
            lambda *sent: tuple(send(value, stay, 1) for value in sent),
            lambda *sent: tuple(jnp.zeros_like(value) for value in sent),
            *values,
        )

    x_half, = exchange(cut_half(acts, grads, own_info, half_place))
    grads_ys, grads_zs, x_half = lax.optimization_barrier((grads_ys, grads_zs, x_half))
    grads_yc, grads_zc = exchange(grads_ys, grads_zs)
    factor = 1.0 / (TOK * math.sqrt(width * grads.shape[1]))

    grads_yc, ys_one, zs_one = lax.optimization_barrier((grads_yc, ys_one, zs_one))
    gram = grams(flags, grads, x_half, grads_ys, grads_yc, grads_zs, grads_zc)

    vmem = pl.BlockSpec(memory_space=pltpu.VMEM)
    hbm = pl.BlockSpec(memory_space=pl.ANY)
    all_sums = jax.ShapeDtypeStruct((6, DOMAINS, LANES), jnp.float32)
    all_notes = jax.ShapeDtypeStruct((6, INFO, LANES), acts.dtype)
    notes_v = pltpu.VMEM(all_notes.shape, acts.dtype)
    sums_v = pltpu.VMEM(all_sums.shape, jnp.float32)

    def call(kernel, name, vmem_bytes, width, extra, operands, out_shape):
        return pl.pallas_call(
            kernel,
            in_specs=[hbm] * len(operands),
            out_specs=[vmem] * len(out_shape),
            out_shape=out_shape,
            scratch_shapes=[pltpu.VMEM((6, rows + INFO, width), acts.dtype)] + extra + [
                pltpu.VMEM((4, rows, rows), jnp.float32),
                pltpu.VMEM((2, rows, rows), jnp.float32),
                pltpu.VMEM((4, examples, rows), jnp.float32),
                pltpu.SemaphoreType.DMA((12,)),
            ],
            compiler_params=pltpu.CompilerParams(vmem_limit_bytes=vmem_bytes),
            cost_estimate=SMALL,
            name=name,
        )(*operands)

    one, two = chunks(quarter)
    extra = [
        pltpu.VMEM((rows, 2 * quarter), acts.dtype),
        pltpu.VMEM((rows + INFO, 2 * quarter), acts.dtype),
    ]
    partial = functools.partial
    sums, notes = call(
        partial(same_one_kernel, factor), "same_one", VMEM_BYTES, one, extra,
        (own_info, acts, x_half, ys_one, zs_one, gram), [all_sums, all_notes],
    )
    cut_zc_two, sums = lax.optimization_barrier((cut_zc_two, sums))
    zc_two = send(cut_zc_two, along, 1)
    extra = [notes_v, sums_v]
    sums, notes = call(
        partial(cross_kernel, factor, 0), "cross_one", PAIRS_VMEM_BYTES, one, extra,
        (notes, sums, acts, x_half, ys_one, yc_one, zs_one, zc_one, gram), [all_sums, all_notes],
    )
    sums, = call(
        partial(same_two_kernel, factor, one), "same_two", PAIRS_VMEM_BYTES, two, extra,
        (notes, sums, acts, x_half, ys_two, zs_two, gram), [all_sums],
    )
    sums = call(
        partial(cross_kernel, factor, one), "cross_two", PAIRS_VMEM_BYTES, two, extra,
        (notes, sums, acts, x_half, ys_two, yc_two, zs_two, zc_two, gram),
        [jax.ShapeDtypeStruct((DOMAINS, examples), jnp.float32)] * 6,
    )

    total = sums[XS]
    total = total + send(sums[ZS], against, 0)
    total = total + send(sums[ZC], against, 1)
    total = total + send(sums[YS], across, 0)
    total = total + send(sums[YC], across, 1)
    total = total + send(sums[XC], stay, 1)
    return total.T


def solution(mesh):
    in_specs = (
        P(("groups", "ex"), None),
        P(("groups", "ex"), None),
        P(("groups", "ex")),
        P(("groups", "ex"), None),
    )
    out_specs = P(("groups", "ex"), None)
    return jax.shard_map(
        per_device, mesh=mesh, in_specs=in_specs, out_specs=out_specs, check_vma=False
    )
```

```python
import functools
import math

import jax
import jax.numpy as jnp
from jax import lax
from jax.experimental import pallas as pl
from jax.experimental.pallas import tpu as pltpu
from jax.sharding import PartitionSpec as P

TOK = 8
TOK_BITS = 3
DOMAINS = 48
LANES = 128
VMEM_BYTES = 63 * 1024 * 1024
PAIRS_VMEM_BYTES = 44 * 1024 * 1024

INFO = 16

XS, XC, YS, YC, ZS, ZC = range(6)
PAIRS = (
    (YS, XS, 1), (YS, ZS, 1), (YS, XC, 0), (XC, XS, 0),
    (YC, XC, 1), (YC, ZC, 1), (YC, ZS, 0), (YS, ZC, 0), (YC, XS, 0),
)
ONLY = {2: 0, 6: 0, 7: 1, 8: 1}
SLOT = (0, 1, 2, 3, 4, 5, 6, 6, 2)
FIRST = (0, 1, 2, 3)
SMALL = pl.CostEstimate(flops=1, bytes_accessed=1, transcendentals=0)
NT = (((1,), (1,)), ((), ()))
NN = (((1,), (0,)), ((), ()))


def across(chip):
    return chip ^ 1


def along(chip):
    return chip + 2 if chip & 1 else chip - 2


def against(chip):
    return chip - 2 if chip & 1 else chip + 2


def stay(chip):
    return chip


def send(value, move, flip):
    chips = lax.axis_size("ex") // 2
    pairs = [
        (2 * chip + core, 2 * (move(chip) % chips) + (core ^ flip))
        for chip in range(chips)
        for core in range(2)
    ]
    return lax.ppermute(value, "ex", pairs)


def token_major(rows):
    to = lax.broadcasted_iota(jnp.int32, (rows, rows), 0)
    source = lax.broadcasted_iota(jnp.int32, (rows, rows), 1)
    examples = rows // TOK
    place = (source & (TOK - 1)) * examples + lax.shift_right_logical(source, TOK_BITS)
    return (place == to).astype(jnp.bfloat16)


def reorder(order, block):
    return jnp.dot(order, block, preferred_element_type=jnp.float32).astype(jnp.bfloat16)


def put(target, value, info):
    rows = value.shape[0]
    target[:rows, :] = value
    target[rows:, :] = jnp.concatenate([info[...]] * (target.shape[1] // LANES), axis=1)


def chunks(quarter):
    second = quarter // LANES * 3 // 10 * LANES
    return quarter - second, second


def cut_kernel(places, info, y_acts, z_acts, y_one, z_one, y_two, z_two, order):
    rows, split = order.shape[0], y_one.shape[1]
    order[...] = token_major(rows)
    put(y_one, reorder(order[...], y_acts[:, :split]), info)
    put(z_one, z_acts[:, :split], info)
    y_two[...] = reorder(order[...], y_acts[:, split:])
    z_two[...] = z_acts[:, split:]


def cut(acts, info, places):
    rows, width = acts.shape
    quarter = width // 4
    one, two = chunks(quarter)
    shapes = [(rows + INFO, one)] * 2 + [(rows, two)] * 2
    return pl.pallas_call(
        cut_kernel,
        grid_spec=pltpu.PrefetchScalarGridSpec(
            num_scalar_prefetch=1,
            grid=(1,),
            in_specs=[
                pl.BlockSpec((INFO, LANES), lambda i, p: (0, 0)),
                pl.BlockSpec((rows, quarter), lambda i, p: (0, p[0])),
                pl.BlockSpec((rows, quarter), lambda i, p: (0, p[1])),
            ],
            out_specs=[pl.BlockSpec(shape, lambda i, p: (0, 0)) for shape in shapes],
            scratch_shapes=[pltpu.VMEM((rows, rows), jnp.bfloat16)],
        ),
        out_shape=[jax.ShapeDtypeStruct(shape, acts.dtype) for shape in shapes],
        compiler_params=pltpu.CompilerParams(vmem_limit_bytes=VMEM_BYTES),
        cost_estimate=SMALL,
        name="cut",
    )(places, info, acts, acts)


def half_kernel(steps, place, info, acts, grads, out):
    @pl.when(pl.program_id(0) < steps)
    def _():
        put(out, acts[...], info)

    @pl.when(pl.program_id(0) >= steps)
    def _():
        put(out, grads[...], info)


def cut_half(acts, grads, info, place):
    rows, width = acts.shape
    half, depth = width // 2, grads.shape[1]
    step = math.gcd(math.gcd(half, depth), 512)
    steps = half // step
    return pl.pallas_call(
        functools.partial(half_kernel, steps),
        grid_spec=pltpu.PrefetchScalarGridSpec(
            num_scalar_prefetch=1,
            grid=(steps + depth // step,),
            in_specs=[
                pl.BlockSpec((INFO, LANES), lambda i, p: (0, 0)),
                pl.BlockSpec((rows, step), lambda i, p: (0, p[0] * steps + jnp.minimum(i, steps - 1))),
                pl.BlockSpec((rows, step), lambda i, p: (0, jnp.maximum(i - steps, 0))),
            ],
            out_specs=pl.BlockSpec((rows + INFO, step), lambda i, p: (0, i)),
        ),
        out_shape=jax.ShapeDtypeStruct((rows + INFO, half + depth), acts.dtype),
        compiler_params=pltpu.CompilerParams(vmem_limit_bytes=VMEM_BYTES),
        cost_estimate=SMALL,
        name="half",
    )(place, info, acts, grads)


def guarded(pair, mirrored, work):
    if pair in ONLY:
        pl.when(mirrored == ONLY[pair])(work)
    else:
        work()


def grams_kernel(flags, xs, xc, ys, yc, zs, zc, out, held, result, in_sems, out_sems):
    mirrored = flags[0]
    rows, depth = xs.shape
    order = token_major(rows)
    sources = (xs, xc.at[:rows, xc.shape[1] - depth:], ys, yc, zs, zc)
    loads = [
        pltpu.make_async_copy(source, held.at[at], in_sems.at[at])
        for at, source in enumerate(sources)
    ]
    for block in (YS, XS, ZS, XC, YC, ZC):
        loads[block].start()
    here = set()

    def ready(*blocks):
        for block in blocks:
            if block not in here:
                here.add(block)
                loads[block].wait()
                if block in (YS, YC):
                    held[block] = reorder(order, held[block])

    for pair, (one, two, _) in enumerate(PAIRS):
        ready(one, two)
        slot = SLOT[pair]

        def work(one=one, two=two, slot=slot):
            result[slot] = lax.dot_general(
                held[one], held[two], NT, preferred_element_type=jnp.float32
            )
            pltpu.make_async_copy(result.at[slot], out.at[slot], out_sems.at[slot]).start()

        guarded(pair, mirrored, work)
    for slot in range(7):
        pltpu.make_async_copy(result.at[slot], out.at[slot], out_sems.at[slot]).wait()


def grams(flags, grads, *messages):
    rows, width = grads.shape
    return pl.pallas_call(
        grams_kernel,
        in_specs=[pl.BlockSpec(memory_space=pltpu.SMEM)] + [pl.BlockSpec(memory_space=pl.ANY)] * 6,
        out_specs=pl.BlockSpec(memory_space=pl.ANY),
        out_shape=jax.ShapeDtypeStruct((7, rows, rows), jnp.float32),
        scratch_shapes=[
            pltpu.VMEM((6, rows, width), grads.dtype),
            pltpu.VMEM((7, rows, rows), jnp.float32),
            pltpu.SemaphoreType.DMA((6,)),
            pltpu.SemaphoreType.DMA((7,)),
        ],
        compiler_params=pltpu.CompilerParams(vmem_limit_bytes=VMEM_BYTES),
        cost_estimate=SMALL,
        name="grams",
    )(flags, grads, *messages)


def product(one, two, inner):
    rows = inner.shape[0]
    inner[...] = lax.dot_general(
        one[:rows, :], two[:rows, :], NT, preferred_element_type=jnp.float32
    )


def token_sums(inner, gram, sums, ordered=True):
    examples, rows = sums.shape
    if ordered:
        sums[...] = sum(
            inner[at:at + examples, :] * gram[at:at + examples, :]
            for at in range(0, rows, examples)
        )
    else:
        weighted = inner[...] * gram[...]
        sums[...] = weighted.reshape(examples, TOK, rows).sum(axis=1)


def two_parts(value):
    high = value.astype(jnp.bfloat16)
    return high, (value - high.astype(jnp.float32)).astype(jnp.bfloat16)


def dot_parts(value, table):
    high, low = two_parts(value)
    return lax.dot_general(low, table, NT, preferred_element_type=jnp.float32) + lax.dot_general(
        high, table, NT, preferred_element_type=jnp.float32
    )


def side_by_side(values):
    return jnp.concatenate(values, axis=1)


def domain_sums(pairs, factor, place, info, sums):
    count, examples, rows = sums.shape
    example = lax.broadcasted_iota(jnp.int32, (LANES, rows), 0)
    column = lax.broadcasted_iota(jnp.int32, (LANES, rows), 1)
    gather = (lax.shift_right_logical(column, TOK_BITS) == example).astype(jnp.bfloat16)
    tiles = dot_parts(sums[...].reshape(count * examples, rows), gather)
    tiles = tiles.reshape(count, examples, LANES)
    mirrored, core, side = place
    lane = lax.broadcasted_iota(jnp.int32, (1, LANES), 1)
    row = lax.broadcasted_iota(jnp.int32, (DOMAINS, LANES), 0)
    hot = {
        block: ((value.astype(jnp.int32) == row) & (lane < examples)).astype(jnp.bfloat16)
        for block, value in info.items()
    }

    def listed_flag(block, apart):
        return jnp.sum(jnp.where(lane == examples + apart, info[block], 0.0), axis=1, keepdims=True)

    pad = jnp.zeros((LANES - examples, LANES), jnp.float32)
    groups = {}
    for at, pair in pairs:
        one, two, apart = PAIRS[pair]
        if one == XC:
            two_leads = core == 0
        elif two in (XS, XC):
            two_leads = side == 0
        else:
            two_leads = side == 1
        flag = jnp.where(two_leads, listed_flag(two, apart), listed_flag(one, apart))
        if pair in ONLY:
            flag = jnp.where(mirrored == ONLY[pair], flag, 0.0)
        tile = jnp.concatenate([tiles[at], pad], axis=0) * (flag * factor)
        groups.setdefault(one, []).append((two, *two_parts(tile)))
    total = {}

    def add(block, term):
        total[block] = total[block] + term if block in total else term

    for one, group in groups.items():
        others = side_by_side([hot[two] for two, _, _ in group])
        highs = side_by_side([high for _, high, _ in group])
        lows = side_by_side([low for _, _, low in group])
        add(one, lax.dot_general(
            side_by_side([others, others]), side_by_side([highs, lows]), NT,
            preferred_element_type=jnp.float32,
        ))
        columns_of = lax.dot_general(
            side_by_side([hot[one], hot[one]]), jnp.concatenate([highs, lows], axis=0), NN,
            preferred_element_type=jnp.float32,
        )
        for at, (two, _, _) in enumerate(group):
            add(two, columns_of[:, at * LANES:(at + 1) * LANES])
    return total


def copies_of(loads, sems):
    return {
        key: pltpu.make_async_copy(source, target, sems.at[at])
        for at, (key, (source, target)) in enumerate(loads.items())
    }


def start(copies, *keys):
    for key in keys:
        copies[key].start()


def wait(copies, *keys):
    for key in keys:
        copies[key].wait()


def info_row(notes, block):
    return notes[block].astype(jnp.float32)[:1]


def columns(ref, at, width):
    return ref.at[:, pl.ds(pl.multiple_of(at, LANES), width)]


def same_one_kernel(factor, own_info, acts, x_half, ys, zs, gram, out, notes,
                    held, own_v, half_v, gram_v, inner, sums, sems):
    rows, width = inner.shape[1], held.shape[2]
    quarter = acts.shape[1] // 4
    core, side = position()
    mirrored = core ^ side
    in_half = (1 - side) * quarter
    half_at = core * 2 * quarter
    copies = copies_of({
        XS: (columns(acts, half_at + in_half, width), held.at[XS, :rows]),
        XC: (columns(x_half, in_half, width), held.at[XC]),
        YS: (ys, held.at[YS]),
        ZS: (zs, held.at[ZS]),
        "g0": (gram.at[0], gram_v.at[0]),
        "g1": (gram.at[1], gram_v.at[1]),
        "g2": (gram.at[2], gram_v.at[2]),
        "own": (columns(acts, half_at, 2 * quarter), own_v),
        "half": (x_half.at[:, :2 * quarter], half_v),
        "g3": (gram.at[3], gram_v.at[3]),
        "info": (own_info, held.at[XS, rows:, :LANES]),
    }, sems)
    start(copies, YS, XS, "g0", ZS, "info")
    wait(copies, YS, XS, "info")
    start(copies, "g1", XC, "g2")
    product(held.at[YS], held.at[XS], inner.at[0])
    wait(copies, "g0", ZS)
    product(held.at[YS], held.at[ZS], inner.at[1])
    token_sums(inner.at[0], gram_v.at[0], sums.at[0])
    start(copies, "own", "half", "g3")
    wait(copies, "g1", XC, "g2")
    product(held.at[YS], held.at[XC], inner.at[0])
    token_sums(inner.at[1], gram_v.at[1], sums.at[1])
    wait(copies, "own", "half")
    product(half_v, own_v, inner.at[1])
    token_sums(inner.at[0], gram_v.at[2], sums.at[2])
    wait(copies, "g3")
    token_sums(inner.at[1], gram_v.at[3], sums.at[3], ordered=False)
    notes[...] = jnp.zeros_like(notes)
    for block in (XS, XC, YS, ZS):
        notes[block] = held[block, rows:, :LANES]
    info = {block: info_row(notes, block) for block in (XS, XC, YS, ZS)}
    total = domain_sums(tuple(enumerate(FIRST)), factor, (mirrored, core, side), info, sums)
    out[...] = jnp.zeros_like(out)
    for block, value in total.items():
        out[block] = value


def same_two_kernel(factor, at, notes, earlier, acts, x_half, ys, zs, gram, out,
                    held, notes_v, earlier_v, gram_v, inner, sums, sems):
    rows, width = inner.shape[1], held.shape[2]
    quarter = acts.shape[1] // 4
    core, side = position()
    mirrored = core ^ side
    in_half = (1 - side) * quarter
    copies = copies_of({
        XS: (columns(acts, core * 2 * quarter + in_half + at, width), held.at[XS, :rows]),
        XC: (columns(x_half, in_half + at, width), held.at[XC]),
        YS: (ys, held.at[YS, :rows]),
        ZS: (zs, held.at[ZS, :rows]),
        "g0": (gram.at[0], gram_v.at[0]),
        "g1": (gram.at[1], gram_v.at[1]),
        "g2": (gram.at[2], gram_v.at[2]),
        "notes": (notes, notes_v),
        "earlier": (earlier, earlier_v),
    }, sems)
    start(copies, YS, XS, ZS, "g0", "g1", XC, "g2", "notes", "earlier")
    wait(copies, YS, XS)
    product(held.at[YS], held.at[XS], inner.at[0])
    wait(copies, ZS, "g0")
    product(held.at[YS], held.at[ZS], inner.at[1])
    token_sums(inner.at[0], gram_v.at[0], sums.at[0])
    wait(copies, "g1", XC, "g2", "notes", "earlier")
    product(held.at[YS], held.at[XC], inner.at[0])
    token_sums(inner.at[1], gram_v.at[1], sums.at[1])
    token_sums(inner.at[0], gram_v.at[2], sums.at[2])
    info = {block: info_row(notes_v, block) for block in (XS, XC, YS, ZS)}
    pairs = ((0, 0), (1, 1), (2, 2))
    total = domain_sums(pairs, factor, (mirrored, core, side), info, sums)
    out[...] = earlier_v[...]
    for block, value in total.items():
        out[block] = earlier_v[block] + value


def position():
    me = lax.axis_index("ex")
    return me & 1, lax.shift_right_logical(me, 1) & 1


def cross_kernel(factor, at, notes, earlier, *refs):
    (acts, x_half, ys, yc, zs, zc, gram), refs = refs[:7], refs[7:]
    outs, (held, notes_v, earlier_v, gram_v, inner, sums, sems) = refs[:-7], refs[-7:]
    rows, width = inner.shape[1], held.shape[2]
    quarter = acts.shape[1] // 4
    core, side = position()
    mirrored = core ^ side
    in_half = (1 - side) * quarter
    work_at = core * 2 * quarter + in_half
    copies = copies_of({
        XS: (columns(acts, work_at + at, width), held.at[XS, :rows, :]),
        XC: (columns(x_half, in_half + at, width), held.at[XC]),
        YS: (ys, held.at[YS, :ys.shape[0]]),
        YC: (yc, held.at[YC, :yc.shape[0]]),
        ZS: (zs, held.at[ZS, :zs.shape[0]]),
        ZC: (zc, held.at[ZC, :zc.shape[0]]),
        "g4": (gram.at[4], gram_v.at[0]),
        "g5": (gram.at[5], gram_v.at[1]),
        "g6": (gram.at[6], gram_v.at[2]),
        "g2": (gram.at[2], gram_v.at[3]),
        "notes": (notes, notes_v),
        "earlier": (earlier, earlier_v),
    }, sems)
    start(copies, YC, XC, ZC)
    wait(copies, YC, XC)
    start(copies, "g4", YS, ZS)
    product(held.at[YC], held.at[XC], inner.at[0])
    wait(copies, ZC)
    start(copies, "g5", XS)
    product(held.at[YC], held.at[ZC], inner.at[1])
    wait(copies, "g4", YS, ZS)
    start(copies, "g6", "g2", "notes", "earlier")
    token_sums(inner.at[0], gram_v.at[0], sums.at[0])
    product(held.at[jnp.where(mirrored == 0, YC, YS)], held.at[jnp.where(mirrored == 0, ZS, ZC)], inner.at[0])
    wait(copies, "g5", XS)
    token_sums(inner.at[1], gram_v.at[1], sums.at[1])
    wait(copies, "g6", "g2", "notes", "earlier")

    @pl.when(mirrored == 1)
    def _():
        product(held.at[YC], held.at[XS], inner.at[1])
        token_sums(inner.at[0], gram_v.at[2], sums.at[2])
        token_sums(inner.at[1], gram_v.at[3], sums.at[3])

    @pl.when(mirrored == 0)
    def _():
        token_sums(inner.at[0], gram_v.at[2], sums.at[2])
        sums[3] = jnp.zeros(sums.shape[1:], jnp.float32)

    if at == 0:
        total_out, notes_out = outs
        for block in (YC, ZC):
            notes_v[block] = held[block, rows:, :LANES]
        notes_out[...] = notes_v[...]
    info = {block: info_row(notes_v, block) for block in range(6)}
    pairs = ((0, 4), (1, 5), (2, 6), (2, 7), (3, 8))
    total = domain_sums(pairs, factor, (mirrored, core, side), info, sums)
    examples = sums.shape[1]
    for block, value in total.items():
        value = value + earlier_v[block]
        if at == 0:
            total_out[block] = value
        else:
            outs[block][...] = value[:, :examples]


def per_device(acts, grads, domain, listed):
    rows, width = acts.shape
    examples = rows // TOK
    quarter = width // 4
    me = lax.axis_index("ex")
    core = me % 2
    side = (me // 2) % 2
    mirrored = core ^ side

    flags = jnp.stack([mirrored]).astype(jnp.int32)
    places = jnp.stack([core * 2 + side, core * 2 + (1 - side)]).astype(jnp.int32)
    cross_places = jnp.stack([(1 - core) * 2 + side, (1 - core) * 2 + (1 - side)]).astype(jnp.int32)
    half_place = jnp.stack([1 - core]).astype(jnp.int32)

    own_info = jnp.concatenate(
        [domain, listed[0], jnp.zeros((LANES - examples - 2,), jnp.int32)]
    )
    own_info = jnp.broadcast_to(own_info.astype(acts.dtype)[None, :], (INFO, LANES))

    grads_ys = send(grads, across, 0)
    grads_zs = send(grads, along, 0)
    cut_ys, cut_zs, cut_ys_two, cut_zs_two = cut(acts, own_info, places)
    own_info, _ = lax.optimization_barrier((own_info, cut_ys))
    cut_yc, cut_zc, cut_yc_two, cut_zc_two = cut(acts, own_info, cross_places)
    own_info, _ = lax.optimization_barrier((own_info, cut_yc))
    ys_one = send(cut_ys, across, 0)
    zs_one = send(cut_zs, along, 0)
    ys_two = send(cut_ys_two, across, 0)
    yc_one = send(cut_yc, across, 1)
    zc_one = send(cut_zc, along, 1)

    def exchange(*values):
        return lax.cond(
            listed[0, 0] < 2,
            lambda *sent: tuple(send(value, stay, 1) for value in sent),
            lambda *sent: tuple(jnp.zeros_like(value) for value in sent),
            *values,
        )

    x_half, = exchange(cut_half(acts, grads, own_info, half_place))
    grads_ys, grads_zs, x_half = lax.optimization_barrier((grads_ys, grads_zs, x_half))
    grads_yc, grads_zc = exchange(grads_ys, grads_zs)
    factor = 1.0 / (TOK * math.sqrt(width * grads.shape[1]))

    gram = grams(flags, grads, x_half, grads_ys, grads_yc, grads_zs, grads_zc)
    cut_zs_two, cut_yc_two, gram = lax.optimization_barrier((cut_zs_two, cut_yc_two, gram))
    zs_two = send(cut_zs_two, along, 0)
    yc_two = send(cut_yc_two, across, 1)

    vmem = pl.BlockSpec(memory_space=pltpu.VMEM)
    hbm = pl.BlockSpec(memory_space=pl.ANY)
    all_sums = jax.ShapeDtypeStruct((6, DOMAINS, LANES), jnp.float32)
    all_notes = jax.ShapeDtypeStruct((6, INFO, LANES), acts.dtype)
    notes_v = pltpu.VMEM(all_notes.shape, acts.dtype)
    sums_v = pltpu.VMEM(all_sums.shape, jnp.float32)

    def call(kernel, name, vmem_bytes, width, extra, operands, out_shape):
        return pl.pallas_call(
            kernel,
            in_specs=[hbm] * len(operands),
            out_specs=[vmem] * len(out_shape),
            out_shape=out_shape,
            scratch_shapes=[pltpu.VMEM((6, rows + INFO, width), acts.dtype)] + extra + [
                pltpu.VMEM((4, rows, rows), jnp.float32),
                pltpu.VMEM((2, rows, rows), jnp.float32),
                pltpu.VMEM((4, examples, rows), jnp.float32),
                pltpu.SemaphoreType.DMA((12,)),
            ],
            compiler_params=pltpu.CompilerParams(vmem_limit_bytes=vmem_bytes),
            cost_estimate=SMALL,
            name=name,
        )(*operands)

    one, two = chunks(quarter)
    extra = [
        pltpu.VMEM((rows, 2 * quarter), acts.dtype),
        pltpu.VMEM((rows + INFO, 2 * quarter), acts.dtype),
    ]
    partial = functools.partial
    sums, notes = call(
        partial(same_one_kernel, factor), "same_one", VMEM_BYTES, one, extra,
        (own_info, acts, x_half, ys_one, zs_one, gram), [all_sums, all_notes],
    )
    cut_zc_two, sums = lax.optimization_barrier((cut_zc_two, sums))
    zc_two = send(cut_zc_two, along, 1)
    extra = [notes_v, sums_v]
    sums, notes = call(
        partial(cross_kernel, factor, 0), "cross_one", PAIRS_VMEM_BYTES, one, extra,
        (notes, sums, acts, x_half, ys_one, yc_one, zs_one, zc_one, gram), [all_sums, all_notes],
    )
    sums, = call(
        partial(same_two_kernel, factor, one), "same_two", PAIRS_VMEM_BYTES, two, extra,
        (notes, sums, acts, x_half, ys_two, zs_two, gram), [all_sums],
    )
    sums = call(
        partial(cross_kernel, factor, one), "cross_two", PAIRS_VMEM_BYTES, two, extra,
        (notes, sums, acts, x_half, ys_two, yc_two, zs_two, zc_two, gram),
        [jax.ShapeDtypeStruct((DOMAINS, examples), jnp.float32)] * 6,
    )

    total = sums[XS]
    total = total + send(sums[ZS], against, 0)
    total = total + send(sums[ZC], against, 1)
    total = total + send(sums[YS], across, 0)
    total = total + send(sums[YC], across, 1)
    total = total + send(sums[XC], stay, 1)
    return total.T


def solution(mesh):
    in_specs = (
        P(("groups", "ex"), None),
        P(("groups", "ex"), None),
        P(("groups", "ex")),
        P(("groups", "ex"), None),
    )
    out_specs = P(("groups", "ex"), None)
    return jax.shard_map(
        per_device, mesh=mesh, in_specs=in_specs, out_specs=out_specs, check_vma=False
    )
```

```python
import functools
import math

import jax
import jax.numpy as jnp
from jax import lax
from jax.experimental import pallas as pl
from jax.experimental.pallas import tpu as pltpu
from jax.sharding import PartitionSpec as P

TOK = 8
TOK_BITS = 3
DOMAINS = 48
LANES = 128
VMEM_BYTES = 63 * 1024 * 1024
PAIRS_VMEM_BYTES = 44 * 1024 * 1024

INFO = 16

XS, XC, YS, YC, ZS, ZC = range(6)
PAIRS = (
    (YS, XS, 1), (YS, ZS, 1), (YS, XC, 0), (XC, XS, 0),
    (YC, XC, 1), (YC, ZC, 1), (YC, ZS, 0), (YS, ZC, 0), (YC, XS, 0),
)
ONLY = {2: 0, 6: 0, 7: 1, 8: 1}
SLOT = (0, 1, 2, 3, 4, 5, 6, 6, 2)
SLOTS = 7
FIRST = (0, 1, 2, 3)
SMALL = pl.CostEstimate(flops=1, bytes_accessed=1, transcendentals=0)
NT = (((1,), (1,)), ((), ()))
NN = (((1,), (0,)), ((), ()))


def across(chip):
    return chip ^ 1


def along(chip):
    return chip + 2 if chip & 1 else chip - 2


def against(chip):
    return chip - 2 if chip & 1 else chip + 2


def stay(chip):
    return chip


def send(value, move, flip):
    chips = lax.axis_size("ex") // 2
    pairs = [
        (2 * chip + core, 2 * (move(chip) % chips) + (core ^ flip))
        for chip in range(chips)
        for core in range(2)
    ]
    return lax.ppermute(value, "ex", pairs)


def token_major(rows):
    to = lax.broadcasted_iota(jnp.int32, (rows, rows), 0)
    source = lax.broadcasted_iota(jnp.int32, (rows, rows), 1)
    examples = rows // TOK
    place = (source & (TOK - 1)) * examples + lax.shift_right_logical(source, TOK_BITS)
    return (place == to).astype(jnp.bfloat16)


def reorder(order, block):
    return jnp.dot(order, block, preferred_element_type=jnp.float32).astype(jnp.bfloat16)


def put(target, value, info):
    rows = value.shape[0]
    target[:rows, :] = value
    target[rows:, :] = jnp.concatenate([info[...]] * (target.shape[1] // LANES), axis=1)


def chunks(quarter):
    second = quarter // LANES // 5 * LANES
    return quarter - second, second


def cut_kernel(places, info, y_acts, z_acts, y_one, z_one, y_two, z_two, order):
    rows, split = order.shape[0], y_one.shape[1]
    order[...] = token_major(rows)
    put(y_one, reorder(order[...], y_acts[:, :split]), info)
    put(z_one, z_acts[:, :split], info)
    y_two[...] = reorder(order[...], y_acts[:, split:])
    z_two[...] = z_acts[:, split:]


def cut(acts, info, places):
    rows, width = acts.shape
    quarter = width // 4
    one, two = chunks(quarter)
    shapes = [(rows + INFO, one)] * 2 + [(rows, two)] * 2
    return pl.pallas_call(
        cut_kernel,
        grid_spec=pltpu.PrefetchScalarGridSpec(
            num_scalar_prefetch=1,
            grid=(1,),
            in_specs=[
                pl.BlockSpec((INFO, LANES), lambda i, p: (0, 0)),
                pl.BlockSpec((rows, quarter), lambda i, p: (0, p[0])),
                pl.BlockSpec((rows, quarter), lambda i, p: (0, p[1])),
            ],
            out_specs=[pl.BlockSpec(shape, lambda i, p: (0, 0)) for shape in shapes],
            scratch_shapes=[pltpu.VMEM((rows, rows), jnp.bfloat16)],
        ),
        out_shape=[jax.ShapeDtypeStruct(shape, acts.dtype) for shape in shapes],
        compiler_params=pltpu.CompilerParams(vmem_limit_bytes=VMEM_BYTES),
        cost_estimate=SMALL,
        name="cut",
    )(places, info, acts, acts)


def half_kernel(steps, place, info, acts, grads, out):
    @pl.when(pl.program_id(0) < steps)
    def _():
        put(out, acts[...], info)

    @pl.when(pl.program_id(0) >= steps)
    def _():
        put(out, grads[...], info)


def cut_half(acts, grads, info, place):
    rows, width = acts.shape
    half, depth = width // 2, grads.shape[1]
    step = math.gcd(math.gcd(half, depth), 512)
    steps = half // step
    return pl.pallas_call(
        functools.partial(half_kernel, steps),
        grid_spec=pltpu.PrefetchScalarGridSpec(
            num_scalar_prefetch=1,
            grid=(steps + depth // step,),
            in_specs=[
                pl.BlockSpec((INFO, LANES), lambda i, p: (0, 0)),
                pl.BlockSpec((rows, step), lambda i, p: (0, p[0] * steps + jnp.minimum(i, steps - 1))),
                pl.BlockSpec((rows, step), lambda i, p: (0, jnp.maximum(i - steps, 0))),
            ],
            out_specs=pl.BlockSpec((rows + INFO, step), lambda i, p: (0, i)),
        ),
        out_shape=jax.ShapeDtypeStruct((rows + INFO, half + depth), acts.dtype),
        compiler_params=pltpu.CompilerParams(vmem_limit_bytes=VMEM_BYTES),
        cost_estimate=SMALL,
        name="half",
    )(place, info, acts, grads)


def grams_kernel(table, xs, xc, ys, yc, zs, zc, out, held, result, in_sems, out_sems):
    rows, depth = xs.shape
    order = token_major(rows)
    sources = (xs, xc.at[:rows, xc.shape[1] - depth:], ys, yc, zs, zc)
    loads = [
        pltpu.make_async_copy(source, held.at[at], in_sems.at[at])
        for at, source in enumerate(sources)
    ]
    for load in loads:
        load.start()
    for load in loads:
        load.wait()
    for block in (YS, YC):
        held[block] = reorder(order, held[block])

    def leave(slot):
        return pltpu.make_async_copy(result.at[slot], out.at[slot], out_sems.at[slot])

    @pl.loop(0, SLOTS)
    def _(slot):
        result[slot] = lax.dot_general(
            held[table[slot]], held[table[SLOTS + slot]], NT, preferred_element_type=jnp.float32
        )
        leave(slot).start()

    for slot in range(SLOTS):
        leave(slot).wait()


def grams(table, grads, *messages):
    rows, width = grads.shape
    return pl.pallas_call(
        grams_kernel,
        in_specs=[pl.BlockSpec(memory_space=pltpu.SMEM)] + [pl.BlockSpec(memory_space=pl.ANY)] * 6,
        out_specs=pl.BlockSpec(memory_space=pl.ANY),
        out_shape=jax.ShapeDtypeStruct((SLOTS, rows, rows), jnp.float32),
        scratch_shapes=[
            pltpu.VMEM((6, rows, width), grads.dtype),
            pltpu.VMEM((SLOTS, rows, rows), jnp.float32),
            pltpu.SemaphoreType.DMA((6,)),
            pltpu.SemaphoreType.DMA((SLOTS,)),
        ],
        compiler_params=pltpu.CompilerParams(vmem_limit_bytes=VMEM_BYTES),
        cost_estimate=SMALL,
        name="grams",
    )(table, grads, *messages)


def product(one, two, inner):
    rows = inner.shape[0]
    inner[...] = lax.dot_general(
        one[:rows, :], two[:rows, :], NT, preferred_element_type=jnp.float32
    )


def token_sums(inner, gram, sums, ordered=True):
    examples, rows = sums.shape
    if ordered:
        sums[...] = sum(
            inner[at:at + examples, :] * gram[at:at + examples, :]
            for at in range(0, rows, examples)
        )
    else:
        weighted = inner[...] * gram[...]
        sums[...] = weighted.reshape(examples, TOK, rows).sum(axis=1)


def two_parts(value):
    high = value.astype(jnp.bfloat16)
    return high, (value - high.astype(jnp.float32)).astype(jnp.bfloat16)


def dot_parts(value, table):
    high, low = two_parts(value)
    return lax.dot_general(low, table, NT, preferred_element_type=jnp.float32) + lax.dot_general(
        high, table, NT, preferred_element_type=jnp.float32
    )


def side_by_side(values):
    return jnp.concatenate(values, axis=1)


def domain_sums(pairs, factor, place, info, sums):
    count, examples, rows = sums.shape
    example = lax.broadcasted_iota(jnp.int32, (LANES, rows), 0)
    column = lax.broadcasted_iota(jnp.int32, (LANES, rows), 1)
    gather = (lax.shift_right_logical(column, TOK_BITS) == example).astype(jnp.bfloat16)
    tiles = dot_parts(sums[...].reshape(count * examples, rows), gather)
    tiles = tiles.reshape(count, examples, LANES)
    mirrored, core, side = place
    lane = lax.broadcasted_iota(jnp.int32, (1, LANES), 1)
    row = lax.broadcasted_iota(jnp.int32, (DOMAINS, LANES), 0)
    hot = {
        block: ((value.astype(jnp.int32) == row) & (lane < examples)).astype(jnp.bfloat16)
        for block, value in info.items()
    }

    def listed_flag(block, apart):
        return jnp.sum(jnp.where(lane == examples + apart, info[block], 0.0), axis=1, keepdims=True)

    pad = jnp.zeros((LANES - examples, LANES), jnp.float32)
    groups = {}
    for at, pair in pairs:
        one, two, apart = PAIRS[pair]
        if one == XC:
            two_leads = core == 0
        elif two in (XS, XC):
            two_leads = side == 0
        else:
            two_leads = side == 1
        flag = jnp.where(two_leads, listed_flag(two, apart), listed_flag(one, apart))
        if pair in ONLY:
            flag = jnp.where(mirrored == ONLY[pair], flag, 0.0)
        tile = jnp.concatenate([tiles[at], pad], axis=0) * (flag * factor)
        groups.setdefault(one, []).append((two, *two_parts(tile)))
    total = {}

    def add(block, term):
        total[block] = total[block] + term if block in total else term

    for one, group in groups.items():
        others = side_by_side([hot[two] for two, _, _ in group])
        highs = side_by_side([high for _, high, _ in group])
        lows = side_by_side([low for _, _, low in group])
        add(one, lax.dot_general(
            side_by_side([others, others]), side_by_side([highs, lows]), NT,
            preferred_element_type=jnp.float32,
        ))
        columns_of = lax.dot_general(
            side_by_side([hot[one], hot[one]]), jnp.concatenate([highs, lows], axis=0), NN,
            preferred_element_type=jnp.float32,
        )
        for at, (two, _, _) in enumerate(group):
            add(two, columns_of[:, at * LANES:(at + 1) * LANES])
    return total


def copies_of(loads, sems):
    return {
        key: pltpu.make_async_copy(source, target, sems.at[at])
        for at, (key, (source, target)) in enumerate(loads.items())
    }


def start(copies, *keys):
    for key in keys:
        copies[key].start()


def wait(copies, *keys):
    for key in keys:
        copies[key].wait()


def info_row(notes, block):
    return notes[block].astype(jnp.float32)[:1]


def columns(ref, at, width):
    return ref.at[:, pl.ds(pl.multiple_of(at, LANES), width)]


def same_one_kernel(factor, own_info, acts, x_half, ys, zs, gram, out, notes,
                    held, own_v, half_v, gram_v, inner, sums, sems):
    rows, width = inner.shape[1], held.shape[2]
    quarter = acts.shape[1] // 4
    core, side = position()
    mirrored = core ^ side
    in_half = (1 - side) * quarter
    half_at = core * 2 * quarter
    copies = copies_of({
        XS: (columns(acts, half_at + in_half, width), held.at[XS, :rows]),
        XC: (columns(x_half, in_half, width), held.at[XC]),
        YS: (ys, held.at[YS]),
        ZS: (zs, held.at[ZS]),
        "g0": (gram.at[0], gram_v.at[0]),
        "g1": (gram.at[1], gram_v.at[1]),
        "g2": (gram.at[2], gram_v.at[2]),
        "own": (columns(acts, half_at, 2 * quarter), own_v),
        "half": (x_half.at[:, :2 * quarter], half_v),
        "g3": (gram.at[3], gram_v.at[3]),
        "info": (own_info, held.at[XS, rows:, :LANES]),
    }, sems)
    start(copies, YS, XS, "info", ZS, "g0", XC, "g1", "g2", "own", "half", "g3")
    wait(copies, YS, XS, "info")
    product(held.at[YS], held.at[XS], inner.at[0])
    wait(copies, "g0", ZS)
    product(held.at[YS], held.at[ZS], inner.at[1])
    token_sums(inner.at[0], gram_v.at[0], sums.at[0])
    wait(copies, "g1", XC, "g2")
    product(held.at[YS], held.at[XC], inner.at[0])
    token_sums(inner.at[1], gram_v.at[1], sums.at[1])
    wait(copies, "own", "half")
    product(half_v, own_v, inner.at[1])
    token_sums(inner.at[0], gram_v.at[2], sums.at[2])
    wait(copies, "g3")
    token_sums(inner.at[1], gram_v.at[3], sums.at[3], ordered=False)
    notes[...] = jnp.zeros_like(notes)
    for block in (XS, XC, YS, ZS):
        notes[block] = held[block, rows:, :LANES]
    info = {block: info_row(notes, block) for block in (XS, XC, YS, ZS)}
    total = domain_sums(tuple(enumerate(FIRST)), factor, (mirrored, core, side), info, sums)
    out[...] = jnp.zeros_like(out)
    for block, value in total.items():
        out[block] = value


def same_two_kernel(factor, at, notes, earlier, acts, x_half, ys, zs, gram, out,
                    held, notes_v, earlier_v, gram_v, inner, sums, sems):
    rows, width = inner.shape[1], held.shape[2]
    quarter = acts.shape[1] // 4
    core, side = position()
    mirrored = core ^ side
    in_half = (1 - side) * quarter
    copies = copies_of({
        XS: (columns(acts, core * 2 * quarter + in_half + at, width), held.at[XS, :rows]),
        XC: (columns(x_half, in_half + at, width), held.at[XC]),
        YS: (ys, held.at[YS, :rows]),
        ZS: (zs, held.at[ZS, :rows]),
        "g0": (gram.at[0], gram_v.at[0]),
        "g1": (gram.at[1], gram_v.at[1]),
        "g2": (gram.at[2], gram_v.at[2]),
        "notes": (notes, notes_v),
        "earlier": (earlier, earlier_v),
    }, sems)
    start(copies, YS, XS, ZS, "g0", "g1", XC, "g2", "notes", "earlier")
    wait(copies, YS, XS)
    product(held.at[YS], held.at[XS], inner.at[0])
    wait(copies, ZS, "g0")
    product(held.at[YS], held.at[ZS], inner.at[1])
    token_sums(inner.at[0], gram_v.at[0], sums.at[0])
    wait(copies, "g1", XC, "g2", "notes", "earlier")
    product(held.at[YS], held.at[XC], inner.at[0])
    token_sums(inner.at[1], gram_v.at[1], sums.at[1])
    token_sums(inner.at[0], gram_v.at[2], sums.at[2])
    info = {block: info_row(notes_v, block) for block in (XS, XC, YS, ZS)}
    pairs = ((0, 0), (1, 1), (2, 2))
    total = domain_sums(pairs, factor, (mirrored, core, side), info, sums)
    out[...] = earlier_v[...]
    for block, value in total.items():
        out[block] = earlier_v[block] + value


def position():
    me = lax.axis_index("ex")
    return me & 1, lax.shift_right_logical(me, 1) & 1


def cross_kernel(factor, at, notes, earlier, *refs):
    (acts, x_half, ys, yc, zs, zc, gram), refs = refs[:7], refs[7:]
    outs, (held, notes_v, earlier_v, gram_v, inner, sums, sems) = refs[:-7], refs[-7:]
    rows, width = inner.shape[1], held.shape[2]
    quarter = acts.shape[1] // 4
    core, side = position()
    mirrored = core ^ side
    in_half = (1 - side) * quarter
    work_at = core * 2 * quarter + in_half
    copies = copies_of({
        XS: (columns(acts, work_at + at, width), held.at[XS, :rows, :]),
        XC: (columns(x_half, in_half + at, width), held.at[XC]),
        YS: (ys, held.at[YS, :ys.shape[0]]),
        YC: (yc, held.at[YC, :yc.shape[0]]),
        ZS: (zs, held.at[ZS, :zs.shape[0]]),
        ZC: (zc, held.at[ZC, :zc.shape[0]]),
        "g4": (gram.at[4], gram_v.at[0]),
        "g5": (gram.at[5], gram_v.at[1]),
        "g6": (gram.at[6], gram_v.at[2]),
        "g2": (gram.at[2], gram_v.at[3]),
        "notes": (notes, notes_v),
        "earlier": (earlier, earlier_v),
    }, sems)
    start(copies, YC, XC, ZC, "g4", YS, ZS, "g5", XS, "g6", "g2", "notes", "earlier")
    wait(copies, YC, XC)
    product(held.at[YC], held.at[XC], inner.at[0])
    wait(copies, ZC)
    product(held.at[YC], held.at[ZC], inner.at[1])
    wait(copies, "g4", YS, ZS)
    token_sums(inner.at[0], gram_v.at[0], sums.at[0])
    product(held.at[jnp.where(mirrored == 0, YC, YS)], held.at[jnp.where(mirrored == 0, ZS, ZC)], inner.at[0])
    wait(copies, "g5", XS)
    token_sums(inner.at[1], gram_v.at[1], sums.at[1])
    wait(copies, "g6", "g2", "notes", "earlier")

    @pl.when(mirrored == 1)
    def _():
        product(held.at[YC], held.at[XS], inner.at[1])
        token_sums(inner.at[0], gram_v.at[2], sums.at[2])
        token_sums(inner.at[1], gram_v.at[3], sums.at[3])

    @pl.when(mirrored == 0)
    def _():
        token_sums(inner.at[0], gram_v.at[2], sums.at[2])
        sums[3] = jnp.zeros(sums.shape[1:], jnp.float32)

    if at == 0:
        total_out, notes_out = outs
        for block in (YC, ZC):
            notes_v[block] = held[block, rows:, :LANES]
        notes_out[...] = notes_v[...]
    info = {block: info_row(notes_v, block) for block in range(6)}
    pairs = ((0, 4), (1, 5), (2, 6), (2, 7), (3, 8))
    total = domain_sums(pairs, factor, (mirrored, core, side), info, sums)
    examples = sums.shape[1]
    for block, value in total.items():
        value = value + earlier_v[block]
        if at == 0:
            total_out[block] = value
        else:
            outs[block][...] = value[:, :examples]


def per_device(acts, grads, domain, listed):
    rows, width = acts.shape
    examples = rows // TOK
    quarter = width // 4
    me = lax.axis_index("ex")
    core = me % 2
    side = (me // 2) % 2
    mirrored = core ^ side

    pair_of = [
        [pair for pair in range(len(PAIRS)) if SLOT[pair] == slot] for slot in range(SLOTS)
    ]

    def listing(end):
        return [
            PAIRS[pairs[0]][end] if len(pairs) == 1 else jnp.where(
                mirrored == ONLY[pairs[0]], PAIRS[pairs[0]][end], PAIRS[pairs[1]][end])
            for pairs in pair_of
        ]

    table = jnp.stack([jnp.asarray(block, jnp.int32) for block in listing(0) + listing(1)])
    places = jnp.stack([core * 2 + side, core * 2 + (1 - side)]).astype(jnp.int32)
    cross_places = jnp.stack([(1 - core) * 2 + side, (1 - core) * 2 + (1 - side)]).astype(jnp.int32)
    half_place = jnp.stack([1 - core]).astype(jnp.int32)

    own_info = jnp.concatenate(
        [domain, listed[0], jnp.zeros((LANES - examples - 2,), jnp.int32)]
    )
    own_info = jnp.broadcast_to(own_info.astype(acts.dtype)[None, :], (INFO, LANES))

    grads_ys = send(grads, across, 0)
    grads_zs = send(grads, along, 0)
    cut_ys, cut_zs, cut_ys_two, cut_zs_two = cut(acts, own_info, places)
    own_info, _ = lax.optimization_barrier((own_info, cut_ys))
    cut_yc, cut_zc, cut_yc_two, cut_zc_two = cut(acts, own_info, cross_places)
    own_info, _ = lax.optimization_barrier((own_info, cut_yc))
    ys_one = send(cut_ys, across, 0)
    zs_one = send(cut_zs, along, 0)
    ys_two = send(cut_ys_two, across, 0)
    yc_one = send(cut_yc, across, 1)
    zc_one = send(cut_zc, along, 1)

    def exchange(*values):
        return lax.cond(
            listed[0, 0] < 2,
            lambda *sent: tuple(send(value, stay, 1) for value in sent),
            lambda *sent: tuple(jnp.zeros_like(value) for value in sent),
            *values,
        )

    x_half, = exchange(cut_half(acts, grads, own_info, half_place))
    grads_ys, grads_zs, x_half = lax.optimization_barrier((grads_ys, grads_zs, x_half))
    grads_yc, grads_zc = exchange(grads_ys, grads_zs)
    factor = 1.0 / (TOK * math.sqrt(width * grads.shape[1]))

    gram = grams(table, grads, x_half, grads_ys, grads_yc, grads_zs, grads_zc)
    cut_zs_two, cut_yc_two, gram = lax.optimization_barrier((cut_zs_two, cut_yc_two, gram))
    zs_two = send(cut_zs_two, along, 0)
    yc_two = send(cut_yc_two, across, 1)

    vmem = pl.BlockSpec(memory_space=pltpu.VMEM)
    hbm = pl.BlockSpec(memory_space=pl.ANY)
    all_sums = jax.ShapeDtypeStruct((6, DOMAINS, LANES), jnp.float32)
    all_notes = jax.ShapeDtypeStruct((6, INFO, LANES), acts.dtype)
    notes_v = pltpu.VMEM(all_notes.shape, acts.dtype)
    sums_v = pltpu.VMEM(all_sums.shape, jnp.float32)

    def call(kernel, name, vmem_bytes, width, extra, operands, out_shape):
        return pl.pallas_call(
            kernel,
            in_specs=[hbm] * len(operands),
            out_specs=[vmem] * len(out_shape),
            out_shape=out_shape,
            scratch_shapes=[pltpu.VMEM((6, rows + INFO, width), acts.dtype)] + extra + [
                pltpu.VMEM((4, rows, rows), jnp.float32),
                pltpu.VMEM((2, rows, rows), jnp.float32),
                pltpu.VMEM((4, examples, rows), jnp.float32),
                pltpu.SemaphoreType.DMA((12,)),
            ],
            compiler_params=pltpu.CompilerParams(vmem_limit_bytes=vmem_bytes),
            cost_estimate=SMALL,
            name=name,
        )(*operands)

    one, two = chunks(quarter)
    extra = [
        pltpu.VMEM((rows, 2 * quarter), acts.dtype),
        pltpu.VMEM((rows + INFO, 2 * quarter), acts.dtype),
    ]
    partial = functools.partial
    sums, notes = call(
        partial(same_one_kernel, factor), "same_one", VMEM_BYTES, one, extra,
        (own_info, acts, x_half, ys_one, zs_one, gram), [all_sums, all_notes],
    )
    cut_zc_two, sums = lax.optimization_barrier((cut_zc_two, sums))
    zc_two = send(cut_zc_two, along, 1)
    extra = [notes_v, sums_v]
    sums, notes = call(
        partial(cross_kernel, factor, 0), "cross_one", PAIRS_VMEM_BYTES, one, extra,
        (notes, sums, acts, x_half, ys_one, yc_one, zs_one, zc_one, gram), [all_sums, all_notes],
    )
    sums, = call(
        partial(same_two_kernel, factor, one), "same_two", PAIRS_VMEM_BYTES, two, extra,
        (notes, sums, acts, x_half, ys_two, zs_two, gram), [all_sums],
    )
    sums = call(
        partial(cross_kernel, factor, one), "cross_two", PAIRS_VMEM_BYTES, two, extra,
        (notes, sums, acts, x_half, ys_two, yc_two, zs_two, zc_two, gram),
        [jax.ShapeDtypeStruct((DOMAINS, examples), jnp.float32)] * 6,
    )

    total = sums[XS]
    total = total + send(sums[ZS], against, 0)
    total = total + send(sums[ZC], against, 1)
    total = total + send(sums[YS], across, 0)
    total = total + send(sums[YC], across, 1)
    total = total + send(sums[XC], stay, 1)
    return total.T


def solution(mesh):
    in_specs = (
        P(("groups", "ex"), None),
        P(("groups", "ex"), None),
        P(("groups", "ex")),
        P(("groups", "ex"), None),
    )
    out_specs = P(("groups", "ex"), None)
    return jax.shard_map(
        per_device, mesh=mesh, in_specs=in_specs, out_specs=out_specs, check_vma=False
    )
```

```python
import functools
import math

import jax
import jax.numpy as jnp
from jax import lax
from jax.experimental import pallas as pl
from jax.experimental.pallas import tpu as pltpu
from jax.sharding import PartitionSpec as P

TOK = 8
TOK_BITS = 3
DOMAINS = 48
LANES = 128
VMEM_BYTES = 63 * 1024 * 1024
LAST_VMEM_BYTES = 44 * 1024 * 1024

INFO = 16

XS, XC, YS, YC, ZS, ZC = range(6)
PAIRS = (
    (YS, XS, 1), (YS, ZS, 1), (YS, XC, 0), (XC, XS, 0),
    (YC, XC, 1), (YC, ZC, 1), (YC, ZS, 0), (YS, ZC, 0), (YC, XS, 0),
)
ONLY = {2: 0, 6: 0, 7: 1, 8: 1}
SLOT = (0, 1, 2, 3, 4, 5, 6, 6, 2)
SLOTS = 7
FIRST = (0, 1, 2, 3)
SMALL = pl.CostEstimate(flops=1, bytes_accessed=1, transcendentals=0)
NT = (((1,), (1,)), ((), ()))
NN = (((1,), (0,)), ((), ()))


def across(chip):
    return chip ^ 1


def along(chip):
    return chip + 2 if chip & 1 else chip - 2


def against(chip):
    return chip - 2 if chip & 1 else chip + 2


def stay(chip):
    return chip


def send(value, move, flip):
    chips = lax.axis_size("ex") // 2
    pairs = [
        (2 * chip + core, 2 * (move(chip) % chips) + (core ^ flip))
        for chip in range(chips)
        for core in range(2)
    ]
    return lax.ppermute(value, "ex", pairs)


def token_major(rows):
    to = lax.broadcasted_iota(jnp.int32, (rows, rows), 0)
    source = lax.broadcasted_iota(jnp.int32, (rows, rows), 1)
    examples = rows // TOK
    place = (source & (TOK - 1)) * examples + lax.shift_right_logical(source, TOK_BITS)
    return (place == to).astype(jnp.bfloat16)


def reorder(order, block):
    return jnp.dot(order, block, preferred_element_type=jnp.float32).astype(jnp.bfloat16)


def put(target, value, info):
    rows = value.shape[0]
    target[:rows, :] = value
    target[rows:, :] = jnp.concatenate([info[...]] * (target.shape[1] // LANES), axis=1)


def chunks(quarter):
    second = quarter // LANES * 3 // 10 * LANES
    return quarter - second, second


def cut_kernel(places, info, y_acts, z_acts, y_one, z_one, y_two, z_two, order):
    rows, split = order.shape[0], y_one.shape[1]
    order[...] = token_major(rows)
    put(y_one, reorder(order[...], y_acts[:, :split]), info)
    put(z_one, z_acts[:, :split], info)
    y_two[...] = reorder(order[...], y_acts[:, split:])
    z_two[...] = z_acts[:, split:]


def cut(acts, info, places):
    rows, width = acts.shape
    quarter = width // 4
    one, two = chunks(quarter)
    shapes = [(rows + INFO, one)] * 2 + [(rows, two)] * 2
    return pl.pallas_call(
        cut_kernel,
        grid_spec=pltpu.PrefetchScalarGridSpec(
            num_scalar_prefetch=1,
            grid=(1,),
            in_specs=[
                pl.BlockSpec((INFO, LANES), lambda i, p: (0, 0)),
                pl.BlockSpec((rows, quarter), lambda i, p: (0, p[0])),
                pl.BlockSpec((rows, quarter), lambda i, p: (0, p[1])),
            ],
            out_specs=[pl.BlockSpec(shape, lambda i, p: (0, 0)) for shape in shapes],
            scratch_shapes=[pltpu.VMEM((rows, rows), jnp.bfloat16)],
        ),
        out_shape=[jax.ShapeDtypeStruct(shape, acts.dtype) for shape in shapes],
        compiler_params=pltpu.CompilerParams(vmem_limit_bytes=VMEM_BYTES),
        cost_estimate=SMALL,
        name="cut",
    )(places, info, acts, acts)


def half_kernel(steps, place, info, acts, grads, out):
    @pl.when(pl.program_id(0) < steps)
    def _():
        put(out, acts[...], info)

    @pl.when(pl.program_id(0) >= steps)
    def _():
        put(out, grads[...], info)


def cut_half(acts, grads, info, place):
    rows, width = acts.shape
    half, depth = width // 2, grads.shape[1]
    step = math.gcd(math.gcd(half, depth), 512)
    steps = half // step
    return pl.pallas_call(
        functools.partial(half_kernel, steps),
        grid_spec=pltpu.PrefetchScalarGridSpec(
            num_scalar_prefetch=1,
            grid=(steps + depth // step,),
            in_specs=[
                pl.BlockSpec((INFO, LANES), lambda i, p: (0, 0)),
                pl.BlockSpec((rows, step), lambda i, p: (0, p[0] * steps + jnp.minimum(i, steps - 1))),
                pl.BlockSpec((rows, step), lambda i, p: (0, jnp.maximum(i - steps, 0))),
            ],
            out_specs=pl.BlockSpec((rows + INFO, step), lambda i, p: (0, i)),
        ),
        out_shape=jax.ShapeDtypeStruct((rows + INFO, half + depth), acts.dtype),
        compiler_params=pltpu.CompilerParams(vmem_limit_bytes=VMEM_BYTES),
        cost_estimate=SMALL,
        name="half",
    )(place, info, acts, grads)


def grams_kernel(table, xs, xc, ys, yc, zs, zc, out, held, result, in_sems, out_sems):
    rows, depth = xs.shape
    order = token_major(rows)
    sources = (xs, xc.at[:rows, xc.shape[1] - depth:], ys, yc, zs, zc)
    loads = [
        pltpu.make_async_copy(source, held.at[at], in_sems.at[at])
        for at, source in enumerate(sources)
    ]
    for load in loads:
        load.start()
    for load in loads:
        load.wait()
    for block in (YS, YC):
        held[block] = reorder(order, held[block])

    def leave(slot):
        return pltpu.make_async_copy(result.at[slot], out.at[slot], out_sems.at[slot])

    @pl.loop(0, SLOTS)
    def _(slot):
        result[slot] = lax.dot_general(
            held[table[slot]], held[table[SLOTS + slot]], NT, preferred_element_type=jnp.float32
        )
        leave(slot).start()

    for slot in range(SLOTS):
        leave(slot).wait()


def grams(table, grads, *messages):
    rows, width = grads.shape
    return pl.pallas_call(
        grams_kernel,
        in_specs=[pl.BlockSpec(memory_space=pltpu.SMEM)] + [pl.BlockSpec(memory_space=pl.ANY)] * 6,
        out_specs=pl.BlockSpec(memory_space=pl.ANY),
        out_shape=jax.ShapeDtypeStruct((SLOTS, rows, rows), jnp.float32),
        scratch_shapes=[
            pltpu.VMEM((6, rows, width), grads.dtype),
            pltpu.VMEM((SLOTS, rows, rows), jnp.float32),
            pltpu.SemaphoreType.DMA((6,)),
            pltpu.SemaphoreType.DMA((SLOTS,)),
        ],
        compiler_params=pltpu.CompilerParams(vmem_limit_bytes=VMEM_BYTES),
        cost_estimate=SMALL,
        name="grams",
    )(table, grads, *messages)


def product(one, two, inner):
    rows = inner.shape[0]
    inner[...] = lax.dot_general(
        one[:rows, :], two[:rows, :], NT, preferred_element_type=jnp.float32
    )


def token_sums(inner, gram, sums, ordered=True):
    examples, rows = sums.shape
    if ordered:
        sums[...] = sum(
            inner[at:at + examples, :] * gram[at:at + examples, :]
            for at in range(0, rows, examples)
        )
    else:
        weighted = inner[...] * gram[...]
        sums[...] = weighted.reshape(examples, TOK, rows).sum(axis=1)


def two_parts(value):
    high = value.astype(jnp.bfloat16)
    return high, (value - high.astype(jnp.float32)).astype(jnp.bfloat16)


def dot_parts(value, table):
    high, low = two_parts(value)
    return lax.dot_general(low, table, NT, preferred_element_type=jnp.float32) + lax.dot_general(
        high, table, NT, preferred_element_type=jnp.float32
    )


def side_by_side(values):
    return jnp.concatenate(values, axis=1)


def domain_sums(pairs, factor, place, info, sums):
    count, examples, rows = sums.shape
    example = lax.broadcasted_iota(jnp.int32, (LANES, rows), 0)
    column = lax.broadcasted_iota(jnp.int32, (LANES, rows), 1)
    gather = (lax.shift_right_logical(column, TOK_BITS) == example).astype(jnp.bfloat16)
    tiles = dot_parts(sums[...].reshape(count * examples, rows), gather)
    tiles = tiles.reshape(count, examples, LANES)
    mirrored, core, side = place
    lane = lax.broadcasted_iota(jnp.int32, (1, LANES), 1)
    row = lax.broadcasted_iota(jnp.int32, (DOMAINS, LANES), 0)
    hot = {
        block: ((value.astype(jnp.int32) == row) & (lane < examples)).astype(jnp.bfloat16)
        for block, value in info.items()
    }

    def listed_flag(block, apart):
        return jnp.sum(jnp.where(lane == examples + apart, info[block], 0.0), axis=1, keepdims=True)

    pad = jnp.zeros((LANES - examples, LANES), jnp.float32)
    groups = {}
    for at, pair in pairs:
        one, two, apart = PAIRS[pair]
        if one == XC:
            two_leads = core == 0
        elif two in (XS, XC):
            two_leads = side == 0
        else:
            two_leads = side == 1
        flag = jnp.where(two_leads, listed_flag(two, apart), listed_flag(one, apart))
        if pair in ONLY:
            flag = jnp.where(mirrored == ONLY[pair], flag, 0.0)
        tile = jnp.concatenate([tiles[at], pad], axis=0) * (flag * factor)
        groups.setdefault(one, []).append((two, *two_parts(tile)))
    total = {}

    def add(block, term):
        total[block] = total[block] + term if block in total else term

    for one, group in groups.items():
        others = side_by_side([hot[two] for two, _, _ in group])
        highs = side_by_side([high for _, high, _ in group])
        lows = side_by_side([low for _, _, low in group])
        add(one, lax.dot_general(
            side_by_side([others, others]), side_by_side([highs, lows]), NT,
            preferred_element_type=jnp.float32,
        ))
        columns_of = lax.dot_general(
            side_by_side([hot[one], hot[one]]), jnp.concatenate([highs, lows], axis=0), NN,
            preferred_element_type=jnp.float32,
        )
        for at, (two, _, _) in enumerate(group):
            add(two, columns_of[:, at * LANES:(at + 1) * LANES])
    return total


def copies_of(loads, sems):
    return {
        key: pltpu.make_async_copy(source, target, sems.at[at])
        for at, (key, (source, target)) in enumerate(loads.items())
    }


def start(copies, *keys):
    for key in keys:
        copies[key].start()


def wait(copies, *keys):
    for key in keys:
        copies[key].wait()


def info_row(notes, block):
    return notes[block].astype(jnp.float32)[:1]


def columns(ref, at, width):
    return ref.at[:, pl.ds(pl.multiple_of(at, LANES), width)]


def same_one_kernel(factor, own_info, acts, x_half, ys, zs, gram, out, notes,
                    held, own_v, half_v, gram_v, inner, sums, sems):
    rows, width = inner.shape[1], held.shape[2]
    quarter = acts.shape[1] // 4
    core, side = position()
    mirrored = core ^ side
    in_half = (1 - side) * quarter
    half_at = core * 2 * quarter
    copies = copies_of({
        XS: (columns(acts, half_at + in_half, width), held.at[XS, :rows]),
        XC: (columns(x_half, in_half, width), held.at[XC]),
        YS: (ys, held.at[YS]),
        ZS: (zs, held.at[ZS]),
        "g0": (gram.at[0], gram_v.at[0]),
        "g1": (gram.at[1], gram_v.at[1]),
        "g2": (gram.at[2], gram_v.at[2]),
        "own": (columns(acts, half_at, 2 * quarter), own_v),
        "half": (x_half.at[:, :2 * quarter], half_v),
        "g3": (gram.at[3], gram_v.at[3]),
        "info": (own_info, held.at[XS, rows:, :LANES]),
    }, sems)
    start(copies, YS, XS, "info", ZS, "g0", XC, "g1", "g2", "own", "half", "g3")
    wait(copies, YS, XS, "info")
    product(held.at[YS], held.at[XS], inner.at[0])
    wait(copies, "g0", ZS)
    product(held.at[YS], held.at[ZS], inner.at[1])
    token_sums(inner.at[0], gram_v.at[0], sums.at[0])
    wait(copies, "g1", XC, "g2")
    product(held.at[YS], held.at[XC], inner.at[0])
    token_sums(inner.at[1], gram_v.at[1], sums.at[1])
    wait(copies, "own", "half")
    product(half_v, own_v, inner.at[1])
    token_sums(inner.at[0], gram_v.at[2], sums.at[2])
    wait(copies, "g3")
    token_sums(inner.at[1], gram_v.at[3], sums.at[3], ordered=False)
    notes[...] = jnp.zeros_like(notes)
    for block in (XS, XC, YS, ZS):
        notes[block] = held[block, rows:, :LANES]
    info = {block: info_row(notes, block) for block in (XS, XC, YS, ZS)}
    total = domain_sums(tuple(enumerate(FIRST)), factor, (mirrored, core, side), info, sums)
    out[...] = jnp.zeros_like(out)
    for block, value in total.items():
        out[block] = value


def same_two_kernel(factor, at, notes, earlier, acts, x_half, ys, zs, gram, out,
                    held, notes_v, earlier_v, gram_v, inner, sums, sems):
    rows, width = inner.shape[1], held.shape[2]
    quarter = acts.shape[1] // 4
    core, side = position()
    mirrored = core ^ side
    in_half = (1 - side) * quarter
    copies = copies_of({
        XS: (columns(acts, core * 2 * quarter + in_half + at, width), held.at[XS, :rows]),
        XC: (columns(x_half, in_half + at, width), held.at[XC]),
        YS: (ys, held.at[YS, :rows]),
        ZS: (zs, held.at[ZS, :rows]),
        "g0": (gram.at[0], gram_v.at[0]),
        "g1": (gram.at[1], gram_v.at[1]),
        "g2": (gram.at[2], gram_v.at[2]),
        "notes": (notes, notes_v),
        "earlier": (earlier, earlier_v),
    }, sems)
    start(copies, YS, XS, ZS, "g0", "g1", XC, "g2", "notes", "earlier")
    wait(copies, YS, XS)
    product(held.at[YS], held.at[XS], inner.at[0])
    wait(copies, ZS, "g0")
    product(held.at[YS], held.at[ZS], inner.at[1])
    token_sums(inner.at[0], gram_v.at[0], sums.at[0])
    wait(copies, "g1", XC, "g2", "notes", "earlier")
    product(held.at[YS], held.at[XC], inner.at[0])
    token_sums(inner.at[1], gram_v.at[1], sums.at[1])
    token_sums(inner.at[0], gram_v.at[2], sums.at[2])
    info = {block: info_row(notes_v, block) for block in (XS, XC, YS, ZS)}
    pairs = ((0, 0), (1, 1), (2, 2))
    total = domain_sums(pairs, factor, (mirrored, core, side), info, sums)
    out[...] = earlier_v[...]
    for block, value in total.items():
        out[block] = earlier_v[block] + value


def position():
    me = lax.axis_index("ex")
    return me & 1, lax.shift_right_logical(me, 1) & 1


def cross_kernel(factor, at, notes, earlier, *refs):
    (acts, x_half, ys, yc, zs, zc, gram), refs = refs[:7], refs[7:]
    outs, (held, notes_v, earlier_v, gram_v, inner, sums, sems) = refs[:-7], refs[-7:]
    rows, width = inner.shape[1], held.shape[2]
    quarter = acts.shape[1] // 4
    core, side = position()
    mirrored = core ^ side
    in_half = (1 - side) * quarter
    work_at = core * 2 * quarter + in_half
    copies = copies_of({
        XS: (columns(acts, work_at + at, width), held.at[XS, :rows, :]),
        XC: (columns(x_half, in_half + at, width), held.at[XC]),
        YS: (ys, held.at[YS, :ys.shape[0]]),
        YC: (yc, held.at[YC, :yc.shape[0]]),
        ZS: (zs, held.at[ZS, :zs.shape[0]]),
        ZC: (zc, held.at[ZC, :zc.shape[0]]),
        "g4": (gram.at[4], gram_v.at[0]),
        "g5": (gram.at[5], gram_v.at[1]),
        "g6": (gram.at[6], gram_v.at[2]),
        "g2": (gram.at[2], gram_v.at[3]),
        "notes": (notes, notes_v),
        "earlier": (earlier, earlier_v),
    }, sems)
    start(copies, YC, XC, ZC, "g4", YS, ZS, "g5", XS, "g6", "g2", "notes", "earlier")
    wait(copies, YC, XC)
    product(held.at[YC], held.at[XC], inner.at[0])
    wait(copies, ZC)
    product(held.at[YC], held.at[ZC], inner.at[1])
    wait(copies, "g4", YS, ZS)
    token_sums(inner.at[0], gram_v.at[0], sums.at[0])
    product(held.at[jnp.where(mirrored == 0, YC, YS)], held.at[jnp.where(mirrored == 0, ZS, ZC)], inner.at[0])
    wait(copies, "g5", XS)
    token_sums(inner.at[1], gram_v.at[1], sums.at[1])
    wait(copies, "g6", "g2", "notes", "earlier")

    @pl.when(mirrored == 1)
    def _():
        product(held.at[YC], held.at[XS], inner.at[1])
        token_sums(inner.at[0], gram_v.at[2], sums.at[2])
        token_sums(inner.at[1], gram_v.at[3], sums.at[3])

    @pl.when(mirrored == 0)
    def _():
        token_sums(inner.at[0], gram_v.at[2], sums.at[2])
        sums[3] = jnp.zeros(sums.shape[1:], jnp.float32)

    if at == 0:
        total_out, notes_out = outs
        for block in (YC, ZC):
            notes_v[block] = held[block, rows:, :LANES]
        notes_out[...] = notes_v[...]
    info = {block: info_row(notes_v, block) for block in range(6)}
    pairs = ((0, 4), (1, 5), (2, 6), (2, 7), (3, 8))
    total = domain_sums(pairs, factor, (mirrored, core, side), info, sums)
    examples = sums.shape[1]
    for block, value in total.items():
        value = value + earlier_v[block]
        if at == 0:
            total_out[block] = value
        else:
            outs[block][...] = value[:, :examples]


def per_device(acts, grads, domain, listed):
    rows, width = acts.shape
    examples = rows // TOK
    quarter = width // 4
    me = lax.axis_index("ex")
    core = me % 2
    side = (me // 2) % 2
    mirrored = core ^ side

    pair_of = [
        [pair for pair in range(len(PAIRS)) if SLOT[pair] == slot] for slot in range(SLOTS)
    ]

    def listing(end):
        return [
            PAIRS[pairs[0]][end] if len(pairs) == 1 else jnp.where(
                mirrored == ONLY[pairs[0]], PAIRS[pairs[0]][end], PAIRS[pairs[1]][end])
            for pairs in pair_of
        ]

    table = jnp.stack([jnp.asarray(block, jnp.int32) for block in listing(0) + listing(1)])
    places = jnp.stack([core * 2 + side, core * 2 + (1 - side)]).astype(jnp.int32)
    cross_places = jnp.stack([(1 - core) * 2 + side, (1 - core) * 2 + (1 - side)]).astype(jnp.int32)
    half_place = jnp.stack([1 - core]).astype(jnp.int32)

    own_info = jnp.concatenate(
        [domain, listed[0], jnp.zeros((LANES - examples - 2,), jnp.int32)]
    )
    own_info = jnp.broadcast_to(own_info.astype(acts.dtype)[None, :], (INFO, LANES))

    grads_ys = send(grads, across, 0)
    grads_zs = send(grads, along, 0)
    cut_ys, cut_zs, cut_ys_two, cut_zs_two = cut(acts, own_info, places)
    own_info, _ = lax.optimization_barrier((own_info, cut_ys))
    cut_yc, cut_zc, cut_yc_two, cut_zc_two = cut(acts, own_info, cross_places)
    own_info, _ = lax.optimization_barrier((own_info, cut_yc))
    ys_one = send(cut_ys, across, 0)
    zs_one = send(cut_zs, along, 0)
    ys_two = send(cut_ys_two, across, 0)
    yc_one = send(cut_yc, across, 1)
    zc_one = send(cut_zc, along, 1)

    def exchange(*values):
        return lax.cond(
            listed[0, 0] < 2,
            lambda *sent: tuple(send(value, stay, 1) for value in sent),
            lambda *sent: tuple(jnp.zeros_like(value) for value in sent),
            *values,
        )

    x_half, = exchange(cut_half(acts, grads, own_info, half_place))
    grads_ys, grads_zs, x_half = lax.optimization_barrier((grads_ys, grads_zs, x_half))
    grads_yc, grads_zc = exchange(grads_ys, grads_zs)
    factor = 1.0 / (TOK * math.sqrt(width * grads.shape[1]))

    gram = grams(table, grads, x_half, grads_ys, grads_yc, grads_zs, grads_zc)
    cut_zs_two, cut_yc_two, gram = lax.optimization_barrier((cut_zs_two, cut_yc_two, gram))
    zs_two = send(cut_zs_two, along, 0)
    yc_two = send(cut_yc_two, across, 1)

    vmem = pl.BlockSpec(memory_space=pltpu.VMEM)
    hbm = pl.BlockSpec(memory_space=pl.ANY)
    all_sums = jax.ShapeDtypeStruct((6, DOMAINS, LANES), jnp.float32)
    all_notes = jax.ShapeDtypeStruct((6, INFO, LANES), acts.dtype)
    notes_v = pltpu.VMEM(all_notes.shape, acts.dtype)
    sums_v = pltpu.VMEM(all_sums.shape, jnp.float32)

    def call(kernel, name, vmem_bytes, width, extra, operands, out_shape):
        return pl.pallas_call(
            kernel,
            in_specs=[hbm] * len(operands),
            out_specs=[vmem] * len(out_shape),
            out_shape=out_shape,
            scratch_shapes=[pltpu.VMEM((6, rows + INFO, width), acts.dtype)] + extra + [
                pltpu.VMEM((4, rows, rows), jnp.float32),
                pltpu.VMEM((2, rows, rows), jnp.float32),
                pltpu.VMEM((4, examples, rows), jnp.float32),
                pltpu.SemaphoreType.DMA((12,)),
            ],
            compiler_params=pltpu.CompilerParams(vmem_limit_bytes=vmem_bytes),
            cost_estimate=SMALL,
            name=name,
        )(*operands)

    one, two = chunks(quarter)
    extra = [
        pltpu.VMEM((rows, 2 * quarter), acts.dtype),
        pltpu.VMEM((rows + INFO, 2 * quarter), acts.dtype),
    ]
    partial = functools.partial
    sums, notes = call(
        partial(same_one_kernel, factor), "same_one", VMEM_BYTES, one, extra,
        (own_info, acts, x_half, ys_one, zs_one, gram), [all_sums, all_notes],
    )
    cut_zc_two, sums = lax.optimization_barrier((cut_zc_two, sums))
    zc_two = send(cut_zc_two, along, 1)
    extra = [notes_v, sums_v]
    sums, notes = call(
        partial(cross_kernel, factor, 0), "cross_one", LAST_VMEM_BYTES, one, extra,
        (notes, sums, acts, x_half, ys_one, yc_one, zs_one, zc_one, gram), [all_sums, all_notes],
    )
    sums, = call(
        partial(same_two_kernel, factor, one), "same_two", LAST_VMEM_BYTES, two, extra,
        (notes, sums, acts, x_half, ys_two, zs_two, gram), [all_sums],
    )
    sums = call(
        partial(cross_kernel, factor, one), "cross_two", LAST_VMEM_BYTES, two, extra,
        (notes, sums, acts, x_half, ys_two, yc_two, zs_two, zc_two, gram),
        [jax.ShapeDtypeStruct((DOMAINS, examples), jnp.float32)] * 6,
    )

    total = sums[XS]
    total = total + send(sums[ZS], against, 0)
    total = total + send(sums[ZC], against, 1)
    total = total + send(sums[YS], across, 0)
    total = total + send(sums[YC], across, 1)
    total = total + send(sums[XC], stay, 1)
    return total.T


def solution(mesh):
    in_specs = (
        P(("groups", "ex"), None),
        P(("groups", "ex"), None),
        P(("groups", "ex")),
        P(("groups", "ex"), None),
    )
    out_specs = P(("groups", "ex"), None)
    return jax.shard_map(
        per_device, mesh=mesh, in_specs=in_specs, out_specs=out_specs, check_vma=False
    )
```

```python
import functools
import math

import jax
import jax.numpy as jnp
from jax import lax
from jax.experimental import pallas as pl
from jax.experimental.pallas import tpu as pltpu
from jax.sharding import PartitionSpec as P

TOK = 8
TOK_BITS = 3
DOMAINS = 48
LANES = 128
VMEM_BYTES = 63 * 1024 * 1024
LAST_VMEM_BYTES = 30 * 1024 * 1024

INFO = 16

XS, XC, YS, YC, ZS, ZC = range(6)
PAIRS = (
    (YS, XS, 1), (YS, ZS, 1), (YS, XC, 0), (XC, XS, 0),
    (YC, XC, 1), (YC, ZC, 1), (YC, ZS, 0), (YS, ZC, 0), (YC, XS, 0),
)
ONLY = {2: 0, 6: 0, 7: 1, 8: 1}
SLOT = (0, 1, 6, 2, 3, 4, 5, 5, 6)
SLOTS = 7
SAME_SLOTS = 3
FIRST = (0, 1, 2, 3)
SMALL = pl.CostEstimate(flops=1, bytes_accessed=1, transcendentals=0)
NT = (((1,), (1,)), ((), ()))
NN = (((1,), (0,)), ((), ()))


def across(chip):
    return chip ^ 1


def along(chip):
    return chip + 2 if chip & 1 else chip - 2


def against(chip):
    return chip - 2 if chip & 1 else chip + 2


def stay(chip):
    return chip


def send(value, move, flip):
    chips = lax.axis_size("ex") // 2
    pairs = [
        (2 * chip + core, 2 * (move(chip) % chips) + (core ^ flip))
        for chip in range(chips)
        for core in range(2)
    ]
    return lax.ppermute(value, "ex", pairs)


def token_major(rows):
    to = lax.broadcasted_iota(jnp.int32, (rows, rows), 0)
    source = lax.broadcasted_iota(jnp.int32, (rows, rows), 1)
    examples = rows // TOK
    place = (source & (TOK - 1)) * examples + lax.shift_right_logical(source, TOK_BITS)
    return (place == to).astype(jnp.bfloat16)


def reorder(order, block):
    return jnp.dot(order, block, preferred_element_type=jnp.float32).astype(jnp.bfloat16)


def put(target, value, info):
    rows = value.shape[0]
    target[:rows, :] = value
    target[rows:, :] = jnp.concatenate([info[...]] * (target.shape[1] // LANES), axis=1)


def chunks(quarter):
    second = quarter // LANES * 3 // 10 * LANES
    return quarter - second, second


def cut_kernel(places, info, y_acts, z_acts, y_one, z_one, y_two, z_two, order):
    rows, split = order.shape[0], y_one.shape[1]
    order[...] = token_major(rows)
    put(y_one, reorder(order[...], y_acts[:, :split]), info)
    put(z_one, z_acts[:, :split], info)
    y_two[...] = reorder(order[...], y_acts[:, split:])
    z_two[...] = z_acts[:, split:]


def cut(acts, info, places):
    rows, width = acts.shape
    quarter = width // 4
    one, two = chunks(quarter)
    shapes = [(rows + INFO, one)] * 2 + [(rows, two)] * 2
    return pl.pallas_call(
        cut_kernel,
        grid_spec=pltpu.PrefetchScalarGridSpec(
            num_scalar_prefetch=1,
            grid=(1,),
            in_specs=[
                pl.BlockSpec((INFO, LANES), lambda i, p: (0, 0)),
                pl.BlockSpec((rows, quarter), lambda i, p: (0, p[0])),
                pl.BlockSpec((rows, quarter), lambda i, p: (0, p[1])),
            ],
            out_specs=[pl.BlockSpec(shape, lambda i, p: (0, 0)) for shape in shapes],
            scratch_shapes=[pltpu.VMEM((rows, rows), jnp.bfloat16)],
        ),
        out_shape=[jax.ShapeDtypeStruct(shape, acts.dtype) for shape in shapes],
        compiler_params=pltpu.CompilerParams(vmem_limit_bytes=VMEM_BYTES),
        cost_estimate=SMALL,
        name="cut",
    )(places, info, acts, acts)


def half_kernel(steps, place, info, acts, grads, out):
    @pl.when(pl.program_id(0) < steps)
    def _():
        put(out, acts[...], info)

    @pl.when(pl.program_id(0) >= steps)
    def _():
        put(out, grads[...], info)


def cut_half(acts, grads, info, place):
    rows, width = acts.shape
    half, depth = width // 2, grads.shape[1]
    step = math.gcd(math.gcd(half, depth), 512)
    steps = half // step
    return pl.pallas_call(
        functools.partial(half_kernel, steps),
        grid_spec=pltpu.PrefetchScalarGridSpec(
            num_scalar_prefetch=1,
            grid=(steps + depth // step,),
            in_specs=[
                pl.BlockSpec((INFO, LANES), lambda i, p: (0, 0)),
                pl.BlockSpec((rows, step), lambda i, p: (0, p[0] * steps + jnp.minimum(i, steps - 1))),
                pl.BlockSpec((rows, step), lambda i, p: (0, jnp.maximum(i - steps, 0))),
            ],
            out_specs=pl.BlockSpec((rows + INFO, step), lambda i, p: (0, i)),
        ),
        out_shape=jax.ShapeDtypeStruct((rows + INFO, half + depth), acts.dtype),
        compiler_params=pltpu.CompilerParams(vmem_limit_bytes=VMEM_BYTES),
        cost_estimate=SMALL,
        name="half",
    )(place, info, acts, grads)


def grams_kernel(table, xs, xc, ys, yc, zs, zc, same, cross, held, result, in_sems, out_sems):
    rows, depth = xs.shape
    order = token_major(rows)
    sources = (xs, xc.at[:rows, xc.shape[1] - depth:], ys, yc, zs, zc)
    loads = [
        pltpu.make_async_copy(source, held.at[at], in_sems.at[at])
        for at, source in enumerate(sources)
    ]
    for load in loads:
        load.start()
    for load in loads:
        load.wait()
    for block in (YS, YC):
        held[block] = reorder(order, held[block])

    def leave(slot, array, at):
        return pltpu.make_async_copy(result.at[slot], array.at[at], out_sems.at[slot])

    @pl.loop(0, SLOTS)
    def _(slot):
        result[slot] = lax.dot_general(
            held[table[slot]], held[table[SLOTS + slot]], NT, preferred_element_type=jnp.float32
        )

        @pl.when(slot < SAME_SLOTS)
        def _():
            leave(slot, same, slot).start()

        @pl.when(slot >= SAME_SLOTS)
        def _():
            leave(slot, cross, slot - SAME_SLOTS).start()

    for slot in range(SLOTS):
        array, at = (same, slot) if slot < SAME_SLOTS else (cross, slot - SAME_SLOTS)
        leave(slot, array, at).wait()


def grams(table, grads, *messages):
    rows, width = grads.shape
    return pl.pallas_call(
        grams_kernel,
        in_specs=[pl.BlockSpec(memory_space=pltpu.SMEM)] + [pl.BlockSpec(memory_space=pl.ANY)] * 6,
        out_specs=[pl.BlockSpec(memory_space=pl.ANY)] * 2,
        out_shape=[
            jax.ShapeDtypeStruct((count, rows, rows), jnp.float32)
            for count in (SAME_SLOTS, SLOTS - SAME_SLOTS)
        ],
        scratch_shapes=[
            pltpu.VMEM((6, rows, width), grads.dtype),
            pltpu.VMEM((SLOTS, rows, rows), jnp.float32),
            pltpu.SemaphoreType.DMA((6,)),
            pltpu.SemaphoreType.DMA((SLOTS,)),
        ],
        compiler_params=pltpu.CompilerParams(vmem_limit_bytes=VMEM_BYTES),
        cost_estimate=SMALL,
        name="grams",
    )(table, grads, *messages)


def product(one, two, inner):
    rows = inner.shape[0]
    inner[...] = lax.dot_general(
        one[:rows, :], two[:rows, :], NT, preferred_element_type=jnp.float32
    )


def token_sums(inner, gram, sums, ordered=True):
    examples, rows = sums.shape
    if ordered:
        sums[...] = sum(
            inner[at:at + examples, :] * gram[at:at + examples, :]
            for at in range(0, rows, examples)
        )
    else:
        weighted = inner[...] * gram[...]
        sums[...] = weighted.reshape(examples, TOK, rows).sum(axis=1)


def two_parts(value):
    high = value.astype(jnp.bfloat16)
    return high, (value - high.astype(jnp.float32)).astype(jnp.bfloat16)


def dot_parts(value, table):
    high, low = two_parts(value)
    return lax.dot_general(low, table, NT, preferred_element_type=jnp.float32) + lax.dot_general(
        high, table, NT, preferred_element_type=jnp.float32
    )


def side_by_side(values):
    return jnp.concatenate(values, axis=1)


def domain_sums(pairs, factor, place, info, sums):
    count, examples, rows = sums.shape
    example = lax.broadcasted_iota(jnp.int32, (LANES, rows), 0)
    column = lax.broadcasted_iota(jnp.int32, (LANES, rows), 1)
    gather = (lax.shift_right_logical(column, TOK_BITS) == example).astype(jnp.bfloat16)
    tiles = dot_parts(sums[...].reshape(count * examples, rows), gather)
    tiles = tiles.reshape(count, examples, LANES)
    mirrored, core, side = place
    lane = lax.broadcasted_iota(jnp.int32, (1, LANES), 1)
    row = lax.broadcasted_iota(jnp.int32, (DOMAINS, LANES), 0)
    hot = {
        block: ((value.astype(jnp.int32) == row) & (lane < examples)).astype(jnp.bfloat16)
        for block, value in info.items()
    }

    def listed_flag(block, apart):
        return jnp.sum(jnp.where(lane == examples + apart, info[block], 0.0), axis=1, keepdims=True)

    pad = jnp.zeros((LANES - examples, LANES), jnp.float32)
    groups = {}
    for at, pair in pairs:
        one, two, apart = PAIRS[pair]
        if one == XC:
            two_leads = core == 0
        elif two in (XS, XC):
            two_leads = side == 0
        else:
            two_leads = side == 1
        flag = jnp.where(two_leads, listed_flag(two, apart), listed_flag(one, apart))
        if pair in ONLY:
            flag = jnp.where(mirrored == ONLY[pair], flag, 0.0)
        tile = jnp.concatenate([tiles[at], pad], axis=0) * (flag * factor)
        groups.setdefault(one, []).append((two, *two_parts(tile)))
    total = {}

    def add(block, term):
        total[block] = total[block] + term if block in total else term

    for one, group in groups.items():
        others = side_by_side([hot[two] for two, _, _ in group])
        highs = side_by_side([high for _, high, _ in group])
        lows = side_by_side([low for _, _, low in group])
        add(one, lax.dot_general(
            side_by_side([others, others]), side_by_side([highs, lows]), NT,
            preferred_element_type=jnp.float32,
        ))
        columns_of = lax.dot_general(
            side_by_side([hot[one], hot[one]]), jnp.concatenate([highs, lows], axis=0), NN,
            preferred_element_type=jnp.float32,
        )
        for at, (two, _, _) in enumerate(group):
            add(two, columns_of[:, at * LANES:(at + 1) * LANES])
    return total


def copies_of(loads, sems):
    return {
        key: pltpu.make_async_copy(source, target, sems.at[at])
        for at, (key, (source, target)) in enumerate(loads.items())
    }


def start(copies, *keys):
    for key in keys:
        copies[key].start()


def wait(copies, *keys):
    for key in keys:
        copies[key].wait()


def info_row(notes, block):
    return notes[block].astype(jnp.float32)[:1]


def columns(ref, at, width):
    return ref.at[:, pl.ds(pl.multiple_of(at, LANES), width)]


def same_one_kernel(factor, xs, acts, x_half, ys, zs, gram, cross_gram, out, notes,
                    held, own_v, half_v, gram_v, inner, sums, sems):
    rows, width = inner.shape[1], held.shape[2]
    quarter = acts.shape[1] // 4
    core, side = position()
    mirrored = core ^ side
    in_half = (1 - side) * quarter
    half_at = core * 2 * quarter
    copies = copies_of({
        XS: (xs, held.at[XS]),
        XC: (columns(x_half, in_half, width), held.at[XC]),
        YS: (ys, held.at[YS]),
        ZS: (zs, held.at[ZS]),
        "g0": (gram.at[0], gram_v.at[0]),
        "g1": (gram.at[1], gram_v.at[1]),
        "g2": (cross_gram.at[3], gram_v.at[2]),
        "own": (columns(acts, half_at, 2 * quarter), own_v),
        "half": (x_half.at[:, :2 * quarter], half_v),
        "g3": (gram.at[2], gram_v.at[3]),
    }, sems)
    start(copies, YS, XS, ZS, "g0", XC, "g1", "g2", "own", "half", "g3")
    wait(copies, YS, XS)
    product(held.at[YS], held.at[XS], inner.at[0])
    wait(copies, "g0", ZS)
    product(held.at[YS], held.at[ZS], inner.at[1])
    token_sums(inner.at[0], gram_v.at[0], sums.at[0])
    wait(copies, "g1", XC, "g2")
    product(held.at[YS], held.at[XC], inner.at[0])
    token_sums(inner.at[1], gram_v.at[1], sums.at[1])
    wait(copies, "own", "half")
    product(half_v, own_v, inner.at[1])
    token_sums(inner.at[0], gram_v.at[2], sums.at[2])
    wait(copies, "g3")
    token_sums(inner.at[1], gram_v.at[3], sums.at[3], ordered=False)
    notes[...] = jnp.zeros_like(notes)
    for block in (XS, XC, YS, ZS):
        notes[block] = held[block, rows:, :LANES]
    info = {block: info_row(notes, block) for block in (XS, XC, YS, ZS)}
    total = domain_sums(tuple(enumerate(FIRST)), factor, (mirrored, core, side), info, sums)
    out[...] = jnp.zeros_like(out)
    for block, value in total.items():
        out[block] = value


def same_two_kernel(factor, quarter, at, notes, earlier, xs, x_half, ys, zs, gram, cross_gram, out,
                    held, notes_v, earlier_v, gram_v, inner, sums, sems):
    rows, width = inner.shape[1], held.shape[2]
    core, side = position()
    mirrored = core ^ side
    in_half = (1 - side) * quarter
    copies = copies_of({
        XS: (xs, held.at[XS, :rows]),
        XC: (columns(x_half, in_half + at, width), held.at[XC]),
        YS: (ys, held.at[YS, :rows]),
        ZS: (zs, held.at[ZS, :rows]),
        "g0": (gram.at[0], gram_v.at[0]),
        "g1": (gram.at[1], gram_v.at[1]),
        "g2": (cross_gram.at[3], gram_v.at[2]),
        "notes": (notes, notes_v),
        "earlier": (earlier, earlier_v),
    }, sems)
    start(copies, YS, XS, ZS, "g0", "g1", XC, "g2", "notes", "earlier")
    wait(copies, YS, XS)
    product(held.at[YS], held.at[XS], inner.at[0])
    wait(copies, ZS, "g0")
    product(held.at[YS], held.at[ZS], inner.at[1])
    token_sums(inner.at[0], gram_v.at[0], sums.at[0])
    wait(copies, "g1", XC, "g2", "notes", "earlier")
    product(held.at[YS], held.at[XC], inner.at[0])
    token_sums(inner.at[1], gram_v.at[1], sums.at[1])
    token_sums(inner.at[0], gram_v.at[2], sums.at[2])
    info = {block: info_row(notes_v, block) for block in (XS, XC, YS, ZS)}
    pairs = ((0, 0), (1, 1), (2, 2))
    total = domain_sums(pairs, factor, (mirrored, core, side), info, sums)
    out[...] = earlier_v[...]
    for block, value in total.items():
        out[block] = earlier_v[block] + value


def position():
    me = lax.axis_index("ex")
    return me & 1, lax.shift_right_logical(me, 1) & 1


def cross_kernel(factor, quarter, at, notes, earlier, *refs):
    (xs, x_half, ys, yc, zs, zc, gram), refs = refs[:7], refs[7:]
    outs, (held, notes_v, earlier_v, gram_v, inner, sums, sems) = refs[:-7], refs[-7:]
    rows, width = inner.shape[1], held.shape[2]
    core, side = position()
    mirrored = core ^ side
    in_half = (1 - side) * quarter
    copies = copies_of({
        XS: (xs, held.at[XS, :xs.shape[0]]),
        XC: (columns(x_half, in_half + at, width), held.at[XC]),
        YS: (ys, held.at[YS, :ys.shape[0]]),
        YC: (yc, held.at[YC, :yc.shape[0]]),
        ZS: (zs, held.at[ZS, :zs.shape[0]]),
        ZC: (zc, held.at[ZC, :zc.shape[0]]),
        "g4": (gram.at[0], gram_v.at[0]),
        "g5": (gram.at[1], gram_v.at[1]),
        "g6": (gram.at[2], gram_v.at[2]),
        "g2": (gram.at[3], gram_v.at[3]),
        "notes": (notes, notes_v),
        "earlier": (earlier, earlier_v),
    }, sems)

    def on_one(act, key):
        pl.when(mirrored == 1)(lambda: act(copies, key))

    def on_zero(act, key):
        pl.when(mirrored == 0)(lambda: act(copies, key))

    start(copies, YC, XC, ZC, "g4")
    on_one(start, YS)
    on_zero(start, ZS)
    start(copies, "g5")
    on_one(start, XS)
    start(copies, "g6")
    on_one(start, "g2")
    start(copies, "notes", "earlier")
    wait(copies, YC, XC)
    product(held.at[YC], held.at[XC], inner.at[0])
    wait(copies, ZC)
    product(held.at[YC], held.at[ZC], inner.at[1])
    wait(copies, "g4")
    on_one(wait, YS)
    on_zero(wait, ZS)
    token_sums(inner.at[0], gram_v.at[0], sums.at[0])
    product(held.at[jnp.where(mirrored == 0, YC, YS)], held.at[jnp.where(mirrored == 0, ZS, ZC)], inner.at[0])
    wait(copies, "g5")
    token_sums(inner.at[1], gram_v.at[1], sums.at[1])
    wait(copies, "g6", "notes", "earlier")

    @pl.when(mirrored == 1)
    def _():
        wait(copies, XS, "g2")
        product(held.at[YC], held.at[XS], inner.at[1])
        token_sums(inner.at[0], gram_v.at[2], sums.at[2])
        token_sums(inner.at[1], gram_v.at[3], sums.at[3])

    @pl.when(mirrored == 0)
    def _():
        token_sums(inner.at[0], gram_v.at[2], sums.at[2])
        sums[3] = jnp.zeros(sums.shape[1:], jnp.float32)

    if at == 0:
        total_out, notes_out = outs
        for block in (YC, ZC):
            notes_v[block] = held[block, rows:, :LANES]
        notes_out[...] = notes_v[...]
    info = {block: info_row(notes_v, block) for block in range(6)}
    pairs = ((0, 4), (1, 5), (2, 6), (2, 7), (3, 8))
    total = domain_sums(pairs, factor, (mirrored, core, side), info, sums)
    examples = sums.shape[1]
    for block, value in total.items():
        value = value + earlier_v[block]
        if at == 0:
            total_out[block] = value
        else:
            outs[block][...] = value[:, :examples]


def per_device(acts, grads, domain, listed):
    rows, width = acts.shape
    examples = rows // TOK
    quarter = width // 4
    me = lax.axis_index("ex")
    core = me % 2
    side = (me // 2) % 2
    mirrored = core ^ side

    pair_of = [
        [pair for pair in range(len(PAIRS)) if SLOT[pair] == slot] for slot in range(SLOTS)
    ]

    def listing(end):
        return [
            PAIRS[pairs[0]][end] if len(pairs) == 1 else jnp.where(
                mirrored == ONLY[pairs[0]], PAIRS[pairs[0]][end], PAIRS[pairs[1]][end])
            for pairs in pair_of
        ]

    table = jnp.stack([jnp.asarray(block, jnp.int32) for block in listing(0) + listing(1)])
    places = jnp.stack([core * 2 + side, core * 2 + (1 - side)]).astype(jnp.int32)
    cross_places = jnp.stack([(1 - core) * 2 + side, (1 - core) * 2 + (1 - side)]).astype(jnp.int32)
    half_place = jnp.stack([1 - core]).astype(jnp.int32)

    own_info = jnp.concatenate(
        [domain, listed[0], jnp.zeros((LANES - examples - 2,), jnp.int32)]
    )
    own_info = jnp.broadcast_to(own_info.astype(acts.dtype)[None, :], (INFO, LANES))

    grads_ys = send(grads, across, 0)
    grads_zs = send(grads, along, 0)
    cut_ys, cut_zs, cut_ys_two, cut_zs_two = cut(acts, own_info, places)
    own_info, _ = lax.optimization_barrier((own_info, cut_ys))
    cut_yc, cut_zc, cut_yc_two, cut_zc_two = cut(acts, own_info, cross_places)
    own_info, _ = lax.optimization_barrier((own_info, cut_yc))
    ys_one = send(cut_ys, across, 0)
    zs_one = send(cut_zs, along, 0)
    ys_two = send(cut_ys_two, across, 0)
    yc_one = send(cut_yc, across, 1)
    zc_one = send(cut_zc, along, 1)

    def exchange(*values):
        return lax.cond(
            listed[0, 0] < 2,
            lambda *sent: tuple(send(value, stay, 1) for value in sent),
            lambda *sent: tuple(jnp.zeros_like(value) for value in sent),
            *values,
        )

    x_half, = exchange(cut_half(acts, grads, own_info, half_place))
    grads_ys, grads_zs, x_half = lax.optimization_barrier((grads_ys, grads_zs, x_half))
    grads_yc, grads_zc = exchange(grads_ys, grads_zs)
    factor = 1.0 / (TOK * math.sqrt(width * grads.shape[1]))

    gram, cross_gram = grams(table, grads, x_half, grads_ys, grads_yc, grads_zs, grads_zc)
    cut_zs_two, cut_yc_two, gram = lax.optimization_barrier((cut_zs_two, cut_yc_two, gram))
    zs_two = send(cut_zs_two, along, 0)
    yc_two = send(cut_yc_two, across, 1)

    vmem = pl.BlockSpec(memory_space=pltpu.VMEM)
    hbm = pl.BlockSpec(memory_space=pl.ANY)
    all_sums = jax.ShapeDtypeStruct((6, DOMAINS, LANES), jnp.float32)
    all_notes = jax.ShapeDtypeStruct((6, INFO, LANES), acts.dtype)
    notes_v = pltpu.VMEM(all_notes.shape, acts.dtype)
    sums_v = pltpu.VMEM(all_sums.shape, jnp.float32)

    def call(kernel, name, vmem_bytes, width, extra, operands, out_shape):
        return pl.pallas_call(
            kernel,
            in_specs=[hbm] * len(operands),
            out_specs=[vmem] * len(out_shape),
            out_shape=out_shape,
            scratch_shapes=[pltpu.VMEM((6, rows + INFO, width), acts.dtype)] + extra + [
                pltpu.VMEM((4, rows, rows), jnp.float32),
                pltpu.VMEM((2, rows, rows), jnp.float32),
                pltpu.VMEM((4, examples, rows), jnp.float32),
                pltpu.SemaphoreType.DMA((12,)),
            ],
            compiler_params=pltpu.CompilerParams(vmem_limit_bytes=vmem_bytes),
            cost_estimate=SMALL,
            name=name,
        )(*operands)

    one, two = chunks(quarter)
    extra = [
        pltpu.VMEM((rows, 2 * quarter), acts.dtype),
        pltpu.VMEM((rows + INFO, 2 * quarter), acts.dtype),
    ]
    partial = functools.partial
    sums, notes = call(
        partial(same_one_kernel, factor), "same_one", VMEM_BYTES, one, extra,
        (cut_zs, acts, x_half, ys_one, zs_one, gram, cross_gram), [all_sums, all_notes],
    )
    cut_zc_two, sums = lax.optimization_barrier((cut_zc_two, sums))
    zc_two = send(cut_zc_two, along, 1)
    extra = [notes_v, sums_v]
    sums, notes = call(
        partial(cross_kernel, factor, quarter, 0), "cross_one", LAST_VMEM_BYTES, one, extra,
        (notes, sums, cut_zs, x_half, ys_one, yc_one, zs_one, zc_one, cross_gram), [all_sums, all_notes],
    )
    sums, = call(
        partial(same_two_kernel, factor, quarter, one), "same_two", LAST_VMEM_BYTES, two, extra,
        (notes, sums, cut_zs_two, x_half, ys_two, zs_two, gram, cross_gram), [all_sums],
    )
    sums = call(
        partial(cross_kernel, factor, quarter, one), "cross_two", LAST_VMEM_BYTES, two, extra,
        (notes, sums, cut_zs_two, x_half, ys_two, yc_two, zs_two, zc_two, cross_gram),
        [jax.ShapeDtypeStruct((DOMAINS, examples), jnp.float32)] * 6,
    )

    total = sums[XS]
    total = total + send(sums[ZS], against, 0)
    total = total + send(sums[ZC], against, 1)
    total = total + send(sums[YS], across, 0)
    total = total + send(sums[YC], across, 1)
    total = total + send(sums[XC], stay, 1)
    return total.T


def solution(mesh):
    in_specs = (
        P(("groups", "ex"), None),
        P(("groups", "ex"), None),
        P(("groups", "ex")),
        P(("groups", "ex"), None),
    )
    out_specs = P(("groups", "ex"), None)
    return jax.shard_map(
        per_device, mesh=mesh, in_specs=in_specs, out_specs=out_specs, check_vma=False
    )
```

```python
import functools
import math

import jax
import jax.numpy as jnp
from jax import lax
from jax.experimental import pallas as pl
from jax.experimental.pallas import tpu as pltpu
from jax.sharding import PartitionSpec as P

TOK = 8
TOK_BITS = 3
DOMAINS = 48
LANES = 128
VMEM_BYTES = 63 * 1024 * 1024
LAST_VMEM_BYTES = 44 * 1024 * 1024

INFO = 16

XS, XC, YS, YC, ZS, ZC = range(6)
PAIRS = (
    (YS, XS, 1), (YS, ZS, 1), (YS, XC, 0), (XC, XS, 0),
    (YC, XC, 1), (YC, ZC, 1), (YC, ZS, 0), (YS, ZC, 0), (YC, XS, 0),
)
ONLY = {2: 0, 6: 0, 7: 1, 8: 1}
SLOT = (0, 1, 6, 2, 3, 4, 5, 5, 6)
SLOTS = 7
SAME_SLOTS = 3
FIRST = (0, 1, 2, 3)
SMALL = pl.CostEstimate(flops=1, bytes_accessed=1, transcendentals=0)
NT = (((1,), (1,)), ((), ()))
NN = (((1,), (0,)), ((), ()))


def across(chip):
    return chip ^ 1


def along(chip):
    return chip + 2 if chip & 1 else chip - 2


def against(chip):
    return chip - 2 if chip & 1 else chip + 2


def stay(chip):
    return chip


def send(value, move, flip):
    chips = lax.axis_size("ex") // 2
    pairs = [
        (2 * chip + core, 2 * (move(chip) % chips) + (core ^ flip))
        for chip in range(chips)
        for core in range(2)
    ]
    return lax.ppermute(value, "ex", pairs)


def token_major(rows):
    to = lax.broadcasted_iota(jnp.int32, (rows, rows), 0)
    source = lax.broadcasted_iota(jnp.int32, (rows, rows), 1)
    examples = rows // TOK
    place = (source & (TOK - 1)) * examples + lax.shift_right_logical(source, TOK_BITS)
    return (place == to).astype(jnp.bfloat16)


def reorder(order, block):
    return jnp.dot(order, block, preferred_element_type=jnp.float32).astype(jnp.bfloat16)


def put(target, value, info):
    rows = value.shape[0]
    target[:rows, :] = value
    target[rows:, :] = jnp.concatenate([info[...]] * (target.shape[1] // LANES), axis=1)


def chunks(quarter):
    second = quarter // LANES * 3 // 10 * LANES
    return quarter - second, second


def cut_kernel(places, info, y_acts, z_acts, y_one, z_one, y_two, z_two, order):
    rows, split = order.shape[0], y_one.shape[1]
    order[...] = token_major(rows)
    put(y_one, reorder(order[...], y_acts[:, :split]), info)
    put(z_one, z_acts[:, :split], info)
    y_two[...] = reorder(order[...], y_acts[:, split:])
    z_two[...] = z_acts[:, split:]


def cut(acts, info, places):
    rows, width = acts.shape
    quarter = width // 4
    one, two = chunks(quarter)
    shapes = [(rows + INFO, one)] * 2 + [(rows, two)] * 2
    return pl.pallas_call(
        cut_kernel,
        grid_spec=pltpu.PrefetchScalarGridSpec(
            num_scalar_prefetch=1,
            grid=(1,),
            in_specs=[
                pl.BlockSpec((INFO, LANES), lambda i, p: (0, 0)),
                pl.BlockSpec((rows, quarter), lambda i, p: (0, p[0])),
                pl.BlockSpec((rows, quarter), lambda i, p: (0, p[1])),
            ],
            out_specs=[pl.BlockSpec(shape, lambda i, p: (0, 0)) for shape in shapes],
            scratch_shapes=[pltpu.VMEM((rows, rows), jnp.bfloat16)],
        ),
        out_shape=[jax.ShapeDtypeStruct(shape, acts.dtype) for shape in shapes],
        compiler_params=pltpu.CompilerParams(vmem_limit_bytes=VMEM_BYTES),
        cost_estimate=SMALL,
        name="cut",
    )(places, info, acts, acts)


def half_kernel(steps, place, info, acts, grads, out):
    @pl.when(pl.program_id(0) < steps)
    def _():
        put(out, acts[...], info)

    @pl.when(pl.program_id(0) >= steps)
    def _():
        put(out, grads[...], info)


def cut_half(acts, grads, info, place):
    rows, width = acts.shape
    half, depth = width // 2, grads.shape[1]
    step = math.gcd(math.gcd(half, depth), 512)
    steps = half // step
    return pl.pallas_call(
        functools.partial(half_kernel, steps),
        grid_spec=pltpu.PrefetchScalarGridSpec(
            num_scalar_prefetch=1,
            grid=(steps + depth // step,),
            in_specs=[
                pl.BlockSpec((INFO, LANES), lambda i, p: (0, 0)),
                pl.BlockSpec((rows, step), lambda i, p: (0, p[0] * steps + jnp.minimum(i, steps - 1))),
                pl.BlockSpec((rows, step), lambda i, p: (0, jnp.maximum(i - steps, 0))),
            ],
            out_specs=pl.BlockSpec((rows + INFO, step), lambda i, p: (0, i)),
        ),
        out_shape=jax.ShapeDtypeStruct((rows + INFO, half + depth), acts.dtype),
        compiler_params=pltpu.CompilerParams(vmem_limit_bytes=VMEM_BYTES),
        cost_estimate=SMALL,
        name="half",
    )(place, info, acts, grads)


def grams_kernel(table, xs, xc, ys, yc, zs, zc, same, cross, held, result, in_sems, out_sems):
    rows, depth = xs.shape
    order = token_major(rows)
    sources = (xs, xc.at[:rows, xc.shape[1] - depth:], ys, yc, zs, zc)
    loads = [
        pltpu.make_async_copy(source, held.at[at], in_sems.at[at])
        for at, source in enumerate(sources)
    ]
    for load in loads:
        load.start()
    for load in loads:
        load.wait()
    for block in (YS, YC):
        held[block] = reorder(order, held[block])

    def leave(slot, array, at):
        return pltpu.make_async_copy(result.at[slot], array.at[at], out_sems.at[slot])

    @pl.loop(0, SLOTS)
    def _(slot):
        result[slot] = lax.dot_general(
            held[table[slot]], held[table[SLOTS + slot]], NT, preferred_element_type=jnp.float32
        )

        @pl.when(slot < SAME_SLOTS)
        def _():
            leave(slot, same, slot).start()

        @pl.when(slot >= SAME_SLOTS)
        def _():
            leave(slot, cross, slot - SAME_SLOTS).start()

    for slot in range(SLOTS):
        array, at = (same, slot) if slot < SAME_SLOTS else (cross, slot - SAME_SLOTS)
        leave(slot, array, at).wait()


def grams(table, grads, *messages):
    rows, width = grads.shape
    return pl.pallas_call(
        grams_kernel,
        in_specs=[pl.BlockSpec(memory_space=pltpu.SMEM)] + [pl.BlockSpec(memory_space=pl.ANY)] * 6,
        out_specs=[pl.BlockSpec(memory_space=pl.ANY)] * 2,
        out_shape=[
            jax.ShapeDtypeStruct((count, rows, rows), jnp.float32)
            for count in (SAME_SLOTS, SLOTS - SAME_SLOTS)
        ],
        scratch_shapes=[
            pltpu.VMEM((6, rows, width), grads.dtype),
            pltpu.VMEM((SLOTS, rows, rows), jnp.float32),
            pltpu.SemaphoreType.DMA((6,)),
            pltpu.SemaphoreType.DMA((SLOTS,)),
        ],
        compiler_params=pltpu.CompilerParams(vmem_limit_bytes=VMEM_BYTES),
        cost_estimate=SMALL,
        name="grams",
    )(table, grads, *messages)


def product(one, two, inner):
    rows = inner.shape[0]
    inner[...] = lax.dot_general(
        one[:rows, :], two[:rows, :], NT, preferred_element_type=jnp.float32
    )


def token_sums(inner, gram, sums, ordered=True):
    examples, rows = sums.shape
    if ordered:
        sums[...] = sum(
            inner[at:at + examples, :] * gram[at:at + examples, :]
            for at in range(0, rows, examples)
        )
    else:
        weighted = inner[...] * gram[...]
        sums[...] = weighted.reshape(examples, TOK, rows).sum(axis=1)


def two_parts(value):
    high = value.astype(jnp.bfloat16)
    return high, (value - high.astype(jnp.float32)).astype(jnp.bfloat16)


def dot_parts(value, table):
    high, low = two_parts(value)
    return lax.dot_general(low, table, NT, preferred_element_type=jnp.float32) + lax.dot_general(
        high, table, NT, preferred_element_type=jnp.float32
    )


def side_by_side(values):
    return jnp.concatenate(values, axis=1)


def domain_sums(pairs, factor, place, info, sums):
    count, examples, rows = sums.shape
    example = lax.broadcasted_iota(jnp.int32, (LANES, rows), 0)
    column = lax.broadcasted_iota(jnp.int32, (LANES, rows), 1)
    gather = (lax.shift_right_logical(column, TOK_BITS) == example).astype(jnp.bfloat16)
    tiles = dot_parts(sums[...].reshape(count * examples, rows), gather)
    tiles = tiles.reshape(count, examples, LANES)
    mirrored, core, side = place
    lane = lax.broadcasted_iota(jnp.int32, (1, LANES), 1)
    row = lax.broadcasted_iota(jnp.int32, (DOMAINS, LANES), 0)
    hot = {
        block: ((value.astype(jnp.int32) == row) & (lane < examples)).astype(jnp.bfloat16)
        for block, value in info.items()
    }

    def listed_flag(block, apart):
        return jnp.sum(jnp.where(lane == examples + apart, info[block], 0.0), axis=1, keepdims=True)

    pad = jnp.zeros((LANES - examples, LANES), jnp.float32)
    groups = {}
    for at, pair in pairs:
        one, two, apart = PAIRS[pair]
        if one == XC:
            two_leads = core == 0
        elif two in (XS, XC):
            two_leads = side == 0
        else:
            two_leads = side == 1
        flag = jnp.where(two_leads, listed_flag(two, apart), listed_flag(one, apart))
        if pair in ONLY:
            flag = jnp.where(mirrored == ONLY[pair], flag, 0.0)
        tile = jnp.concatenate([tiles[at], pad], axis=0) * (flag * factor)
        groups.setdefault(one, []).append((two, *two_parts(tile)))
    total = {}

    def add(block, term):
        total[block] = total[block] + term if block in total else term

    for one, group in groups.items():
        others = side_by_side([hot[two] for two, _, _ in group])
        highs = side_by_side([high for _, high, _ in group])
        lows = side_by_side([low for _, _, low in group])
        add(one, lax.dot_general(
            side_by_side([others, others]), side_by_side([highs, lows]), NT,
            preferred_element_type=jnp.float32,
        ))
        columns_of = lax.dot_general(
            side_by_side([hot[one], hot[one]]), jnp.concatenate([highs, lows], axis=0), NN,
            preferred_element_type=jnp.float32,
        )
        for at, (two, _, _) in enumerate(group):
            add(two, columns_of[:, at * LANES:(at + 1) * LANES])
    return total


def copies_of(loads, sems):
    return {
        key: pltpu.make_async_copy(source, target, sems.at[at])
        for at, (key, (source, target)) in enumerate(loads.items())
    }


def start(copies, *keys):
    for key in keys:
        copies[key].start()


def wait(copies, *keys):
    for key in keys:
        copies[key].wait()


def info_row(notes, block):
    return notes[block].astype(jnp.float32)[:1]


def columns(ref, at, width):
    return ref.at[:, pl.ds(pl.multiple_of(at, LANES), width)]


def same_one_kernel(factor, xs, acts, x_half, ys, zs, gram, cross_gram, out, notes,
                    held, own_v, half_v, gram_v, inner, sums, sems):
    rows, width = inner.shape[1], held.shape[2]
    quarter = acts.shape[1] // 4
    core, side = position()
    mirrored = core ^ side
    in_half = (1 - side) * quarter
    half_at = core * 2 * quarter
    copies = copies_of({
        XS: (xs, held.at[XS]),
        XC: (columns(x_half, in_half, width), held.at[XC]),
        YS: (ys, held.at[YS]),
        ZS: (zs, held.at[ZS]),
        "g0": (gram.at[0], gram_v.at[0]),
        "g1": (gram.at[1], gram_v.at[1]),
        "g2": (cross_gram.at[3], gram_v.at[2]),
        "own": (columns(acts, half_at, 2 * quarter), own_v),
        "half": (x_half.at[:, :2 * quarter], half_v),
        "g3": (gram.at[2], gram_v.at[3]),
    }, sems)
    start(copies, YS, XS, ZS, "g0", XC, "g1", "g2", "own", "half", "g3")
    wait(copies, YS, XS)
    product(held.at[YS], held.at[XS], inner.at[0])
    wait(copies, "g0", ZS)
    product(held.at[YS], held.at[ZS], inner.at[1])
    token_sums(inner.at[0], gram_v.at[0], sums.at[0])
    wait(copies, "g1", XC, "g2")
    product(held.at[YS], held.at[XC], inner.at[0])
    token_sums(inner.at[1], gram_v.at[1], sums.at[1])
    wait(copies, "own", "half")
    product(half_v, own_v, inner.at[1])
    token_sums(inner.at[0], gram_v.at[2], sums.at[2])
    wait(copies, "g3")
    token_sums(inner.at[1], gram_v.at[3], sums.at[3], ordered=False)
    notes[...] = jnp.zeros_like(notes)
    for block in (XS, XC, YS, ZS):
        notes[block] = held[block, rows:, :LANES]
    info = {block: info_row(notes, block) for block in (XS, XC, YS, ZS)}
    total = domain_sums(tuple(enumerate(FIRST)), factor, (mirrored, core, side), info, sums)
    out[...] = jnp.zeros_like(out)
    for block, value in total.items():
        out[block] = value


def same_two_kernel(factor, quarter, at, notes, earlier, xs, x_half, ys, zs, gram, cross_gram, out,
                    held, notes_v, earlier_v, gram_v, inner, sums, sems):
    rows, width = inner.shape[1], held.shape[2]
    core, side = position()
    mirrored = core ^ side
    in_half = (1 - side) * quarter
    copies = copies_of({
        XS: (xs, held.at[XS, :rows]),
        XC: (columns(x_half, in_half + at, width), held.at[XC]),
        YS: (ys, held.at[YS, :rows]),
        ZS: (zs, held.at[ZS, :rows]),
        "g0": (gram.at[0], gram_v.at[0]),
        "g1": (gram.at[1], gram_v.at[1]),
        "g2": (cross_gram.at[3], gram_v.at[2]),
        "notes": (notes, notes_v),
        "earlier": (earlier, earlier_v),
    }, sems)
    start(copies, YS, XS, ZS, "g0", "g1", XC, "g2", "notes", "earlier")
    wait(copies, YS, XS)
    product(held.at[YS], held.at[XS], inner.at[0])
    wait(copies, ZS, "g0")
    product(held.at[YS], held.at[ZS], inner.at[1])
    token_sums(inner.at[0], gram_v.at[0], sums.at[0])
    wait(copies, "g1", XC, "g2", "notes", "earlier")
    product(held.at[YS], held.at[XC], inner.at[0])
    token_sums(inner.at[1], gram_v.at[1], sums.at[1])
    token_sums(inner.at[0], gram_v.at[2], sums.at[2])
    info = {block: info_row(notes_v, block) for block in (XS, XC, YS, ZS)}
    pairs = ((0, 0), (1, 1), (2, 2))
    total = domain_sums(pairs, factor, (mirrored, core, side), info, sums)
    out[...] = earlier_v[...]
    for block, value in total.items():
        out[block] = earlier_v[block] + value


def position():
    me = lax.axis_index("ex")
    return me & 1, lax.shift_right_logical(me, 1) & 1


def cross_kernel(factor, quarter, at, notes, earlier, *refs):
    (xs, x_half, ys, yc, zs, zc, gram), refs = refs[:7], refs[7:]
    outs, (held, notes_v, earlier_v, gram_v, inner, sums, sems) = refs[:-7], refs[-7:]
    rows, width = inner.shape[1], held.shape[2]
    core, side = position()
    mirrored = core ^ side
    in_half = (1 - side) * quarter
    copies = copies_of({
        XS: (xs, held.at[XS, :xs.shape[0]]),
        XC: (columns(x_half, in_half + at, width), held.at[XC]),
        YS: (ys, held.at[YS, :ys.shape[0]]),
        YC: (yc, held.at[YC, :yc.shape[0]]),
        ZS: (zs, held.at[ZS, :zs.shape[0]]),
        ZC: (zc, held.at[ZC, :zc.shape[0]]),
        "g4": (gram.at[0], gram_v.at[0]),
        "g5": (gram.at[1], gram_v.at[1]),
        "g6": (gram.at[2], gram_v.at[2]),
        "g2": (gram.at[3], gram_v.at[3]),
        "notes": (notes, notes_v),
        "earlier": (earlier, earlier_v),
    }, sems)

    def on_one(act, key):
        pl.when(mirrored == 1)(lambda: act(copies, key))

    def on_zero(act, key):
        pl.when(mirrored == 0)(lambda: act(copies, key))

    start(copies, YC, XC, ZC, "g4")
    on_one(start, YS)
    on_zero(start, ZS)
    start(copies, "g5")
    on_one(start, XS)
    start(copies, "g6")
    on_one(start, "g2")
    start(copies, "notes", "earlier")
    wait(copies, YC, XC)
    product(held.at[YC], held.at[XC], inner.at[0])
    wait(copies, ZC)
    product(held.at[YC], held.at[ZC], inner.at[1])
    wait(copies, "g4")
    on_one(wait, YS)
    on_zero(wait, ZS)
    token_sums(inner.at[0], gram_v.at[0], sums.at[0])
    product(held.at[jnp.where(mirrored == 0, YC, YS)], held.at[jnp.where(mirrored == 0, ZS, ZC)], inner.at[0])
    wait(copies, "g5")
    token_sums(inner.at[1], gram_v.at[1], sums.at[1])
    wait(copies, "g6", "notes", "earlier")

    @pl.when(mirrored == 1)
    def _():
        wait(copies, XS, "g2")
        product(held.at[YC], held.at[XS], inner.at[1])
        token_sums(inner.at[0], gram_v.at[2], sums.at[2])
        token_sums(inner.at[1], gram_v.at[3], sums.at[3])

    @pl.when(mirrored == 0)
    def _():
        token_sums(inner.at[0], gram_v.at[2], sums.at[2])
        sums[3] = jnp.zeros(sums.shape[1:], jnp.float32)

    if at == 0:
        total_out, notes_out = outs
        for block in (YC, ZC):
            notes_v[block] = held[block, rows:, :LANES]
        notes_out[...] = notes_v[...]
    info = {block: info_row(notes_v, block) for block in range(6)}
    pairs = ((0, 4), (1, 5), (2, 6), (2, 7), (3, 8))
    total = domain_sums(pairs, factor, (mirrored, core, side), info, sums)
    examples = sums.shape[1]
    for block, value in total.items():
        value = value + earlier_v[block]
        if at == 0:
            total_out[block] = value
        else:
            outs[block][...] = value[:, :examples]


def per_device(acts, grads, domain, listed):
    rows, width = acts.shape
    examples = rows // TOK
    quarter = width // 4
    me = lax.axis_index("ex")
    core = me % 2
    side = (me // 2) % 2
    mirrored = core ^ side

    pair_of = [
        [pair for pair in range(len(PAIRS)) if SLOT[pair] == slot] for slot in range(SLOTS)
    ]

    def listing(end):
        return [
            PAIRS[pairs[0]][end] if len(pairs) == 1 else jnp.where(
                mirrored == ONLY[pairs[0]], PAIRS[pairs[0]][end], PAIRS[pairs[1]][end])
            for pairs in pair_of
        ]

    table = jnp.stack([jnp.asarray(block, jnp.int32) for block in listing(0) + listing(1)])
    places = jnp.stack([core * 2 + side, core * 2 + (1 - side)]).astype(jnp.int32)
    cross_places = jnp.stack([(1 - core) * 2 + side, (1 - core) * 2 + (1 - side)]).astype(jnp.int32)
    half_place = jnp.stack([1 - core]).astype(jnp.int32)

    own_info = jnp.concatenate(
        [domain, listed[0], jnp.zeros((LANES - examples - 2,), jnp.int32)]
    )
    own_info = jnp.broadcast_to(own_info.astype(acts.dtype)[None, :], (INFO, LANES))

    grads_ys = send(grads, across, 0)
    grads_zs = send(grads, along, 0)
    cut_ys, cut_zs, cut_ys_two, cut_zs_two = cut(acts, own_info, places)
    own_info, _ = lax.optimization_barrier((own_info, cut_ys))
    cut_yc, cut_zc, cut_yc_two, cut_zc_two = cut(acts, own_info, cross_places)
    own_info, _ = lax.optimization_barrier((own_info, cut_yc))
    ys_one = send(cut_ys, across, 0)
    zs_one = send(cut_zs, along, 0)
    ys_two = send(cut_ys_two, across, 0)
    yc_one = send(cut_yc, across, 1)
    zc_one = send(cut_zc, along, 1)

    def exchange(*values):
        return lax.cond(
            listed[0, 0] < 2,
            lambda *sent: tuple(send(value, stay, 1) for value in sent),
            lambda *sent: tuple(jnp.zeros_like(value) for value in sent),
            *values,
        )

    x_half, = exchange(cut_half(acts, grads, own_info, half_place))
    grads_ys, grads_zs, x_half = lax.optimization_barrier((grads_ys, grads_zs, x_half))
    grads_yc, grads_zc = exchange(grads_ys, grads_zs)
    factor = 1.0 / (TOK * math.sqrt(width * grads.shape[1]))

    gram, cross_gram = grams(table, grads, x_half, grads_ys, grads_yc, grads_zs, grads_zc)
    cut_zs_two, cut_yc_two, gram = lax.optimization_barrier((cut_zs_two, cut_yc_two, gram))
    zs_two = send(cut_zs_two, along, 0)
    yc_two = send(cut_yc_two, across, 1)

    vmem = pl.BlockSpec(memory_space=pltpu.VMEM)
    hbm = pl.BlockSpec(memory_space=pl.ANY)
    all_sums = jax.ShapeDtypeStruct((6, DOMAINS, LANES), jnp.float32)
    all_notes = jax.ShapeDtypeStruct((6, INFO, LANES), acts.dtype)
    notes_v = pltpu.VMEM(all_notes.shape, acts.dtype)
    sums_v = pltpu.VMEM(all_sums.shape, jnp.float32)

    def call(kernel, name, vmem_bytes, width, extra, operands, out_shape):
        return pl.pallas_call(
            kernel,
            in_specs=[hbm] * len(operands),
            out_specs=[vmem] * len(out_shape),
            out_shape=out_shape,
            scratch_shapes=[pltpu.VMEM((6, rows + INFO, width), acts.dtype)] + extra + [
                pltpu.VMEM((4, rows, rows), jnp.float32),
                pltpu.VMEM((2, rows, rows), jnp.float32),
                pltpu.VMEM((4, examples, rows), jnp.float32),
                pltpu.SemaphoreType.DMA((12,)),
            ],
            compiler_params=pltpu.CompilerParams(vmem_limit_bytes=vmem_bytes),
            cost_estimate=SMALL,
            name=name,
        )(*operands)

    one, two = chunks(quarter)
    extra = [
        pltpu.VMEM((rows, 2 * quarter), acts.dtype),
        pltpu.VMEM((rows + INFO, 2 * quarter), acts.dtype),
    ]
    partial = functools.partial
    sums, notes = call(
        partial(same_one_kernel, factor), "same_one", VMEM_BYTES, one, extra,
        (cut_zs, acts, x_half, ys_one, zs_one, gram, cross_gram), [all_sums, all_notes],
    )
    cut_zc_two, sums = lax.optimization_barrier((cut_zc_two, sums))
    zc_two = send(cut_zc_two, along, 1)
    extra = [notes_v, sums_v]
    sums, notes = call(
        partial(cross_kernel, factor, quarter, 0), "cross_one", LAST_VMEM_BYTES, one, extra,
        (notes, sums, cut_zs, x_half, ys_one, yc_one, zs_one, zc_one, cross_gram), [all_sums, all_notes],
    )
    sums, = call(
        partial(same_two_kernel, factor, quarter, one), "same_two", LAST_VMEM_BYTES, two, extra,
        (notes, sums, cut_zs_two, x_half, ys_two, zs_two, gram, cross_gram), [all_sums],
    )
    sums = call(
        partial(cross_kernel, factor, quarter, one), "cross_two", LAST_VMEM_BYTES, two, extra,
        (notes, sums, cut_zs_two, x_half, ys_two, yc_two, zs_two, zc_two, cross_gram),
        [jax.ShapeDtypeStruct((DOMAINS, examples), jnp.float32)] * 6,
    )

    total = sums[XS]
    total = total + send(sums[ZS], against, 0)
    total = total + send(sums[ZC], against, 1)
    total = total + send(sums[YS], across, 0)
    total = total + send(sums[YC], across, 1)
    total = total + send(sums[XC], stay, 1)
    return total.T


def solution(mesh):
    in_specs = (
        P(("groups", "ex"), None),
        P(("groups", "ex"), None),
        P(("groups", "ex")),
        P(("groups", "ex"), None),
    )
    out_specs = P(("groups", "ex"), None)
    return jax.shard_map(
        per_device, mesh=mesh, in_specs=in_specs, out_specs=out_specs, check_vma=False
    )
```

```python
import functools
import math

import jax
import jax.numpy as jnp
from jax import lax
from jax.experimental import pallas as pl
from jax.experimental.pallas import tpu as pltpu
from jax.sharding import PartitionSpec as P

TOK = 8
TOK_BITS = 3
DOMAINS = 48
LANES = 128
VMEM_BYTES = 63 * 1024 * 1024
LAST_VMEM_BYTES = 44 * 1024 * 1024

INFO = 16

XS, XC, YS, YC, ZS, ZC = range(6)
PAIRS = (
    (YS, XS, 1), (YS, ZS, 1), (YS, XC, 0), (XC, XS, 0),
    (YC, XC, 1), (YC, ZC, 1), (YC, ZS, 0), (YS, ZC, 0), (YC, XS, 0),
)
ONLY = {2: 0, 6: 0, 7: 1, 8: 1}
SLOT = (0, 1, 2, 3, 4, 5, 6, 6, 2)
SLOTS = 7
FIRST = (0, 1, 2, 3)
SMALL = pl.CostEstimate(flops=1, bytes_accessed=1, transcendentals=0)
NT = (((1,), (1,)), ((), ()))
NN = (((1,), (0,)), ((), ()))


def across(chip):
    return chip ^ 1


def along(chip):
    return chip + 2 if chip & 1 else chip - 2


def against(chip):
    return chip - 2 if chip & 1 else chip + 2


def stay(chip):
    return chip


def send(value, move, flip):
    chips = lax.axis_size("ex") // 2
    pairs = [
        (2 * chip + core, 2 * (move(chip) % chips) + (core ^ flip))
        for chip in range(chips)
        for core in range(2)
    ]
    return lax.ppermute(value, "ex", pairs)


def token_major(rows):
    to = lax.broadcasted_iota(jnp.int32, (rows, rows), 0)
    source = lax.broadcasted_iota(jnp.int32, (rows, rows), 1)
    examples = rows // TOK
    place = (source & (TOK - 1)) * examples + lax.shift_right_logical(source, TOK_BITS)
    return (place == to).astype(jnp.bfloat16)


def reorder(order, block):
    return jnp.dot(order, block, preferred_element_type=jnp.float32).astype(jnp.bfloat16)


def put(target, value, info):
    rows = value.shape[0]
    target[:rows, :] = value
    target[rows:, :] = jnp.concatenate([info[...]] * (target.shape[1] // LANES), axis=1)


def chunks(quarter):
    second = quarter // LANES * 3 // 10 * LANES
    return quarter - second, second


def cut_kernel(places, info, y_acts, z_acts, y_one, z_one, y_two, z_two, order):
    rows, split = order.shape[0], y_one.shape[1]
    order[...] = token_major(rows)
    put(y_one, reorder(order[...], y_acts[:, :split]), info)
    put(z_one, z_acts[:, :split], info)
    y_two[...] = reorder(order[...], y_acts[:, split:])
    z_two[...] = z_acts[:, split:]


def cut(acts, info, places):
    rows, width = acts.shape
    quarter = width // 4
    one, two = chunks(quarter)
    shapes = [(rows + INFO, one)] * 2 + [(rows, two)] * 2
    return pl.pallas_call(
        cut_kernel,
        grid_spec=pltpu.PrefetchScalarGridSpec(
            num_scalar_prefetch=1,
            grid=(1,),
            in_specs=[
                pl.BlockSpec((INFO, LANES), lambda i, p: (0, 0)),
                pl.BlockSpec((rows, quarter), lambda i, p: (0, p[0])),
                pl.BlockSpec((rows, quarter), lambda i, p: (0, p[1])),
            ],
            out_specs=[pl.BlockSpec(shape, lambda i, p: (0, 0)) for shape in shapes],
            scratch_shapes=[pltpu.VMEM((rows, rows), jnp.bfloat16)],
        ),
        out_shape=[jax.ShapeDtypeStruct(shape, acts.dtype) for shape in shapes],
        compiler_params=pltpu.CompilerParams(vmem_limit_bytes=VMEM_BYTES),
        cost_estimate=SMALL,
        name="cut",
    )(places, info, acts, acts)


def half_kernel(steps, place, info, acts, grads, out):
    @pl.when(pl.program_id(0) < steps)
    def _():
        put(out, acts[...], info)

    @pl.when(pl.program_id(0) >= steps)
    def _():
        put(out, grads[...], info)


def cut_half(acts, grads, info, place):
    rows, width = acts.shape
    half, depth = width // 2, grads.shape[1]
    step = math.gcd(math.gcd(half, depth), 512)
    steps = half // step
    return pl.pallas_call(
        functools.partial(half_kernel, steps),
        grid_spec=pltpu.PrefetchScalarGridSpec(
            num_scalar_prefetch=1,
            grid=(steps + depth // step,),
            in_specs=[
                pl.BlockSpec((INFO, LANES), lambda i, p: (0, 0)),
                pl.BlockSpec((rows, step), lambda i, p: (0, p[0] * steps + jnp.minimum(i, steps - 1))),
                pl.BlockSpec((rows, step), lambda i, p: (0, jnp.maximum(i - steps, 0))),
            ],
            out_specs=pl.BlockSpec((rows + INFO, step), lambda i, p: (0, i)),
        ),
        out_shape=jax.ShapeDtypeStruct((rows + INFO, half + depth), acts.dtype),
        compiler_params=pltpu.CompilerParams(vmem_limit_bytes=VMEM_BYTES),
        cost_estimate=SMALL,
        name="half",
    )(place, info, acts, grads)


def grams_kernel(table, xs, xc, ys, yc, zs, zc, out, held, result, in_sems, out_sems):
    rows, depth = xs.shape
    order = token_major(rows)
    sources = (xs, xc.at[:rows, xc.shape[1] - depth:], ys, yc, zs, zc)
    loads = [
        pltpu.make_async_copy(source, held.at[at], in_sems.at[at])
        for at, source in enumerate(sources)
    ]
    for load in loads:
        load.start()
    for load in loads:
        load.wait()
    for block in (YS, YC):
        held[block] = reorder(order, held[block])

    def leave(slot):
        return pltpu.make_async_copy(result.at[slot], out.at[slot], out_sems.at[slot])

    @pl.loop(0, SLOTS)
    def _(slot):
        result[slot] = lax.dot_general(
            held[table[slot]], held[table[SLOTS + slot]], NT, preferred_element_type=jnp.float32
        )
        leave(slot).start()

    for slot in range(SLOTS):
        leave(slot).wait()


def grams(table, grads, *messages):
    rows, width = grads.shape
    return pl.pallas_call(
        grams_kernel,
        in_specs=[pl.BlockSpec(memory_space=pltpu.SMEM)] + [pl.BlockSpec(memory_space=pl.ANY)] * 6,
        out_specs=pl.BlockSpec(memory_space=pl.ANY),
        out_shape=jax.ShapeDtypeStruct((SLOTS, rows, rows), jnp.float32),
        scratch_shapes=[
            pltpu.VMEM((6, rows, width), grads.dtype),
            pltpu.VMEM((SLOTS, rows, rows), jnp.float32),
            pltpu.SemaphoreType.DMA((6,)),
            pltpu.SemaphoreType.DMA((SLOTS,)),
        ],
        compiler_params=pltpu.CompilerParams(vmem_limit_bytes=VMEM_BYTES),
        cost_estimate=SMALL,
        name="grams",
    )(table, grads, *messages)


def product(one, two, inner):
    rows = inner.shape[0]
    inner[...] = lax.dot_general(
        one[:rows, :], two[:rows, :], NT, preferred_element_type=jnp.float32
    )


def token_sums(inner, gram, sums, ordered=True):
    examples, rows = sums.shape
    if ordered:
        sums[...] = sum(
            inner[at:at + examples, :] * gram[at:at + examples, :]
            for at in range(0, rows, examples)
        )
    else:
        weighted = inner[...] * gram[...]
        sums[...] = weighted.reshape(examples, TOK, rows).sum(axis=1)


def two_parts(value):
    high = value.astype(jnp.bfloat16)
    return high, (value - high.astype(jnp.float32)).astype(jnp.bfloat16)


def dot_parts(value, table):
    high, low = two_parts(value)
    return lax.dot_general(low, table, NT, preferred_element_type=jnp.float32) + lax.dot_general(
        high, table, NT, preferred_element_type=jnp.float32
    )


def side_by_side(values):
    return jnp.concatenate(values, axis=1)


def tiles_of(sums):
    count, examples, rows = sums.shape
    example = lax.broadcasted_iota(jnp.int32, (LANES, rows), 0)
    column = lax.broadcasted_iota(jnp.int32, (LANES, rows), 1)
    gather = (lax.shift_right_logical(column, TOK_BITS) == example).astype(jnp.bfloat16)
    tiles = dot_parts(sums.reshape(count * examples, rows), gather)
    return tiles.reshape(count, examples, LANES)


def domain_sums(pairs, factor, place, info, tiles):
    examples = tiles[0].shape[0]
    mirrored, core, side = place
    lane = lax.broadcasted_iota(jnp.int32, (1, LANES), 1)
    row = lax.broadcasted_iota(jnp.int32, (DOMAINS, LANES), 0)
    hot = {
        block: ((value.astype(jnp.int32) == row) & (lane < examples)).astype(jnp.bfloat16)
        for block, value in info.items()
    }

    def listed_flag(block, apart):
        return jnp.sum(jnp.where(lane == examples + apart, info[block], 0.0), axis=1, keepdims=True)

    pad = jnp.zeros((LANES - examples, LANES), jnp.float32)
    groups = {}
    for at, pair in pairs:
        one, two, apart = PAIRS[pair]
        if one == XC:
            two_leads = core == 0
        elif two in (XS, XC):
            two_leads = side == 0
        else:
            two_leads = side == 1
        flag = jnp.where(two_leads, listed_flag(two, apart), listed_flag(one, apart))
        if pair in ONLY:
            flag = jnp.where(mirrored == ONLY[pair], flag, 0.0)
        tile = jnp.concatenate([tiles[at], pad], axis=0) * (flag * factor)
        groups.setdefault(one, []).append((two, *two_parts(tile)))
    total = {}

    def add(block, term):
        total[block] = total[block] + term if block in total else term

    for one, group in groups.items():
        others = side_by_side([hot[two] for two, _, _ in group])
        highs = side_by_side([high for _, high, _ in group])
        lows = side_by_side([low for _, _, low in group])
        add(one, lax.dot_general(
            side_by_side([others, others]), side_by_side([highs, lows]), NT,
            preferred_element_type=jnp.float32,
        ))
        columns_of = lax.dot_general(
            side_by_side([hot[one], hot[one]]), jnp.concatenate([highs, lows], axis=0), NN,
            preferred_element_type=jnp.float32,
        )
        for at, (two, _, _) in enumerate(group):
            add(two, columns_of[:, at * LANES:(at + 1) * LANES])
    return total


def copies_of(loads, sems):
    return {
        key: pltpu.make_async_copy(source, target, sems.at[at])
        for at, (key, (source, target)) in enumerate(loads.items())
    }


def start(copies, *keys):
    for key in keys:
        copies[key].start()


def wait(copies, *keys):
    for key in keys:
        copies[key].wait()


def info_row(notes, block):
    return notes[block].astype(jnp.float32)[:1]


def columns(ref, at, width):
    return ref.at[:, pl.ds(pl.multiple_of(at, LANES), width)]


def same_one_kernel(factor, own_info, acts, x_half, ys, zs, gram, out, notes,
                    held, own_v, half_v, gram_v, inner, sums, sems):
    rows, width = inner.shape[1], held.shape[2]
    quarter = acts.shape[1] // 4
    core, side = position()
    mirrored = core ^ side
    in_half = (1 - side) * quarter
    half_at = core * 2 * quarter
    copies = copies_of({
        XS: (columns(acts, half_at + in_half, width), held.at[XS, :rows]),
        XC: (columns(x_half, in_half, width), held.at[XC]),
        YS: (ys, held.at[YS]),
        ZS: (zs, held.at[ZS]),
        "g0": (gram.at[0], gram_v.at[0]),
        "g1": (gram.at[1], gram_v.at[1]),
        "g2": (gram.at[2], gram_v.at[2]),
        "own": (columns(acts, half_at, 2 * quarter), own_v),
        "half": (x_half.at[:, :2 * quarter], half_v),
        "g3": (gram.at[3], gram_v.at[3]),
        "info": (own_info, held.at[XS, rows:, :LANES]),
    }, sems)
    start(copies, YS, XS, "info", ZS, "g0", XC, "g1", "g2", "own", "half", "g3")
    wait(copies, YS, XS, "info")
    product(held.at[YS], held.at[XS], inner.at[0])
    wait(copies, "g0", ZS)
    product(held.at[YS], held.at[ZS], inner.at[1])
    token_sums(inner.at[0], gram_v.at[0], sums.at[0])
    wait(copies, "g1", XC, "g2")
    product(held.at[YS], held.at[XC], inner.at[0])
    token_sums(inner.at[1], gram_v.at[1], sums.at[1])
    wait(copies, "own", "half")
    product(half_v, own_v, inner.at[1])
    token_sums(inner.at[0], gram_v.at[2], sums.at[2])
    wait(copies, "g3")
    token_sums(inner.at[1], gram_v.at[3], sums.at[3], ordered=False)
    notes[...] = jnp.zeros_like(notes)
    for block in (XS, XC, YS, ZS):
        notes[block] = held[block, rows:, :LANES]
    info = {block: info_row(notes, block) for block in (XS, XC, YS, ZS)}
    total = domain_sums(tuple(enumerate(FIRST)), factor, (mirrored, core, side), info, tiles_of(sums[...]))
    out[...] = jnp.zeros_like(out)
    for block, value in total.items():
        out[block] = value


def same_two_kernel(factor, at, notes, earlier, acts, x_half, ys, zs, gram, out,
                    held, notes_v, earlier_v, gram_v, inner, sums, sems):
    rows, width = inner.shape[1], held.shape[2]
    quarter = acts.shape[1] // 4
    core, side = position()
    mirrored = core ^ side
    in_half = (1 - side) * quarter
    copies = copies_of({
        XS: (columns(acts, core * 2 * quarter + in_half + at, width), held.at[XS, :rows]),
        XC: (columns(x_half, in_half + at, width), held.at[XC]),
        YS: (ys, held.at[YS, :rows]),
        ZS: (zs, held.at[ZS, :rows]),
        "g0": (gram.at[0], gram_v.at[0]),
        "g1": (gram.at[1], gram_v.at[1]),
        "g2": (gram.at[2], gram_v.at[2]),
        "notes": (notes, notes_v),
        "earlier": (earlier, earlier_v),
    }, sems)
    start(copies, YS, XS, ZS, "g0", "g1", XC, "g2", "notes", "earlier")
    wait(copies, YS, XS)
    product(held.at[YS], held.at[XS], inner.at[0])
    wait(copies, ZS, "g0")
    product(held.at[YS], held.at[ZS], inner.at[1])
    token_sums(inner.at[0], gram_v.at[0], sums.at[0])
    wait(copies, "g1", XC, "g2", "notes", "earlier")
    product(held.at[YS], held.at[XC], inner.at[0])
    token_sums(inner.at[1], gram_v.at[1], sums.at[1])
    token_sums(inner.at[0], gram_v.at[2], sums.at[2])
    info = {block: info_row(notes_v, block) for block in (XS, XC, YS, ZS)}
    pairs = ((0, 0), (1, 1), (2, 2))
    total = domain_sums(pairs, factor, (mirrored, core, side), info, tiles_of(sums[...]))
    out[...] = earlier_v[...]
    for block, value in total.items():
        out[block] = earlier_v[block] + value


def position():
    me = lax.axis_index("ex")
    return me & 1, lax.shift_right_logical(me, 1) & 1


def cross_kernel(factor, at, notes, earlier, *refs):
    (acts, x_half, ys, yc, zs, zc, gram), refs = refs[:7], refs[7:]
    outs, (held, notes_v, earlier_v, gram_v, inner, sums, sems) = refs[:-7], refs[-7:]
    rows, width = inner.shape[1], held.shape[2]
    quarter = acts.shape[1] // 4
    core, side = position()
    mirrored = core ^ side
    in_half = (1 - side) * quarter
    work_at = core * 2 * quarter + in_half
    copies = copies_of({
        XS: (columns(acts, work_at + at, width), held.at[XS, :rows, :]),
        XC: (columns(x_half, in_half + at, width), held.at[XC]),
        YS: (ys, held.at[YS, :ys.shape[0]]),
        YC: (yc, held.at[YC, :yc.shape[0]]),
        ZS: (zs, held.at[ZS, :zs.shape[0]]),
        ZC: (zc, held.at[ZC, :zc.shape[0]]),
        "g4": (gram.at[4], gram_v.at[0]),
        "g5": (gram.at[5], gram_v.at[1]),
        "g6": (gram.at[6], gram_v.at[2]),
        "g2": (gram.at[2], gram_v.at[3]),
        "notes": (notes, notes_v),
        "earlier": (earlier, earlier_v),
    }, sems)
    start(copies, YC, XC, ZC, "g4", YS, ZS, "g5", XS, "g6", "g2", "notes", "earlier")
    wait(copies, YC, XC)
    product(held.at[YC], held.at[XC], inner.at[0])
    wait(copies, ZC)
    product(held.at[YC], held.at[ZC], inner.at[1])
    wait(copies, "g4", YS, ZS)
    token_sums(inner.at[0], gram_v.at[0], sums.at[0])
    product(held.at[jnp.where(mirrored == 0, YC, YS)], held.at[jnp.where(mirrored == 0, ZS, ZC)], inner.at[0])
    wait(copies, "g5", XS)
    token_sums(inner.at[1], gram_v.at[1], sums.at[1])
    wait(copies, "g6", "g2", "notes", "earlier")
    early = tiles_of(sums[0:2])

    @pl.when(mirrored == 1)
    def _():
        product(held.at[YC], held.at[XS], inner.at[1])
        token_sums(inner.at[0], gram_v.at[2], sums.at[2])
        token_sums(inner.at[1], gram_v.at[3], sums.at[3])

    @pl.when(mirrored == 0)
    def _():
        token_sums(inner.at[0], gram_v.at[2], sums.at[2])
        sums[3] = jnp.zeros(sums.shape[1:], jnp.float32)

    if at == 0:
        total_out, notes_out = outs
        for block in (YC, ZC):
            notes_v[block] = held[block, rows:, :LANES]
        notes_out[...] = notes_v[...]
    info = {block: info_row(notes_v, block) for block in range(6)}
    late = tiles_of(sums[2:4])
    tiles = early[0], early[1], late[0], late[1]
    pairs = ((0, 4), (1, 5), (2, 6), (2, 7), (3, 8))
    total = domain_sums(pairs, factor, (mirrored, core, side), info, tiles)
    examples = sums.shape[1]
    for block, value in total.items():
        value = value + earlier_v[block]
        if at == 0:
            total_out[block] = value
        else:
            outs[block][...] = value[:, :examples]


def per_device(acts, grads, domain, listed):
    rows, width = acts.shape
    examples = rows // TOK
    quarter = width // 4
    me = lax.axis_index("ex")
    core = me % 2
    side = (me // 2) % 2
    mirrored = core ^ side

    pair_of = [
        [pair for pair in range(len(PAIRS)) if SLOT[pair] == slot] for slot in range(SLOTS)
    ]

    def listing(end):
        return [
            PAIRS[pairs[0]][end] if len(pairs) == 1 else jnp.where(
                mirrored == ONLY[pairs[0]], PAIRS[pairs[0]][end], PAIRS[pairs[1]][end])
            for pairs in pair_of
        ]

    table = jnp.stack([jnp.asarray(block, jnp.int32) for block in listing(0) + listing(1)])
    places = jnp.stack([core * 2 + side, core * 2 + (1 - side)]).astype(jnp.int32)
    cross_places = jnp.stack([(1 - core) * 2 + side, (1 - core) * 2 + (1 - side)]).astype(jnp.int32)
    half_place = jnp.stack([1 - core]).astype(jnp.int32)

    own_info = jnp.concatenate(
        [domain, listed[0], jnp.zeros((LANES - examples - 2,), jnp.int32)]
    )
    own_info = jnp.broadcast_to(own_info.astype(acts.dtype)[None, :], (INFO, LANES))

    grads_ys = send(grads, across, 0)
    grads_zs = send(grads, along, 0)
    cut_ys, cut_zs, cut_ys_two, cut_zs_two = cut(acts, own_info, places)
    own_info, _ = lax.optimization_barrier((own_info, cut_ys))
    cut_yc, cut_zc, cut_yc_two, cut_zc_two = cut(acts, own_info, cross_places)
    own_info, _ = lax.optimization_barrier((own_info, cut_yc))
    ys_one = send(cut_ys, across, 0)
    zs_one = send(cut_zs, along, 0)
    ys_two = send(cut_ys_two, across, 0)
    yc_one = send(cut_yc, across, 1)
    zc_one = send(cut_zc, along, 1)

    def exchange(*values):
        return lax.cond(
            listed[0, 0] < 2,
            lambda *sent: tuple(send(value, stay, 1) for value in sent),
            lambda *sent: tuple(jnp.zeros_like(value) for value in sent),
            *values,
        )

    x_half, = exchange(cut_half(acts, grads, own_info, half_place))
    grads_ys, grads_zs, x_half = lax.optimization_barrier((grads_ys, grads_zs, x_half))
    grads_yc, grads_zc = exchange(grads_ys, grads_zs)
    factor = 1.0 / (TOK * math.sqrt(width * grads.shape[1]))

    gram = grams(table, grads, x_half, grads_ys, grads_yc, grads_zs, grads_zc)
    cut_zs_two, cut_yc_two, gram = lax.optimization_barrier((cut_zs_two, cut_yc_two, gram))
    zs_two = send(cut_zs_two, along, 0)
    yc_two = send(cut_yc_two, across, 1)

    vmem = pl.BlockSpec(memory_space=pltpu.VMEM)
    hbm = pl.BlockSpec(memory_space=pl.ANY)
    all_sums = jax.ShapeDtypeStruct((6, DOMAINS, LANES), jnp.float32)
    all_notes = jax.ShapeDtypeStruct((6, INFO, LANES), acts.dtype)
    notes_v = pltpu.VMEM(all_notes.shape, acts.dtype)
    sums_v = pltpu.VMEM(all_sums.shape, jnp.float32)

    def call(kernel, name, vmem_bytes, width, extra, operands, out_shape):
        return pl.pallas_call(
            kernel,
            in_specs=[hbm] * len(operands),
            out_specs=[vmem] * len(out_shape),
            out_shape=out_shape,
            scratch_shapes=[pltpu.VMEM((6, rows + INFO, width), acts.dtype)] + extra + [
                pltpu.VMEM((4, rows, rows), jnp.float32),
                pltpu.VMEM((2, rows, rows), jnp.float32),
                pltpu.VMEM((4, examples, rows), jnp.float32),
                pltpu.SemaphoreType.DMA((12,)),
            ],
            compiler_params=pltpu.CompilerParams(vmem_limit_bytes=vmem_bytes),
            cost_estimate=SMALL,
            name=name,
        )(*operands)

    one, two = chunks(quarter)
    extra = [
        pltpu.VMEM((rows, 2 * quarter), acts.dtype),
        pltpu.VMEM((rows + INFO, 2 * quarter), acts.dtype),
    ]
    partial = functools.partial
    sums, notes = call(
        partial(same_one_kernel, factor), "same_one", VMEM_BYTES, one, extra,
        (own_info, acts, x_half, ys_one, zs_one, gram), [all_sums, all_notes],
    )
    cut_zc_two, sums = lax.optimization_barrier((cut_zc_two, sums))
    zc_two = send(cut_zc_two, along, 1)
    extra = [notes_v, sums_v]
    sums, notes = call(
        partial(cross_kernel, factor, 0), "cross_one", LAST_VMEM_BYTES, one, extra,
        (notes, sums, acts, x_half, ys_one, yc_one, zs_one, zc_one, gram), [all_sums, all_notes],
    )
    sums, = call(
        partial(same_two_kernel, factor, one), "same_two", LAST_VMEM_BYTES, two, extra,
        (notes, sums, acts, x_half, ys_two, zs_two, gram), [all_sums],
    )
    sums = call(
        partial(cross_kernel, factor, one), "cross_two", LAST_VMEM_BYTES, two, extra,
        (notes, sums, acts, x_half, ys_two, yc_two, zs_two, zc_two, gram),
        [jax.ShapeDtypeStruct((DOMAINS, examples), jnp.float32)] * 6,
    )

    total = sums[XS]
    total = total + send(sums[ZS], against, 0)
    total = total + send(sums[ZC], against, 1)
    total = total + send(sums[YS], across, 0)
    total = total + send(sums[YC], across, 1)
    total = total + send(sums[XC], stay, 1)
    return total.T


def solution(mesh):
    in_specs = (
        P(("groups", "ex"), None),
        P(("groups", "ex"), None),
        P(("groups", "ex")),
        P(("groups", "ex"), None),
    )
    out_specs = P(("groups", "ex"), None)
    return jax.shard_map(
        per_device, mesh=mesh, in_specs=in_specs, out_specs=out_specs, check_vma=False
    )
```

```python
import functools
import math

import jax
import jax.numpy as jnp
from jax import lax
from jax.experimental import pallas as pl
from jax.experimental.pallas import tpu as pltpu
from jax.sharding import PartitionSpec as P

TOK = 8
TOK_BITS = 3
DOMAINS = 48
LANES = 128
VMEM_BYTES = 63 * 1024 * 1024
LAST_VMEM_BYTES = 44 * 1024 * 1024

INFO = 16

XS, XC, YS, YC, ZS, ZC = range(6)
PAIRS = (
    (YS, XS, 1), (YS, ZS, 1), (YS, XC, 0), (XC, XS, 0),
    (YC, XC, 1), (YC, ZC, 1), (YC, ZS, 0), (YS, ZC, 0), (YC, XS, 0),
)
ONLY = {2: 0, 6: 0, 7: 1, 8: 1}
SLOT = (0, 1, 2, 3, 4, 5, 6, 6, 2)
SLOTS = 7
FIRST = (0, 1, 2, 3)
SMALL = pl.CostEstimate(flops=1, bytes_accessed=1, transcendentals=0)
NT = (((1,), (1,)), ((), ()))
NN = (((1,), (0,)), ((), ()))


def across(chip):
    return chip ^ 1


def along(chip):
    return chip + 2 if chip & 1 else chip - 2


def against(chip):
    return chip - 2 if chip & 1 else chip + 2


def stay(chip):
    return chip


def send(value, move, flip):
    chips = lax.axis_size("ex") // 2
    pairs = [
        (2 * chip + core, 2 * (move(chip) % chips) + (core ^ flip))
        for chip in range(chips)
        for core in range(2)
    ]
    return lax.ppermute(value, "ex", pairs)


def token_major(rows):
    to = lax.broadcasted_iota(jnp.int32, (rows, rows), 0)
    source = lax.broadcasted_iota(jnp.int32, (rows, rows), 1)
    examples = rows // TOK
    place = (source & (TOK - 1)) * examples + lax.shift_right_logical(source, TOK_BITS)
    return (place == to).astype(jnp.bfloat16)


def reorder(order, block):
    return jnp.dot(order, block, preferred_element_type=jnp.float32).astype(jnp.bfloat16)


def put(target, value, info):
    rows = value.shape[0]
    target[:rows, :] = value
    target[rows:, :] = jnp.concatenate([info[...]] * (target.shape[1] // LANES), axis=1)


def chunks(quarter):
    second = quarter // LANES * 3 // 10 * LANES
    return quarter - second, second


def cut_kernel(places, info, y_acts, z_acts, y_one, z_one, y_two, z_two, order):
    rows, split = order.shape[0], y_one.shape[1]
    order[...] = token_major(rows)
    put(y_one, reorder(order[...], y_acts[:, :split]), info)
    put(z_one, z_acts[:, :split], info)
    y_two[...] = reorder(order[...], y_acts[:, split:])
    z_two[...] = z_acts[:, split:]


def cut(acts, info, places):
    rows, width = acts.shape
    quarter = width // 4
    one, two = chunks(quarter)
    shapes = [(rows + INFO, one)] * 2 + [(rows, two)] * 2
    return pl.pallas_call(
        cut_kernel,
        grid_spec=pltpu.PrefetchScalarGridSpec(
            num_scalar_prefetch=1,
            grid=(1,),
            in_specs=[
                pl.BlockSpec((INFO, LANES), lambda i, p: (0, 0)),
                pl.BlockSpec((rows, quarter), lambda i, p: (0, p[0])),
                pl.BlockSpec((rows, quarter), lambda i, p: (0, p[1])),
            ],
            out_specs=[pl.BlockSpec(shape, lambda i, p: (0, 0)) for shape in shapes],
            scratch_shapes=[pltpu.VMEM((rows, rows), jnp.bfloat16)],
        ),
        out_shape=[jax.ShapeDtypeStruct(shape, acts.dtype) for shape in shapes],
        compiler_params=pltpu.CompilerParams(vmem_limit_bytes=VMEM_BYTES),
        cost_estimate=SMALL,
        name="cut",
    )(places, info, acts, acts)


def half_kernel(steps, place, info, acts, grads, out):
    @pl.when(pl.program_id(0) < steps)
    def _():
        put(out, acts[...], info)

    @pl.when(pl.program_id(0) >= steps)
    def _():
        put(out, grads[...], info)


def cut_half(acts, grads, info, place):
    rows, width = acts.shape
    half, depth = width // 2, grads.shape[1]
    step = math.gcd(math.gcd(half, depth), 512)
    steps = half // step
    return pl.pallas_call(
        functools.partial(half_kernel, steps),
        grid_spec=pltpu.PrefetchScalarGridSpec(
            num_scalar_prefetch=1,
            grid=(steps + depth // step,),
            in_specs=[
                pl.BlockSpec((INFO, LANES), lambda i, p: (0, 0)),
                pl.BlockSpec((rows, step), lambda i, p: (0, p[0] * steps + jnp.minimum(i, steps - 1))),
                pl.BlockSpec((rows, step), lambda i, p: (0, jnp.maximum(i - steps, 0))),
            ],
            out_specs=pl.BlockSpec((rows + INFO, step), lambda i, p: (0, i)),
        ),
        out_shape=jax.ShapeDtypeStruct((rows + INFO, half + depth), acts.dtype),
        compiler_params=pltpu.CompilerParams(vmem_limit_bytes=VMEM_BYTES),
        cost_estimate=SMALL,
        name="half",
    )(place, info, acts, grads)


def grams_kernel(table, xs, xc, ys, yc, zs, zc, out, held, result, in_sems, out_sems):
    rows, depth = xs.shape
    order = token_major(rows)
    sources = (xs, xc.at[:rows, xc.shape[1] - depth:], ys, yc, zs, zc)
    loads = [
        pltpu.make_async_copy(source, held.at[at], in_sems.at[at])
        for at, source in enumerate(sources)
    ]
    for load in loads:
        load.start()
    for load in loads:
        load.wait()
    for block in (YS, YC):
        held[block] = reorder(order, held[block])

    def leave(slot):
        return pltpu.make_async_copy(result.at[slot], out.at[slot], out_sems.at[slot])

    @pl.loop(0, SLOTS)
    def _(slot):
        result[slot] = lax.dot_general(
            held[table[slot]], held[table[SLOTS + slot]], NT, preferred_element_type=jnp.float32
        )
        leave(slot).start()

    for slot in range(SLOTS):
        leave(slot).wait()


def grams(table, grads, *messages):
    rows, width = grads.shape
    return pl.pallas_call(
        grams_kernel,
        in_specs=[pl.BlockSpec(memory_space=pltpu.SMEM)] + [pl.BlockSpec(memory_space=pl.ANY)] * 6,
        out_specs=pl.BlockSpec(memory_space=pl.ANY),
        out_shape=jax.ShapeDtypeStruct((SLOTS, rows, rows), jnp.float32),
        scratch_shapes=[
            pltpu.VMEM((6, rows, width), grads.dtype),
            pltpu.VMEM((SLOTS, rows, rows), jnp.float32),
            pltpu.SemaphoreType.DMA((6,)),
            pltpu.SemaphoreType.DMA((SLOTS,)),
        ],
        compiler_params=pltpu.CompilerParams(vmem_limit_bytes=VMEM_BYTES),
        cost_estimate=SMALL,
        name="grams",
    )(table, grads, *messages)


def product(one, two, inner):
    rows = inner.shape[0]
    inner[...] = lax.dot_general(
        one[:rows, :], two[:rows, :], NT, preferred_element_type=jnp.float32
    )


def token_sums(inner, gram, sums, ordered=True):
    examples, rows = sums.shape
    if ordered:
        sums[...] = sum(
            inner[at:at + examples, :] * gram[at:at + examples, :]
            for at in range(0, rows, examples)
        )
    else:
        weighted = inner[...] * gram[...]
        sums[...] = weighted.reshape(examples, TOK, rows).sum(axis=1)


def two_parts(value):
    high = value.astype(jnp.bfloat16)
    return high, (value - high.astype(jnp.float32)).astype(jnp.bfloat16)


def dot_parts(value, table):
    high, low = two_parts(value)
    return lax.dot_general(low, table, NT, preferred_element_type=jnp.float32) + lax.dot_general(
        high, table, NT, preferred_element_type=jnp.float32
    )


def side_by_side(values):
    return jnp.concatenate(values, axis=1)


def domain_sums(pairs, factor, place, info, sums):
    count, examples, rows = sums.shape
    example = lax.broadcasted_iota(jnp.int32, (LANES, rows), 0)
    column = lax.broadcasted_iota(jnp.int32, (LANES, rows), 1)
    gather = (lax.shift_right_logical(column, TOK_BITS) == example).astype(jnp.bfloat16)
    tiles = dot_parts(sums[...].reshape(count * examples, rows), gather)
    tiles = tiles.reshape(count, examples, LANES)
    mirrored, core, side = place
    lane = lax.broadcasted_iota(jnp.int32, (1, LANES), 1)
    row = lax.broadcasted_iota(jnp.int32, (DOMAINS, LANES), 0)
    hot = {
        block: ((value.astype(jnp.int32) == row) & (lane < examples)).astype(jnp.bfloat16)
        for block, value in info.items()
    }

    def listed_flag(block, apart):
        return jnp.sum(jnp.where(lane == examples + apart, info[block], 0.0), axis=1, keepdims=True)

    pad = jnp.zeros((LANES - examples, LANES), jnp.float32)
    groups = {}
    for at, pair in pairs:
        one, two, apart = PAIRS[pair]
        if one == XC:
            two_leads = core == 0
        elif two in (XS, XC):
            two_leads = side == 0
        else:
            two_leads = side == 1
        flag = jnp.where(two_leads, listed_flag(two, apart), listed_flag(one, apart))
        if pair in ONLY:
            flag = jnp.where(mirrored == ONLY[pair], flag, 0.0)
        tile = jnp.concatenate([tiles[at], pad], axis=0) * (flag * factor)
        groups.setdefault(one, []).append((two, *two_parts(tile)))
    total = {}

    def add(block, term):
        total[block] = total[block] + term if block in total else term

    for one, group in groups.items():
        others = side_by_side([hot[two] for two, _, _ in group])
        highs = side_by_side([high for _, high, _ in group])
        lows = side_by_side([low for _, _, low in group])
        add(one, lax.dot_general(
            side_by_side([others, others]), side_by_side([highs, lows]), NT,
            preferred_element_type=jnp.float32,
        ))
        columns_of = lax.dot_general(
            side_by_side([hot[one], hot[one]]), jnp.concatenate([highs, lows], axis=0), NN,
            preferred_element_type=jnp.float32,
        )
        for at, (two, _, _) in enumerate(group):
            add(two, columns_of[:, at * LANES:(at + 1) * LANES])
    return total


def copies_of(loads, sems):
    return {
        key: pltpu.make_async_copy(source, target, sems.at[at])
        for at, (key, (source, target)) in enumerate(loads.items())
    }


def start(copies, *keys):
    for key in keys:
        copies[key].start()


def wait(copies, *keys):
    for key in keys:
        copies[key].wait()


def info_row(notes, block):
    return notes[block].astype(jnp.float32)[:1]


def columns(ref, at, width):
    return ref.at[:, pl.ds(pl.multiple_of(at, LANES), width)]


def same_one_kernel(factor, own_info, acts, x_half, ys, zs, gram, out, notes,
                    held, own_v, half_v, gram_v, inner, sums, sems):
    rows, width = inner.shape[1], held.shape[2]
    quarter = acts.shape[1] // 4
    core, side = position()
    mirrored = core ^ side
    in_half = (1 - side) * quarter
    half_at = core * 2 * quarter
    copies = copies_of({
        XS: (columns(acts, half_at + in_half, width), held.at[XS, :rows]),
        XC: (columns(x_half, in_half, width), held.at[XC]),
        YS: (ys, held.at[YS]),
        ZS: (zs, held.at[ZS]),
        "g0": (gram.at[0], gram_v.at[0]),
        "g1": (gram.at[1], gram_v.at[1]),
        "g2": (gram.at[2], gram_v.at[2]),
        "own": (columns(acts, half_at, 2 * quarter), own_v),
        "half": (x_half.at[:, :2 * quarter], half_v),
        "g3": (gram.at[3], gram_v.at[3]),
        "info": (own_info, held.at[XS, rows:, :LANES]),
    }, sems)
    start(copies, YS, XS, "info", ZS, "g0", XC, "g1", "g2", "own", "half", "g3")
    wait(copies, YS, XS, "info")
    product(held.at[YS], held.at[XS], inner.at[0])
    wait(copies, "g0", ZS)
    product(held.at[YS], held.at[ZS], inner.at[1])
    token_sums(inner.at[0], gram_v.at[0], sums.at[0])
    wait(copies, "g1", XC, "g2")
    product(held.at[YS], held.at[XC], inner.at[0])
    token_sums(inner.at[1], gram_v.at[1], sums.at[1])
    wait(copies, "own", "half")
    product(half_v, own_v, inner.at[1])
    token_sums(inner.at[0], gram_v.at[2], sums.at[2])
    wait(copies, "g3")
    token_sums(inner.at[1], gram_v.at[3], sums.at[3], ordered=False)
    notes[...] = jnp.zeros_like(notes)
    for block in (XS, XC, YS, ZS):
        notes[block] = held[block, rows:, :LANES]
    info = {block: info_row(notes, block) for block in (XS, XC, YS, ZS)}
    total = domain_sums(tuple(enumerate(FIRST)), factor, (mirrored, core, side), info, sums)
    out[...] = jnp.zeros_like(out)
    for block, value in total.items():
        out[block] = value


def same_two_kernel(factor, at, notes, earlier, acts, x_half, ys, zs, gram, out,
                    held, notes_v, earlier_v, gram_v, inner, sums, sems):
    rows, width = inner.shape[1], held.shape[2]
    quarter = acts.shape[1] // 4
    core, side = position()
    mirrored = core ^ side
    in_half = (1 - side) * quarter
    copies = copies_of({
        XS: (columns(acts, core * 2 * quarter + in_half + at, width), held.at[XS, :rows]),
        XC: (columns(x_half, in_half + at, width), held.at[XC]),
        YS: (ys, held.at[YS, :rows]),
        ZS: (zs, held.at[ZS, :rows]),
        "g0": (gram.at[0], gram_v.at[0]),
        "g1": (gram.at[1], gram_v.at[1]),
        "g2": (gram.at[2], gram_v.at[2]),
        "notes": (notes, notes_v),
        "earlier": (earlier, earlier_v),
    }, sems)
    start(copies, YS, XS, ZS, "g0", "g1", XC, "g2", "notes", "earlier")
    wait(copies, YS, XS)
    product(held.at[YS], held.at[XS], inner.at[0])
    wait(copies, ZS, "g0")
    product(held.at[YS], held.at[ZS], inner.at[1])
    token_sums(inner.at[0], gram_v.at[0], sums.at[0])
    wait(copies, "g1", XC, "g2", "notes", "earlier")
    product(held.at[YS], held.at[XC], inner.at[0])
    token_sums(inner.at[1], gram_v.at[1], sums.at[1])
    token_sums(inner.at[0], gram_v.at[2], sums.at[2])
    info = {block: info_row(notes_v, block) for block in (XS, XC, YS, ZS)}
    pairs = ((0, 0), (1, 1), (2, 2))
    total = domain_sums(pairs, factor, (mirrored, core, side), info, sums)
    out[...] = earlier_v[...]
    for block, value in total.items():
        out[block] = earlier_v[block] + value


def position():
    me = lax.axis_index("ex")
    return me & 1, lax.shift_right_logical(me, 1) & 1


def cross_kernel(factor, at, notes, earlier, *refs):
    (acts, x_half, ys, yc, zs, zc, gram), refs = refs[:7], refs[7:]
    outs, (held, notes_v, earlier_v, gram_v, inner, sums, sems) = refs[:-7], refs[-7:]
    rows, width = inner.shape[1], held.shape[2]
    quarter = acts.shape[1] // 4
    core, side = position()
    mirrored = core ^ side
    in_half = (1 - side) * quarter
    work_at = core * 2 * quarter + in_half
    copies = copies_of({
        XS: (columns(acts, work_at + at, width), held.at[XS, :rows, :]),
        XC: (columns(x_half, in_half + at, width), held.at[XC]),
        YS: (ys, held.at[YS, :ys.shape[0]]),
        YC: (yc, held.at[YC, :yc.shape[0]]),
        ZS: (zs, held.at[ZS, :zs.shape[0]]),
        ZC: (zc, held.at[ZC, :zc.shape[0]]),
        "g4": (gram.at[4], gram_v.at[0]),
        "g5": (gram.at[5], gram_v.at[1]),
        "g6": (gram.at[6], gram_v.at[2]),
        "g2": (gram.at[2], gram_v.at[3]),
        "notes": (notes, notes_v),
        "earlier": (earlier, earlier_v),
    }, sems)
    start(copies, YC, XC, ZC, "g4", YS, ZS, "g5", XS, "g6", "g2", "notes", "earlier")
    wait(copies, YC, XC)
    product(held.at[YC], held.at[XC], inner.at[0])
    wait(copies, ZC)
    product(held.at[YC], held.at[ZC], inner.at[1])
    wait(copies, "g4", YS, ZS)
    token_sums(inner.at[0], gram_v.at[0], sums.at[0])
    product(held.at[jnp.where(mirrored == 0, YC, YS)], held.at[jnp.where(mirrored == 0, ZS, ZC)], inner.at[0])
    wait(copies, "g5", XS)
    token_sums(inner.at[1], gram_v.at[1], sums.at[1])
    wait(copies, "g6", "g2", "notes", "earlier")

    @pl.when(mirrored == 1)
    def _():
        product(held.at[YC], held.at[XS], inner.at[1])
        token_sums(inner.at[0], gram_v.at[2], sums.at[2])
        token_sums(inner.at[1], gram_v.at[3], sums.at[3])

    @pl.when(mirrored == 0)
    def _():
        token_sums(inner.at[0], gram_v.at[2], sums.at[2])
        sums[3] = jnp.zeros(sums.shape[1:], jnp.float32)

    if at == 0:
        total_out, notes_out = outs
        for block in (YC, ZC):
            notes_v[block] = held[block, rows:, :LANES]
        notes_out[...] = notes_v[...]
    info = {block: info_row(notes_v, block) for block in range(6)}
    pairs = ((0, 4), (1, 5), (2, 6), (2, 7), (3, 8))
    total = domain_sums(pairs, factor, (mirrored, core, side), info, sums)
    examples = sums.shape[1]
    for block, value in total.items():
        value = value + earlier_v[block]
        if at == 0:
            total_out[block] = value
        else:
            outs[block][...] = value[:, :examples]


def per_device(acts, grads, domain, listed):
    rows, width = acts.shape
    examples = rows // TOK
    quarter = width // 4
    me = lax.axis_index("ex")
    core = me % 2
    side = (me // 2) % 2
    mirrored = core ^ side

    pair_of = [
        [pair for pair in range(len(PAIRS)) if SLOT[pair] == slot] for slot in range(SLOTS)
    ]

    def listing(end):
        return [
            PAIRS[pairs[0]][end] if len(pairs) == 1 else jnp.where(
                mirrored == ONLY[pairs[0]], PAIRS[pairs[0]][end], PAIRS[pairs[1]][end])
            for pairs in pair_of
        ]

    table = jnp.stack([jnp.asarray(block, jnp.int32) for block in listing(0) + listing(1)])
    places = jnp.stack([core * 2 + side, core * 2 + (1 - side)]).astype(jnp.int32)
    cross_places = jnp.stack([(1 - core) * 2 + side, (1 - core) * 2 + (1 - side)]).astype(jnp.int32)
    half_place = jnp.stack([1 - core]).astype(jnp.int32)

    own_info = jnp.concatenate(
        [domain, listed[0], jnp.zeros((LANES - examples - 2,), jnp.int32)]
    )
    own_info = jnp.broadcast_to(own_info.astype(acts.dtype)[None, :], (INFO, LANES))

    grads_ys = send(grads, across, 0)
    grads_zs = send(grads, along, 0)
    cut_ys, cut_zs, cut_ys_two, cut_zs_two = cut(acts, own_info, places)
    own_info, _ = lax.optimization_barrier((own_info, cut_ys))
    cut_yc, cut_zc, cut_yc_two, cut_zc_two = cut(acts, own_info, cross_places)
    own_info, _ = lax.optimization_barrier((own_info, cut_yc))
    ys_one = send(cut_ys, across, 0)
    zs_one = send(cut_zs, along, 0)
    ys_two = send(cut_ys_two, across, 0)
    yc_one = send(cut_yc, across, 1)
    zc_one = send(cut_zc, along, 1)

    def exchange(*values):
        return lax.cond(
            listed[0, 0] < 2,
            lambda *sent: tuple(send(value, stay, 1) for value in sent),
            lambda *sent: tuple(jnp.zeros_like(value) for value in sent),
            *values,
        )

    x_half, = exchange(cut_half(acts, grads, own_info, half_place))
    grads_ys, grads_zs, x_half = lax.optimization_barrier((grads_ys, grads_zs, x_half))
    grads_yc, grads_zc = exchange(grads_ys, grads_zs)
    factor = 1.0 / (TOK * math.sqrt(width * grads.shape[1]))

    gram = grams(table, grads, x_half, grads_ys, grads_yc, grads_zs, grads_zc)
    cut_zs_two, cut_yc_two, gram = lax.optimization_barrier((cut_zs_two, cut_yc_two, gram))
    zs_two = send(cut_zs_two, along, 0)
    yc_two = send(cut_yc_two, across, 1)

    vmem = pl.BlockSpec(memory_space=pltpu.VMEM)
    hbm = pl.BlockSpec(memory_space=pl.ANY)
    all_sums = jax.ShapeDtypeStruct((6, DOMAINS, LANES), jnp.float32)
    all_notes = jax.ShapeDtypeStruct((6, INFO, LANES), acts.dtype)
    notes_v = pltpu.VMEM(all_notes.shape, acts.dtype)
    sums_v = pltpu.VMEM(all_sums.shape, jnp.float32)

    def call(kernel, name, vmem_bytes, width, extra, operands, out_shape):
        return pl.pallas_call(
            kernel,
            in_specs=[hbm] * len(operands),
            out_specs=[vmem] * len(out_shape),
            out_shape=out_shape,
            scratch_shapes=[pltpu.VMEM((6, rows + INFO, width), acts.dtype)] + extra + [
                pltpu.VMEM((4, rows, rows), jnp.float32),
                pltpu.VMEM((2, rows, rows), jnp.float32),
                pltpu.VMEM((4, examples, rows), jnp.float32),
                pltpu.SemaphoreType.DMA((12,)),
            ],
            compiler_params=pltpu.CompilerParams(vmem_limit_bytes=vmem_bytes),
            cost_estimate=SMALL,
            name=name,
        )(*operands)

    one, two = chunks(quarter)
    extra = [
        pltpu.VMEM((rows, 2 * quarter), acts.dtype),
        pltpu.VMEM((rows + INFO, 2 * quarter), acts.dtype),
    ]
    partial = functools.partial
    sums, notes = call(
        partial(same_one_kernel, factor), "same_one", VMEM_BYTES, one, extra,
        (own_info, acts, x_half, ys_one, zs_one, gram), [all_sums, all_notes],
    )
    cut_zc_two, sums = lax.optimization_barrier((cut_zc_two, sums))
    zc_two = send(cut_zc_two, along, 1)
    extra = [notes_v, sums_v]
    sums, notes = call(
        partial(cross_kernel, factor, 0), "cross_one", LAST_VMEM_BYTES, one, extra,
        (notes, sums, acts, x_half, ys_one, yc_one, zs_one, zc_one, gram), [all_sums, all_notes],
    )
    sums, = call(
        partial(same_two_kernel, factor, one), "same_two", LAST_VMEM_BYTES, two, extra,
        (notes, sums, acts, x_half, ys_two, zs_two, gram), [all_sums],
    )
    sums = call(
        partial(cross_kernel, factor, one), "cross_two", LAST_VMEM_BYTES, two, extra,
        (notes, sums, acts, x_half, ys_two, yc_two, zs_two, zc_two, gram),
        [jax.ShapeDtypeStruct((DOMAINS, examples), jnp.float32)] * 6,
    )

    total = sums[XS]
    total = total + send(sums[ZS], against, 0)
    total = total + send(sums[YS], across, 0)
    total = total + send(sums[ZC], against, 1)
    total = total + send(sums[YC], across, 1)
    total = total + send(sums[XC], stay, 1)
    return total.T


def solution(mesh):
    in_specs = (
        P(("groups", "ex"), None),
        P(("groups", "ex"), None),
        P(("groups", "ex")),
        P(("groups", "ex"), None),
    )
    out_specs = P(("groups", "ex"), None)
    return jax.shard_map(
        per_device, mesh=mesh, in_specs=in_specs, out_specs=out_specs, check_vma=False
    )
```
